256 devices in a mesh: row: 16 (over z, core), col: 16 (over y, x).
Axes of the slice: x: 4, y: 4, z: 8, core: 2. Of those that a mesh axis runs over, the one named last changes fastest.
Arguments:
- embed: bfloat16 [8192, 1024], P(('row', 'col')), may hold values from -0.1875 to 0.1875
- positives: int32 [8192, 4], P('row'), may hold values from 0 to 8191, as said below
- placement: int32 [8192], replicated, may hold values from 0 to 8191, as said below
Outputs:
- embed_grad: float32 [8192, 1024], P(('row', 'col'))
The draws below stay inside these ranges and needn't reach their ends.
Inputs may be any that keep to these rules, and one draw needn't show every extreme that they name: `positives`: each row names 4 different entities, none of them the entity placed at that row's position. `placement`: a permutation of the entity ids.
All inputs are finite; a program needn't handle non-finite values.
Results may differ from the reference program's by a relative error of at most 0.003.
Values may be sent and summed in bfloat16 or wider, within the bound.
A program may use at most 64 MiB of HBM per device.

```python
import jax
import jax.numpy as jnp
from jax import lax

D = 1024
POS = 4
ENTITIES = 8192


def shared_layout(key):
    return jax.random.permutation(jax.random.fold_in(key, 7), jnp.arange(ENTITIES, dtype=jnp.int32)).astype(jnp.int32)


def draw_placement(key, part):
    return shared_layout(key)


def draw_positives(key, part):
    layout = shared_layout(key)
    entity_at = jnp.argsort(layout, stable=True).astype(jnp.int32)
    quarter = ENTITIES // POS
    jitter = jax.random.randint(jax.random.fold_in(key, 9), (ENTITIES, POS), 1, quarter, dtype=jnp.int32)
    offsets = jnp.arange(POS, dtype=jnp.int32)[None, :] * quarter + jitter
    return ((entity_at[:, None] + offsets) % ENTITIES).astype(jnp.int32)


def level_of(own_key, shape, shards, least, top_value):
    loudness, own = 1.0, jax.random.fold_in(own_key, 6)
    for dim, blocks in shards:
        draws = jnp.exp(jax.random.uniform(jax.random.fold_in(own, dim), (blocks,), jnp.float32, least / len(shards), top_value / len(shards)))
        loudness = loudness * jnp.repeat(draws, shape[dim] // blocks).reshape([-1 if axis == dim else 1 for axis in range(len(shape))])
    return loudness


def gaussian(key, dims, spread, limit, pieces=(), held_as=jnp.bfloat16):
    level = level_of(key, dims, pieces, -0.22, 0.18) if pieces else 1.0
    array = jax.random.normal(key, dims, jnp.float32) * spread * level
    return jnp.minimum(jnp.maximum(array, -limit), limit).astype(held_as)


def setup_inputs(seed: int = 0) -> dict:
    key_list = jax.random.split(jax.random.key(seed), 4)
    embed = gaussian(key_list[0], (ENTITIES, D), 0.03125, 0.1875, ((0, 256),))
    positives = draw_positives(jax.random.fold_in(key_list[3], 71), 0)
    placement = draw_placement(jax.random.fold_in(key_list[3], 71), 0)
    return {"embed": embed, "positives": positives, "placement": placement}


logistic_sharpness = 0.02

def positive_rank(matching_pair_affinity_lines):
    affinity_differences = (matching_pair_affinity_lines[:, None, :] - matching_pair_affinity_lines[:, :, None]) / logistic_sharpness
    return 0.5 + lax.optimization_barrier(jnp.sum(jax.nn.sigmoid(affinity_differences), axis=2))

def coefficients(matching_pair_affinity_lines, ranks, slopes, total):
    prank, pullback = jax.vjp(positive_rank, matching_pair_affinity_lines)
    factor = 1.0 / (matching_pair_affinity_lines.shape[1] * total)
    smoothed_ordering_slope = prank / (ranks * ranks) * factor
    prank_grad = -factor / ranks
    pulled = pullback(prank_grad)[0]
    ordering_coefficient_vector = smoothed_ordering_slope / logistic_sharpness
    extra = pulled - ordering_coefficient_vector * slopes
    return (ordering_coefficient_vector, extra)

def sigmoid_sums(cosine_affinity_matrix, matching_pair_affinity_lines, allowed):
    counts = []
    slopes = []
    for element_location in range(matching_pair_affinity_lines.shape[1]):
        difference_before_squash = jax.nn.sigmoid((cosine_affinity_matrix - matching_pair_affinity_lines[:, element_location:element_location + 1]) / logistic_sharpness)
        counts.append(lax.optimization_barrier(jnp.sum(jnp.where(allowed, difference_before_squash, 0.0), axis=1)))
        slopes.append(lax.optimization_barrier(jnp.sum(jnp.where(allowed, difference_before_squash * (1.0 - difference_before_squash), 0.0), axis=1)))
    return (jnp.stack(counts, axis=1), jnp.stack(slopes, axis=1))

def score_grads(cosine_affinity_matrix, matching_pair_affinity_lines, allowed, column_pos, targets, ordering_coefficient_vector, extra):
    dense = jnp.zeros(cosine_affinity_matrix.shape, jnp.float32)
    for element_location in range(matching_pair_affinity_lines.shape[1]):
        difference_before_squash = jax.nn.sigmoid((cosine_affinity_matrix - matching_pair_affinity_lines[:, element_location:element_location + 1]) / logistic_sharpness)
        dense = dense + ordering_coefficient_vector[:, element_location:element_location + 1] * jnp.where(allowed, difference_before_squash * (1.0 - difference_before_squash), 0.0)
    for element_location in range(matching_pair_affinity_lines.shape[1]):
        dense = dense + jnp.where(column_pos[None, :] == targets[:, element_location:element_location + 1], extra[:, element_location:element_location + 1], 0.0)
    return dense.astype(jnp.bfloat16)

def reference(embed, positives, placement):
    total = embed.shape[0]
    block_rows = math_block(total)
    targets_all = jnp.take(placement, positives).astype(jnp.int32)
    column_pos = jnp.arange(total, dtype=jnp.int32)

    def step(grad_cols, block):
        begin = (block * block_rows).astype(jnp.int32)
        rows = lax.dynamic_slice_in_dim(embed, begin, block_rows, 0)
        targets = lax.dynamic_slice_in_dim(targets_all, begin, block_rows, 0)
        cosine_affinity_matrix = jnp.einsum('ad,kd->ak', rows, embed, preferred_element_type=jnp.float32)
        own = begin + jnp.arange(block_rows, dtype=jnp.int32)
        allowed = column_pos[None, :] != own[:, None]
        matching_pair_affinity_lines = jnp.take_along_axis(cosine_affinity_matrix, targets, axis=1)
        counts, slopes = sigmoid_sums(cosine_affinity_matrix, matching_pair_affinity_lines, allowed)
        ranks = 0.5 + counts
        ordering_coefficient_vector, extra = coefficients(matching_pair_affinity_lines, ranks, slopes, total)
        grad_tile = score_grads(cosine_affinity_matrix, matching_pair_affinity_lines, allowed, column_pos, targets, ordering_coefficient_vector, extra)
        grad_rows = jnp.dot(grad_tile, embed, preferred_element_type=jnp.float32)
        grad_cols = grad_cols + lax.dot_general(grad_tile, rows, (((0,), (0,)), ((), ())), preferred_element_type=jnp.float32)
        return (grad_cols, grad_rows)
    blocks = jnp.arange(total // block_rows, dtype=jnp.int32)
    grad_cols, grad_rows = lax.scan(step, jnp.zeros(embed.shape, jnp.float32), blocks)
    return grad_rows.reshape(embed.shape) + grad_cols

def math_block(total):
    block_rows = 512
    while total % block_rows != 0:
        block_rows = block_rows // 2
    return block_rows
```

```python
import functools

import jax
import jax.numpy as jnp
from jax import lax
from jax.experimental import pallas as pl
from jax.experimental.pallas import tpu as pltpu
from jax.sharding import PartitionSpec as P

MESH = pl.DeviceIdType.MESH
TAU = 0.02
HALF = 0.5 / TAU
F32, BF16, I32 = jnp.float32, jnp.bfloat16, jnp.int32

ROWS, COLS, ZS = 16, 16, 8
SHARD, WIDTH, POS = 32, 1024, 4
BLOCK = SHARD * COLS
LANES = 128
STEP = 64

PLANE = (
    (2, 2), (2, 3), (3, 2), (2, 1), (1, 2), (2, 0), (0, 2), (3, 1),
    (1, 3), (3, 3), (1, 1), (3, 0), (0, 3), (1, 0), (0, 1),
)


def remote(src, dst, send, recv, device):
    return pltpu.make_async_remote_copy(
        src_ref=src, dst_ref=dst, send_sem=send, recv_sem=recv,
        device_id=device, device_id_type=MESH,
    )


def kernel(
    embed, positives, placement, out,
    a_buf, c_buf, s_ref, vi, vj, gi, gj, part, landed, mine,
    pos_in, place_in, tgt, pt, we, x1s, x1r, x2s, x2r, jp, jw, jt, jc,
    in_sem, plane_s, plane_r, z_s, z_r, sib_s, sib_r,
    x1_ss, x1_rs, x2_ss, x2_rs, p_ss, p_rs, w_ss, w_rs, g_ss, g_rs,
):
    r, c = lax.axis_index("row"), lax.axis_index("col")
    z, core = r // 2, r % 2
    y, x = c // 4, c % 4

    def in_plane(o):
        return (r, ((y + o[0]) % 4) * 4 + (x + o[1]) % 4)

    def in_line(d, k=0):
        return (((z + d) % ZS) * 2 + (core + k) % 2, c)

    loads = [
        pltpu.make_async_copy(embed, a_buf.at[c], in_sem.at[0]),
        pltpu.make_async_copy(embed, c_buf.at[r], in_sem.at[1]),
        pltpu.make_async_copy(positives, pos_in, in_sem.at[2]),
        pltpu.make_async_copy(placement, place_in, in_sem.at[3]),
    ]
    for load in loads:
        load.start()
    barrier = pltpu.get_barrier_semaphore()

    def greet(o, carry):
        pl.semaphore_signal(barrier, inc=1, device_id=(r, c ^ o), device_id_type=MESH)
        pl.semaphore_signal(barrier, inc=1, device_id=(r ^ o, c), device_id_type=MESH)
        return carry

    lax.fori_loop(1, 16, greet, 0)
    for load in loads:
        load.wait()
    pl.semaphore_wait(barrier, 30)

    sent, plane = [], []
    todo = iter(list(enumerate(PLANE)))

    def send_plane(count):
        for _ in range(count):
            i, o = next(todo)
            copy = remote(a_buf.at[c], a_buf.at[c], plane_s.at[i], plane_r.at[i], in_plane(o))
            copy.start()
            sent.append(copy)

    for i, d in enumerate((4, 3, 5, 2, 6, 1, 7)):
        copy = remote(c_buf.at[r], c_buf.at[r], z_s.at[d], z_r.at[d], in_line(d))
        copy.start()
        sent.append(copy)
        send_plane(2)
    own = remote(c_buf.at[r], c_buf.at[r], sib_s.at[0], sib_r.at[0], in_line(0, 1))
    own.start()
    sent.append(own)
    send_plane(1)

    table = place_in[...]
    high = (table // 64).astype(F32).astype(BF16)
    low = (table % 64).astype(F32).astype(BF16)
    lane_id = lax.broadcasted_iota(I32, (LANES, BLOCK), 0)
    row_id = lax.broadcasted_iota(I32, (64, BLOCK), 0)
    for m in range(POS):
        entity = pos_in[m : m + 1, :]
        hot = jnp.where(lane_id == entity % LANES, 1.0, 0.0).astype(BF16)
        value = jnp.dot(high, hot, preferred_element_type=F32) * 64.0 + jnp.dot(
            low, hot, preferred_element_type=F32
        )
        found = jnp.sum(jnp.where(row_id == entity // LANES, value, 0.0), axis=0, keepdims=True)
        pt[POS + m : POS + m + 1, :] = found
        where = found.astype(I32)
        here = (where // SHARD) % COLS == c
        tgt[m : m + 1, :] = jnp.where(here, (where // BLOCK) * SHARD + where % SHARD, -1)

    for d in (1, 7, 2, 6, 3, 5, 4):
        back = (((z + ZS - d) % ZS) * 2 + core) % ROWS
        remote(c_buf.at[back], c_buf.at[back], z_s.at[d], z_r.at[d], in_line(d)).wait_recv()
        copy = remote(c_buf.at[back], c_buf.at[back], sib_s.at[d], sib_r.at[d], in_line(0, 1))
        copy.start()
        sent.append(copy)
    for i, o in enumerate(PLANE):
        back = ((y + 4 - o[0]) % 4) * 4 + (x + 4 - o[1]) % 4
        remote(a_buf.at[back], a_buf.at[back], plane_s.at[i], plane_r.at[i], in_plane(o)).wait_recv()
    for d in range(ZS):
        back = ((z + ZS - d) % ZS) * 2 + (1 - core)
        remote(c_buf.at[back], c_buf.at[back], sib_s.at[d], sib_r.at[d], in_line(0, 1)).wait_recv()

    anchors = a_buf[...].reshape(BLOCK, WIDTH)
    for h in range(2):
        cand = c_buf[8 * h : 8 * h + 8].reshape(BLOCK // 2, WIDTH)
        s_ref[256 * h : 256 * h + 256, :] = HALF * lax.dot_general(
            cand, anchors, (((1,), (1,)), ((), ())), preferred_element_type=F32
        )
    tile = s_ref[pl.ds(pl.multiple_of(r * SHARD, SHARD), SHARD), pl.ds(pl.multiple_of(y * LANES, LANES), LANES)]
    me_row = lax.broadcasted_iota(I32, (SHARD, LANES), 0)
    me_lane = lax.broadcasted_iota(I32, (SHARD, LANES), 1)
    s_ref[pl.ds(pl.multiple_of(r * SHARD, SHARD), SHARD), pl.ds(pl.multiple_of(y * LANES, LANES), LANES)] = (
        jnp.where(me_lane - x * SHARD == me_row, -1e30, tile)
    )

    iota_k = lax.broadcasted_iota(I32, (STEP, LANES), 0)
    iota_a = lax.broadcasted_iota(I32, (STEP, LANES), 1)
    steps = BLOCK // STEP

    def fold(value):
        return jnp.sum(value.reshape(STEP // 8, 8, LANES), axis=0)

    def cut(q):
        return slice(q * LANES, (q + 1) * LANES)

    for q in range(4):
        rows = [tgt[m : m + 1, cut(q)] for m in range(POS)]

        def pick(i, acc, q=q, rows=rows):
            k0 = pl.multiple_of(i * STEP, STEP)
            score = s_ref[pl.ds(k0, STEP), cut(q)]
            return tuple(
                acc[m] + fold(jnp.where(iota_k == rows[m] - k0, score, 0.0)) for m in range(POS)
            )

        acc = lax.fori_loop(0, steps, pick, (jnp.zeros((8, LANES), F32),) * POS)
        for m in range(POS):
            half, lane = q // 2, (q % 2) * LANES
            x1s[half * POS + m : half * POS + m + 1, lane : lane + LANES] = jnp.sum(
                acc[m], axis=0, keepdims=True
            )

    def exchange(src, dst, ss, rs, peer):
        def start(o, carry):
            remote(src, dst, ss.at[o], rs.at[o], peer(o)).start()
            return carry

        lax.fori_loop(1, 16, start, 0)

    def arrive(src, dst, ss, rs, peer, index):
        def wait(o, carry):
            remote(src, dst.at[index ^ o], ss.at[o], rs.at[o], peer(o)).wait_recv()
            return carry

        lax.fori_loop(1, 16, wait, 0)

    def leave(src, dst, ss, rs, peer):
        def wait(o, carry):
            remote(src, dst, ss.at[o], rs.at[o], peer(o)).wait_send()
            return carry

        lax.fori_loop(1, 16, wait, 0)

    def peer_c(o):
        return (r, c ^ o)

    def peer_r(o):
        return (r ^ o, c)

    exchange(x1s, x1r.at[c], x1_ss, x1_rs, peer_c)
    x1r[c] = x1s[...]
    arrive(x1s, x1r, x1_ss, x1_rs, peer_c, c)
    total = jnp.sum(x1r[...], axis=0)
    pt[0:POS, 0:256] = total[0:POS]
    pt[0:POS, 256:512] = total[POS : 2 * POS]

    group = pl.ds(pl.multiple_of(y * LANES, LANES), LANES)
    exchange(pt.at[:, group], jp.at[r], p_ss, p_rs, peer_r)
    jp[r] = pt[:, group]

    for q in range(4):
        rows = [pt[m : m + 1, cut(q)] for m in range(POS)]

        def count(i, acc, q=q, rows=rows):
            k0 = pl.multiple_of(i * STEP, STEP)
            score = s_ref[pl.ds(k0, STEP), cut(q)]
            new = []
            for m in range(POS):
                u = 1.0 + jnp.tanh(score - rows[m])
                v = u * (2.0 - u)
                vi[m, pl.ds(k0, STEP), cut(q)] = v
                new.append(acc[2 * m] + fold(u))
                new.append(acc[2 * m + 1] + fold(v))
            return tuple(new)

        acc = lax.fori_loop(0, steps, count, (jnp.zeros((8, LANES), F32),) * (2 * POS))
        for m in range(POS):
            x2s[m : m + 1, cut(q)] = jnp.sum(acc[2 * m], axis=0, keepdims=True)
            x2s[POS + m : POS + m + 1, cut(q)] = jnp.sum(acc[2 * m + 1], axis=0, keepdims=True)
    exchange(x2s, x2r.at[c], x2_ss, x2_rs, peer_c)
    x2r[c] = x2s[...]

    def columns(src, first):
        jt[...] = jnp.transpose(src[...].reshape(ROWS * 8, LANES))
        mine_cols = jt[pl.ds(pl.multiple_of(x * SHARD, SHARD), SHARD), :]
        for b in range(ROWS):
            for n in range(8):
                jc[first + n, b * SHARD : (b + 1) * SHARD, :] = jnp.broadcast_to(
                    mine_cols[:, b * 8 + n : b * 8 + n + 1], (SHARD, LANES)
                )

    arrive(pt.at[:, group], jp, p_ss, p_rs, peer_r, r)
    columns(jp, 0)

    def slopes(i, carry):
        k0 = pl.multiple_of(i * STEP, STEP)
        for m in range(POS):
            col = jc[m, pl.ds(k0, STEP), :]
            for q in range(4):
                u = 1.0 + jnp.tanh(s_ref[pl.ds(k0, STEP), cut(q)] - col)
                vj[m, pl.ds(k0, STEP), cut(q)] = u * (2.0 - u)
            where = jc[POS + m, pl.ds(k0, STEP), :].astype(I32)
            jc[POS + m, pl.ds(k0, STEP), :] = jnp.where(
                where // BLOCK == r, where % BLOCK, -1
            ).astype(F32)
        return carry

    lax.fori_loop(0, steps, slopes, 0)

    arrive(x2s, x2r, x2_ss, x2_rs, peer_c, c)
    total = jnp.sum(x2r[...], axis=0)
    factor = 1.0 / (POS * SHARD * ROWS * COLS)
    p = [pt[m : m + 1, :] for m in range(POS)]
    rank = [0.5 + 0.5 * total[m : m + 1] for m in range(POS)]
    slope = [0.25 * total[POS + m : POS + m + 1] for m in range(POS)]
    prank = [jnp.full((1, BLOCK), 1.0, F32) for _ in range(POS)]
    grad = [-factor / rank[m] for m in range(POS)]
    pulled = [jnp.zeros((1, BLOCK), F32) for _ in range(POS)]
    for m in range(POS):
        for n in range(m + 1, POS):
            t = jnp.tanh(p[n] - p[m])
            prank[m] = prank[m] + 0.5 * (1.0 + t)
            prank[n] = prank[n] + 0.5 * (1.0 - t)
            pair = (0.25 / TAU) * (1.0 - t) * (1.0 + t) * (grad[n] - grad[m])
            pulled[m] = pulled[m] + pair
            pulled[n] = pulled[n] - pair
    for m in range(POS):
        weight = prank[m] / (rank[m] * rank[m]) * factor / TAU
        we[m : m + 1, :] = 0.25 * weight
        we[POS + m : POS + m + 1, :] = pulled[m] - weight * slope[m]

    exchange(we.at[:, group], jw.at[r], w_ss, w_rs, peer_r)
    jw[r] = we[:, group]

    for q in range(4):
        rows = [tgt[m : m + 1, cut(q)] for m in range(POS)]
        weights = [we[m : m + 1, cut(q)] for m in range(POS)]
        extras = [we[POS + m : POS + m + 1, cut(q)] for m in range(POS)]

        def tile_i(i, carry, q=q, rows=rows, weights=weights, extras=extras):
            k0 = pl.multiple_of(i * STEP, STEP)
            dense = weights[0] * vi[0, pl.ds(k0, STEP), cut(q)]
            for m in range(1, POS):
                dense = dense + weights[m] * vi[m, pl.ds(k0, STEP), cut(q)]
            for m in range(POS):
                dense = dense + jnp.where(iota_k == rows[m] - k0, extras[m], 0.0)
            gi[pl.ds(k0, STEP), cut(q)] = dense.astype(BF16)
            return carry

        lax.fori_loop(0, steps, tile_i, 0)

    arrive(we.at[:, group], jw, w_ss, w_rs, peer_r, r)
    columns(jw, 2 * POS)

    cand = c_buf[...].reshape(BLOCK, WIDTH)
    wide = 2 * LANES
    for h in range(2):
        def tile_j(i, carry, h=h):
            k0 = pl.multiple_of(i * STEP, STEP)
            for q in (2 * h, 2 * h + 1):
                dense = jc[2 * POS, pl.ds(k0, STEP), :] * vj[0, pl.ds(k0, STEP), cut(q)]
                for m in range(1, POS):
                    dense = dense + jc[2 * POS + m, pl.ds(k0, STEP), :] * vj[m, pl.ds(k0, STEP), cut(q)]
                lane = (iota_a + q * LANES).astype(F32)
                for m in range(POS):
                    dense = dense + jnp.where(
                        jc[POS + m, pl.ds(k0, STEP), :] == lane,
                        jc[3 * POS + m, pl.ds(k0, STEP), :],
                        0.0,
                    )
                gj[pl.ds(k0, STEP), cut(q)] = dense.astype(BF16)
            return carry

        lax.fori_loop(0, steps, tile_j, 0)
        half = slice(h * wide, (h + 1) * wide)
        dims = (((0,), (0,)), ((), ()))
        product = lax.dot_general(gi[:, half], cand, dims, preferred_element_type=F32)
        product = product + lax.dot_general(gj[:, half], cand, dims, preferred_element_type=F32)
        part[8 * h : 8 * h + 8] = product.astype(BF16).reshape(8, SHARD, WIDTH)

        @pl.when(c // 8 == h)
        def _(product=product, h=h):
            mine[...] = product.reshape(8, SHARD, WIDTH)

        def push(n, carry, h=h):
            to = 8 * h + n

            @pl.when(to != c)
            def _():
                remote(part.at[to], landed.at[c], g_ss.at[to], g_rs.at[c], (r, to)).start()

            return carry

        lax.fori_loop(0, 8, push, 0)

    out[...] = mine[c % 8]

    def gather_sum(o, carry):
        frm = c ^ o
        remote(part.at[frm], landed.at[frm], g_ss.at[frm], g_rs.at[frm], (r, frm)).wait_recv()
        out[...] += landed[frm].astype(F32)
        return carry

    lax.fori_loop(1, 16, gather_sum, 0)

    def sent_all(o, carry):
        frm = c ^ o
        remote(part.at[frm], landed.at[frm], g_ss.at[frm], g_rs.at[frm], (r, frm)).wait_send()
        return carry

    lax.fori_loop(1, 16, sent_all, 0)
    leave(x1s, x1r.at[c], x1_ss, x1_rs, peer_c)
    leave(x2s, x2r.at[c], x2_ss, x2_rs, peer_c)
    leave(pt.at[:, group], jp.at[r], p_ss, p_rs, peer_r)
    leave(we.at[:, group], jw.at[r], w_ss, w_rs, peer_r)
    for copy in sent:
        copy.wait_send()


def body(embed, positives, placement):
    dma = pltpu.SemaphoreType.DMA
    return pl.pallas_call(
        kernel,
        out_shape=jax.ShapeDtypeStruct((SHARD, WIDTH), F32),
        in_specs=[pl.BlockSpec(memory_space=pl.ANY)] * 3,
        out_specs=pl.BlockSpec(memory_space=pltpu.VMEM),
        scratch_shapes=[
            pltpu.VMEM((COLS, SHARD, WIDTH), BF16),
            pltpu.VMEM((ROWS, SHARD, WIDTH), BF16),
            pltpu.VMEM((BLOCK, BLOCK), F32),
            pltpu.VMEM((POS, BLOCK, BLOCK), F32),
            pltpu.VMEM((POS, BLOCK, BLOCK), F32),
            pltpu.VMEM((BLOCK, BLOCK), BF16),
            pltpu.VMEM((BLOCK, BLOCK), BF16),
            pltpu.VMEM((COLS, SHARD, WIDTH), BF16),
            pltpu.VMEM((COLS, SHARD, WIDTH), BF16),
            pltpu.VMEM((8, SHARD, WIDTH), F32),
            pltpu.VMEM((POS, BLOCK), I32),
            pltpu.VMEM((64, LANES), I32),
            pltpu.VMEM((8, BLOCK), I32),
            pltpu.VMEM((8, BLOCK), F32),
            pltpu.VMEM((8, BLOCK), F32),
            pltpu.VMEM((8, BLOCK // 2), F32),
            pltpu.VMEM((COLS, 8, BLOCK // 2), F32),
            pltpu.VMEM((8, BLOCK), F32),
            pltpu.VMEM((COLS, 8, BLOCK), F32),
            pltpu.VMEM((ROWS, 8, LANES), F32),
            pltpu.VMEM((ROWS, 8, LANES), F32),
            pltpu.VMEM((LANES, LANES), F32),
            pltpu.VMEM((4 * POS, BLOCK, LANES), F32),
            dma((4,)),
        ]
        + [dma((16,))] * 16,
        compiler_params=pltpu.CompilerParams(
            collective_id=0, has_side_effects=True, vmem_limit_bytes=48 * 1024 * 1024
        ),
        cost_estimate=pl.CostEstimate(flops=1 << 31, bytes_accessed=1 << 22, transcendentals=1 << 21),
        name="smooth_ap",
    )(embed, positives.T, placement.reshape(64, LANES))


def solution(mesh):
    return jax.shard_map(
        body,
        mesh=mesh,
        in_specs=(P(("row", "col"), None), P("row", None), P()),
        out_specs=P(("row", "col"), None),
        check_vma=False,
    )
```

```python
import functools

import jax
import jax.numpy as jnp
from jax import lax
from jax.experimental import pallas as pl
from jax.experimental.pallas import tpu as pltpu
from jax.sharding import PartitionSpec as P

MESH = pl.DeviceIdType.MESH
TAU = 0.02
HALF = 0.5 / TAU
F32, BF16, I32 = jnp.float32, jnp.bfloat16, jnp.int32

ROWS, COLS, ZS = 16, 16, 8
SHARD, WIDTH, POS = 32, 1024, 4
BLOCK = SHARD * COLS
LANES = 128
STEP = 64

NARROW = 256
BROAD = WIDTH - NARROW

LINE = (
    (4, 0), (3, 1), (5, 0), (4, 1), (3, 0), (5, 1), (2, 0), (6, 1),
    (2, 1), (6, 0), (1, 0), (7, 1), (1, 1), (7, 0), (0, 1),
)


def remote(src, dst, send, recv, device):
    return pltpu.make_async_remote_copy(
        src_ref=src, dst_ref=dst, send_sem=send, recv_sem=recv,
        device_id=device, device_id_type=MESH,
    )


def kernel(
    embed, positives, placement, out,
    a_buf, c_buf, s_ref, vi, vj, gi, gj, part, landed, mine, z_part, z_landed, z_mine,
    pos_in, place_in, tgt, pt, we, x1s, x1r, x2s, x2r, jp, jw, jt, jc,
    in_sem, plane_s, plane_r, z_s, z_r, sib_s, sib_r,
    x1_ss, x1_rs, x2_ss, x2_rs, p_ss, p_rs, w_ss, w_rs, g_ss, g_rs, h_ss, h_rs,
):
    r, c = lax.axis_index("row"), lax.axis_index("col")
    z, core = r // 2, r % 2
    y, x = c // 4, c % 4

    def in_plane(o):
        return (r, ((y + o[0]) % 4) * 4 + (x + o[1]) % 4)

    def in_line(d, k=0):
        return (((z + d) % ZS) * 2 + (core + k) % 2, c)

    loads = [
        pltpu.make_async_copy(embed, a_buf.at[c], in_sem.at[0]),
        pltpu.make_async_copy(embed, c_buf.at[r], in_sem.at[1]),
        pltpu.make_async_copy(positives, pos_in, in_sem.at[2]),
        pltpu.make_async_copy(placement, place_in, in_sem.at[3]),
    ]
    for load in loads:
        load.start()
    barrier = pltpu.get_barrier_semaphore()

    def greet(o, carry):
        pl.semaphore_signal(barrier, inc=1, device_id=(r, c ^ o), device_id_type=MESH)
        pl.semaphore_signal(barrier, inc=1, device_id=(r ^ o, c), device_id_type=MESH)
        return carry

    lax.fori_loop(1, 16, greet, 0)
    for load in loads:
        load.wait()
    pl.semaphore_wait(barrier, 30)

    sent = []

    def go(src, dst, ss, rs, device):
        copy = remote(src, dst, ss, rs, device)
        copy.start()
        sent.append(copy)

    def z_send(d, block, rows, step, slot):
        view = c_buf.at[block, rows]
        go(view, view, z_s.at[slot], z_r.at[slot], in_line(step % ZS))

    def z_wait(d, rows, slot):
        view = c_buf.at[from_z(d), rows]
        remote(view, view, z_s.at[slot], z_r.at[slot], in_line(d % ZS)).wait_recv()

    def from_z(d, k=0):
        return ((z + ZS - d) % ZS) * 2 + (core + k) % 2

    def from_plane(dy, dx):
        return ((y + 4 - dy) % 4) * 4 + (x + 4 - dx) % 4

    def a_send(block, rows, dy, dx, slot):
        view = a_buf.at[block, rows]
        go(view, view, plane_s.at[slot], plane_r.at[slot], in_plane((dy, dx)))

    def a_wait(dy, dx, rows, slot):
        view = a_buf.at[from_plane(dy, dx), rows]
        remote(view, view, plane_s.at[slot], plane_r.at[slot], in_plane((dy, dx))).wait_recv()

    def sib_send(d, rows, slot):
        view = c_buf.at[from_z(d), rows]
        go(view, view, sib_s.at[slot], sib_r.at[slot], in_line(0, 1))

    def sib_wait(d, rows, slot):
        view = c_buf.at[from_z(d, 1), rows]
        remote(view, view, sib_s.at[slot], sib_r.at[slot], in_line(0, 1)).wait_recv()

    every, top, low_half = pl.ds(0, SHARD), pl.ds(0, SHARD // 2), pl.ds(SHARD // 2, SHARD // 2)
    z_send(2, r, every, 2, 2)
    z_send(-2, r, every, -2, 6)
    a_send(c, every, 0, 2, 1)
    a_send(c, every, 2, 0, 4)
    z_send(1, r, every, 1, 1)
    z_send(-1, r, every, -1, 7)
    for d in (1, 3):
        a_send(c, every, 0, d, d - 1)
        a_send(c, every, d, 0, d + 2)
    sib_send(0, every, 0)

    table = place_in[...]
    high = (table // 64).astype(F32).astype(BF16)
    low = (table % 64).astype(F32).astype(BF16)
    lane_id = lax.broadcasted_iota(I32, (LANES, BLOCK), 0)
    row_id = lax.broadcasted_iota(I32, (64, BLOCK), 0)
    for m in range(POS):
        entity = pos_in[m : m + 1, :]
        hot = jnp.where(lane_id == entity % LANES, 1.0, 0.0).astype(BF16)
        value = jnp.dot(high, hot, preferred_element_type=F32) * 64.0 + jnp.dot(
            low, hot, preferred_element_type=F32
        )
        found = jnp.sum(jnp.where(row_id == entity // LANES, value, 0.0), axis=0, keepdims=True)
        pt[POS + m : POS + m + 1, :] = found
        where = found.astype(I32)
        here = (where // SHARD) % COLS == c
        tgt[m : m + 1, :] = jnp.where(here, (where // BLOCK) * SHARD + where % SHARD, -1)

    def turn(d):
        a_wait(0, d, every, d - 1)
        for e in (2, 1, 3):
            a_send(from_plane(0, d), top, e, 0, 6 + 3 * (d - 1) + e - 1)
        a_wait(d, 0, every, d + 2)
        for e in (2, 1, 3):
            a_send(from_plane(d, 0), low_half, 0, e, 15 + 3 * (d - 1) + e - 1)

    turn(1)
    turn(3)
    z_wait(2, every, 2)
    z_send(4, from_z(2), top, 2, 4)
    z_send(3, from_z(2), every, 1, 3)
    z_wait(-2, every, 6)
    z_send(-4, from_z(-2), low_half, -2, 8)
    z_send(-3, from_z(-2), every, -1, 5)
    turn(2)
    for d, slot in ((2, 2), (-2, 6)):
        sib_send(d, every, slot)
    for d, slot in ((1, 1), (-1, 7)):
        z_wait(d, every, slot)
        sib_send(d, every, slot)
    for d, slot in ((3, 3), (-3, 5)):
        z_wait(d, every, slot)
        sib_send(d, every, slot)
    z_wait(4, top, 4)
    sib_send(4, top, 4)
    z_wait(-4, low_half, 8)
    sib_send(-4, low_half, 8)
    for d in (1, 3, 2):
        for e in (1, 3, 2):
            a_wait(e, d, top, 6 + 3 * (d - 1) + e - 1)
            a_wait(d, e, low_half, 15 + 3 * (d - 1) + e - 1)
    for d, slot in ((0, 0), (1, 1), (-1, 7), (2, 2), (-2, 6), (3, 3), (-3, 5)):
        sib_wait(d, every, slot)
    sib_wait(4, top, 4)
    sib_wait(-4, low_half, 8)

    anchors = a_buf[...].reshape(BLOCK, WIDTH)
    for h in range(2):
        cand = c_buf[8 * h : 8 * h + 8].reshape(BLOCK // 2, WIDTH)
        s_ref[256 * h : 256 * h + 256, :] = HALF * lax.dot_general(
            cand, anchors, (((1,), (1,)), ((), ())), preferred_element_type=F32
        )
    tile = s_ref[pl.ds(pl.multiple_of(r * SHARD, SHARD), SHARD), pl.ds(pl.multiple_of(y * LANES, LANES), LANES)]
    me_row = lax.broadcasted_iota(I32, (SHARD, LANES), 0)
    me_lane = lax.broadcasted_iota(I32, (SHARD, LANES), 1)
    s_ref[pl.ds(pl.multiple_of(r * SHARD, SHARD), SHARD), pl.ds(pl.multiple_of(y * LANES, LANES), LANES)] = (
        jnp.where(me_lane - x * SHARD == me_row, -1e30, tile)
    )

    iota_k = lax.broadcasted_iota(I32, (STEP, LANES), 0)
    iota_a = lax.broadcasted_iota(I32, (STEP, LANES), 1)
    steps = BLOCK // STEP

    def fold(value):
        return jnp.sum(value.reshape(STEP // 8, 8, LANES), axis=0)

    def cut(q):
        return slice(q * LANES, (q + 1) * LANES)

    for q in range(4):
        rows = [tgt[m : m + 1, cut(q)] for m in range(POS)]

        def pick(i, acc, q=q, rows=rows):
            k0 = pl.multiple_of(i * STEP, STEP)
            score = s_ref[pl.ds(k0, STEP), cut(q)]
            return tuple(
                acc[m] + fold(jnp.where(iota_k == rows[m] - k0, score, 0.0)) for m in range(POS)
            )

        acc = lax.fori_loop(0, steps, pick, (jnp.zeros((8, LANES), F32),) * POS)
        for m in range(POS):
            half, lane = q // 2, (q % 2) * LANES
            x1s[half * POS + m : half * POS + m + 1, lane : lane + LANES] = jnp.sum(
                acc[m], axis=0, keepdims=True
            )

    def exchange(src, dst, ss, rs, peer):
        def start(o, carry):
            remote(src, dst, ss.at[o], rs.at[o], peer(o)).start()
            return carry

        lax.fori_loop(1, 16, start, 0)

    def arrive(src, dst, ss, rs, peer, index):
        def wait(o, carry):
            remote(src, dst.at[index ^ o], ss.at[o], rs.at[o], peer(o)).wait_recv()
            return carry

        lax.fori_loop(1, 16, wait, 0)

    def leave(src, dst, ss, rs, peer):
        def wait(o, carry):
            remote(src, dst, ss.at[o], rs.at[o], peer(o)).wait_send()
            return carry

        lax.fori_loop(1, 16, wait, 0)

    def peer_c(o):
        return (r, c ^ o)

    def peer_r(o):
        return (r ^ o, c)

    exchange(x1s, x1r.at[c], x1_ss, x1_rs, peer_c)
    x1r[c] = x1s[...]
    arrive(x1s, x1r, x1_ss, x1_rs, peer_c, c)
    total = jnp.sum(x1r[...], axis=0)
    pt[0:POS, 0:256] = total[0:POS]
    pt[0:POS, 256:512] = total[POS : 2 * POS]

    group = pl.ds(pl.multiple_of(y * LANES, LANES), LANES)
    exchange(pt.at[:, group], jp.at[r], p_ss, p_rs, peer_r)
    jp[r] = pt[:, group]

    for q in range(4):
        rows = [pt[m : m + 1, cut(q)] for m in range(POS)]

        def count(i, acc, q=q, rows=rows):
            k0 = pl.multiple_of(i * STEP, STEP)
            score = s_ref[pl.ds(k0, STEP), cut(q)]
            new = []
            for m in range(POS):
                u = 1.0 + jnp.tanh(score - rows[m])
                v = u * (2.0 - u)
                vi[m, pl.ds(k0, STEP), cut(q)] = v
                new.append(acc[2 * m] + fold(u))
                new.append(acc[2 * m + 1] + fold(v))
            return tuple(new)

        acc = lax.fori_loop(0, steps, count, (jnp.zeros((8, LANES), F32),) * (2 * POS))
        for m in range(POS):
            x2s[m : m + 1, cut(q)] = jnp.sum(acc[2 * m], axis=0, keepdims=True)
            x2s[POS + m : POS + m + 1, cut(q)] = jnp.sum(acc[2 * m + 1], axis=0, keepdims=True)
    exchange(x2s, x2r.at[c], x2_ss, x2_rs, peer_c)
    x2r[c] = x2s[...]

    def columns(src, first):
        jt[...] = jnp.transpose(src[...].reshape(ROWS * 8, LANES))
        mine_cols = jt[pl.ds(pl.multiple_of(x * SHARD, SHARD), SHARD), :]
        for b in range(ROWS):
            for n in range(8):
                jc[first + n, b * SHARD : (b + 1) * SHARD, :] = jnp.broadcast_to(
                    mine_cols[:, b * 8 + n : b * 8 + n + 1], (SHARD, LANES)
                )

    arrive(pt.at[:, group], jp, p_ss, p_rs, peer_r, r)
    columns(jp, 0)

    arrive(x2s, x2r, x2_ss, x2_rs, peer_c, c)
    total = jnp.sum(x2r[...], axis=0)
    factor = 1.0 / (POS * SHARD * ROWS * COLS)
    p = [pt[m : m + 1, :] for m in range(POS)]
    rank = [0.5 + 0.5 * total[m : m + 1] for m in range(POS)]
    slope = [0.25 * total[POS + m : POS + m + 1] for m in range(POS)]
    prank = [jnp.full((1, BLOCK), 1.0, F32) for _ in range(POS)]
    grad = [-factor / rank[m] for m in range(POS)]
    pulled = [jnp.zeros((1, BLOCK), F32) for _ in range(POS)]
    for m in range(POS):
        for n in range(m + 1, POS):
            t = jnp.tanh(p[n] - p[m])
            prank[m] = prank[m] + 0.5 * (1.0 + t)
            prank[n] = prank[n] + 0.5 * (1.0 - t)
            pair = (0.25 / TAU) * (1.0 - t) * (1.0 + t) * (grad[n] - grad[m])
            pulled[m] = pulled[m] + pair
            pulled[n] = pulled[n] - pair
    for m in range(POS):
        weight = prank[m] / (rank[m] * rank[m]) * factor / TAU
        we[m : m + 1, :] = 0.25 * weight
        we[POS + m : POS + m + 1, :] = pulled[m] - weight * slope[m]

    exchange(we.at[:, group], jw.at[r], w_ss, w_rs, peer_r)
    jw[r] = we[:, group]

    for q in range(4):
        rows = [tgt[m : m + 1, cut(q)] for m in range(POS)]
        weights = [we[m : m + 1, cut(q)] for m in range(POS)]
        extras = [we[POS + m : POS + m + 1, cut(q)] for m in range(POS)]

        def tile_i(i, carry, q=q, rows=rows, weights=weights, extras=extras):
            k0 = pl.multiple_of(i * STEP, STEP)
            dense = weights[0] * vi[0, pl.ds(k0, STEP), cut(q)]
            for m in range(1, POS):
                dense = dense + weights[m] * vi[m, pl.ds(k0, STEP), cut(q)]
            for m in range(POS):
                dense = dense + jnp.where(iota_k == rows[m] - k0, extras[m], 0.0)
            gi[pl.ds(k0, STEP), cut(q)] = dense.astype(BF16)
            return carry

        lax.fori_loop(0, steps, tile_i, 0)

    def slopes(i, carry):
        k0 = pl.multiple_of(i * STEP, STEP)
        for m in range(POS):
            col = jc[m, pl.ds(k0, STEP), :]
            for q in range(4):
                u = 1.0 + jnp.tanh(s_ref[pl.ds(k0, STEP), cut(q)] - col)
                vj[m, pl.ds(k0, STEP), cut(q)] = u * (2.0 - u)
            where = jc[POS + m, pl.ds(k0, STEP), :].astype(I32)
            jc[POS + m, pl.ds(k0, STEP), :] = jnp.where(
                where // BLOCK == r, where % BLOCK, -1
            ).astype(F32)
        return carry

    lax.fori_loop(0, steps, slopes, 0)

    arrive(we.at[:, group], jw, w_ss, w_rs, peer_r, r)
    columns(jw, 2 * POS)

    def tile_j(i, carry):
        k0 = pl.multiple_of(i * STEP, STEP)
        for q in range(4):
            dense = jc[2 * POS, pl.ds(k0, STEP), :] * vj[0, pl.ds(k0, STEP), cut(q)]
            for m in range(1, POS):
                dense = dense + jc[2 * POS + m, pl.ds(k0, STEP), :] * vj[m, pl.ds(k0, STEP), cut(q)]
            lane = (iota_a + q * LANES).astype(F32)
            for m in range(POS):
                dense = dense + jnp.where(
                    jc[POS + m, pl.ds(k0, STEP), :] == lane,
                    jc[3 * POS + m, pl.ds(k0, STEP), :],
                    0.0,
                )
            gj[pl.ds(k0, STEP), cut(q)] = dense.astype(BF16)
        return carry

    lax.fori_loop(0, steps, tile_j, 0)

    right = a_buf[:, :, BROAD:].reshape(BLOCK, NARROW)
    for h in range(2):
        rows = slice(256 * h, 256 * h + 256)
        product = jnp.dot(gi[rows, :], right, preferred_element_type=F32)
        product = product + jnp.dot(gj[rows, :], right, preferred_element_type=F32)
        z_part[8 * h : 8 * h + 8] = product.astype(BF16).reshape(8, SHARD, NARROW)

        @pl.when(r // 8 == h)
        def _(product=product):
            z_mine[...] = product.reshape(8, SHARD, NARROW)

    for i, o in enumerate(LINE):
        to = ((z + o[0]) % ZS) * 2 + (core + o[1]) % 2
        remote(z_part.at[to], z_landed.at[r], h_ss.at[i], h_rs.at[i], (to, c)).start()

    left = c_buf[:, :, :BROAD].reshape(BLOCK, BROAD)
    wide = 2 * LANES
    dims = (((0,), (0,)), ((), ()))
    for turn_id in range(2):
        h = (c // 8) ^ (1 - turn_id)
        half = pl.ds(pl.multiple_of(h * wide, wide), wide)
        product = lax.dot_general(gi[:, half], left, dims, preferred_element_type=F32)
        product = product + lax.dot_general(gj[:, half], left, dims, preferred_element_type=F32)
        part[pl.ds(h * 8, 8)] = product.astype(BF16).reshape(8, SHARD, BROAD)
        if turn_id == 1:
            mine[...] = product.reshape(8, SHARD, BROAD)

        def push(n, carry):
            to = c ^ n
            remote(part.at[to], landed.at[c], g_ss.at[n], g_rs.at[n], (r, to)).start()
            return carry

        lax.fori_loop(*((8, 16) if turn_id == 0 else (1, 8)), push, 0)

    out[:, BROAD:] = z_mine[r % 8]
    out[:, :BROAD] = mine[c % 8]
    for i, o in reversed(list(enumerate(LINE))):
        frm = from_z(o[0], o[1])
        remote(z_part.at[frm], z_landed.at[frm], h_ss.at[i], h_rs.at[i], (frm, c)).wait_recv()
        out[:, BROAD:] += z_landed[frm].astype(F32)

    def gather_sum(o, carry):
        frm = c ^ o
        remote(part.at[frm], landed.at[frm], g_ss.at[o], g_rs.at[o], (r, frm)).wait_recv()
        out[:, :BROAD] += landed[frm].astype(F32)
        return carry

    lax.fori_loop(1, 16, gather_sum, 0)

    def sent_all(o, carry):
        frm = c ^ o
        remote(part.at[frm], landed.at[frm], g_ss.at[o], g_rs.at[o], (r, frm)).wait_send()
        return carry

    lax.fori_loop(1, 16, sent_all, 0)
    for i, o in enumerate(LINE):
        to = ((z + o[0]) % ZS) * 2 + (core + o[1]) % 2
        remote(z_part.at[to], z_landed.at[r], h_ss.at[i], h_rs.at[i], (to, c)).wait_send()
    leave(x1s, x1r.at[c], x1_ss, x1_rs, peer_c)
    leave(x2s, x2r.at[c], x2_ss, x2_rs, peer_c)
    leave(pt.at[:, group], jp.at[r], p_ss, p_rs, peer_r)
    leave(we.at[:, group], jw.at[r], w_ss, w_rs, peer_r)
    for copy in sent:
        copy.wait_send()


def body(embed, positives, placement):
    dma = pltpu.SemaphoreType.DMA
    return pl.pallas_call(
        kernel,
        out_shape=jax.ShapeDtypeStruct((SHARD, WIDTH), F32),
        in_specs=[pl.BlockSpec(memory_space=pl.ANY)] * 3,
        out_specs=pl.BlockSpec(memory_space=pltpu.VMEM),
        scratch_shapes=[
            pltpu.VMEM((COLS, SHARD, WIDTH), BF16),
            pltpu.VMEM((ROWS, SHARD, WIDTH), BF16),
            pltpu.VMEM((BLOCK, BLOCK), F32),
            pltpu.VMEM((POS, BLOCK, BLOCK), F32),
            pltpu.VMEM((POS, BLOCK, BLOCK), F32),
            pltpu.VMEM((BLOCK, BLOCK), BF16),
            pltpu.VMEM((BLOCK, BLOCK), BF16),
            pltpu.VMEM((COLS, SHARD, BROAD), BF16),
            pltpu.VMEM((COLS, SHARD, BROAD), BF16),
            pltpu.VMEM((8, SHARD, BROAD), F32),
            pltpu.VMEM((ROWS, SHARD, NARROW), BF16),
            pltpu.VMEM((ROWS, SHARD, NARROW), BF16),
            pltpu.VMEM((8, SHARD, NARROW), F32),
            pltpu.VMEM((POS, BLOCK), I32),
            pltpu.VMEM((64, LANES), I32),
            pltpu.VMEM((8, BLOCK), I32),
            pltpu.VMEM((8, BLOCK), F32),
            pltpu.VMEM((8, BLOCK), F32),
            pltpu.VMEM((8, BLOCK // 2), F32),
            pltpu.VMEM((COLS, 8, BLOCK // 2), F32),
            pltpu.VMEM((8, BLOCK), F32),
            pltpu.VMEM((COLS, 8, BLOCK), F32),
            pltpu.VMEM((ROWS, 8, LANES), F32),
            pltpu.VMEM((ROWS, 8, LANES), F32),
            pltpu.VMEM((LANES, LANES), F32),
            pltpu.VMEM((4 * POS, BLOCK, LANES), F32),
            dma((4,)),
            dma((24,)),
            dma((24,)),
        ]
        + [dma((16,))] * 16,
        compiler_params=pltpu.CompilerParams(
            collective_id=0, has_side_effects=True, vmem_limit_bytes=60 * 1024 * 1024
        ),
        cost_estimate=pl.CostEstimate(flops=1 << 31, bytes_accessed=1 << 22, transcendentals=1 << 21),
        name="smooth_ap",
    )(embed, positives.T, placement.reshape(64, LANES))


def solution(mesh):
    return jax.shard_map(
        body,
        mesh=mesh,
        in_specs=(P(("row", "col"), None), P("row", None), P()),
        out_specs=P(("row", "col"), None),
        check_vma=False,
    )
```

```python
import functools

import jax
import jax.numpy as jnp
from jax import lax
from jax.experimental import pallas as pl
from jax.experimental.pallas import tpu as pltpu
from jax.sharding import PartitionSpec as P

MESH = pl.DeviceIdType.MESH
TAU = 0.02
HALF = 0.5 / TAU
F32, BF16, I32 = jnp.float32, jnp.bfloat16, jnp.int32

ROWS, COLS, ZS = 16, 16, 8
SHARD, WIDTH, POS = 32, 1024, 4
BLOCK = SHARD * COLS
LANES = 128
STEP = 64

BROAD, NARROW = 512, 256
LINE_AT, BOTH_AT = BROAD, BROAD + NARROW

LINE = (
    (4, 0), (3, 1), (5, 0), (4, 1), (3, 0), (5, 1), (2, 0), (6, 1),
    (2, 1), (6, 0), (1, 0), (7, 1), (1, 1), (7, 0), (0, 1),
)


def remote(src, dst, send, recv, device):
    return pltpu.make_async_remote_copy(
        src_ref=src, dst_ref=dst, send_sem=send, recv_sem=recv,
        device_id=device, device_id_type=MESH,
    )


def kernel(
    embed, positives, placement, out,
    a_buf, c_buf, s_ref, vi, vj, gi, gj, part, landed, mine, z_part, z_landed, z_mine,
    ez_part, ez_landed, ep_part, ep_landed,
    pos_in, place_in, tgt, pt, we, x1s, x1r, x2s, x2r, jp, jw, jt, jc,
    in_sem, plane_s, plane_r, z_s, z_r, sib_s, sib_r,
    x1_ss, x1_rs, x2_ss, x2_rs, p_ss, p_rs, w_ss, w_rs, g_ss, g_rs, h_ss, h_rs,
    e_ss, e_rs, f_ss, f_rs,
):
    r, c = lax.axis_index("row"), lax.axis_index("col")
    z, core = r // 2, r % 2
    y, x = c // 4, c % 4

    def in_plane(o):
        return (r, ((y + o[0]) % 4) * 4 + (x + o[1]) % 4)

    def in_line(d, k=0):
        return (((z + d) % ZS) * 2 + (core + k) % 2, c)

    loads = [
        pltpu.make_async_copy(embed, a_buf.at[c], in_sem.at[0]),
        pltpu.make_async_copy(embed, c_buf.at[r], in_sem.at[1]),
        pltpu.make_async_copy(positives, pos_in, in_sem.at[2]),
        pltpu.make_async_copy(placement, place_in, in_sem.at[3]),
    ]
    for load in loads:
        load.start()
    barrier = pltpu.get_barrier_semaphore()

    def greet(o, carry):
        pl.semaphore_signal(barrier, inc=1, device_id=(r, c ^ o), device_id_type=MESH)
        pl.semaphore_signal(barrier, inc=1, device_id=(r ^ o, c), device_id_type=MESH)
        return carry

    lax.fori_loop(1, 16, greet, 0)
    for load in loads:
        load.wait()
    pl.semaphore_wait(barrier, 30)

    sent = []

    def go(src, dst, ss, rs, device):
        copy = remote(src, dst, ss, rs, device)
        copy.start()
        sent.append(copy)

    def z_send(d, block, rows, step, slot):
        view = c_buf.at[block, rows]
        go(view, view, z_s.at[slot], z_r.at[slot], in_line(step % ZS))

    def z_wait(d, rows, slot):
        view = c_buf.at[from_z(d), rows]
        remote(view, view, z_s.at[slot], z_r.at[slot], in_line(d % ZS)).wait_recv()

    def from_z(d, k=0):
        return ((z + ZS - d) % ZS) * 2 + (core + k) % 2

    def from_plane(dy, dx):
        return ((y + 4 - dy) % 4) * 4 + (x + 4 - dx) % 4

    def a_send(block, rows, dy, dx, slot):
        view = a_buf.at[block, rows]
        go(view, view, plane_s.at[slot], plane_r.at[slot], in_plane((dy, dx)))

    def a_wait(dy, dx, rows, slot):
        view = a_buf.at[from_plane(dy, dx), rows]
        remote(view, view, plane_s.at[slot], plane_r.at[slot], in_plane((dy, dx))).wait_recv()

    def sib_send(d, rows, slot):
        view = c_buf.at[from_z(d), rows]
        go(view, view, sib_s.at[slot], sib_r.at[slot], in_line(0, 1))

    def sib_wait(d, rows, slot):
        view = c_buf.at[from_z(d, 1), rows]
        remote(view, view, sib_s.at[slot], sib_r.at[slot], in_line(0, 1)).wait_recv()

    every, top, low_half = pl.ds(0, SHARD), pl.ds(0, SHARD // 2), pl.ds(SHARD // 2, SHARD // 2)
    z_send(2, r, every, 2, 2)
    z_send(-2, r, every, -2, 6)
    a_send(c, every, 0, 2, 1)
    a_send(c, every, 2, 0, 4)
    z_send(1, r, every, 1, 1)
    z_send(-1, r, every, -1, 7)
    for d in (1, 3):
        a_send(c, every, 0, d, d - 1)
        a_send(c, every, d, 0, d + 2)
    sib_send(0, every, 0)

    table = place_in[...]
    high = (table // 64).astype(F32).astype(BF16)
    low = (table % 64).astype(F32).astype(BF16)
    lane_id = lax.broadcasted_iota(I32, (LANES, BLOCK), 0)
    row_id = lax.broadcasted_iota(I32, (64, BLOCK), 0)
    for m in range(POS):
        entity = pos_in[m : m + 1, :]
        hot = jnp.where(lane_id == entity % LANES, 1.0, 0.0).astype(BF16)
        value = jnp.dot(high, hot, preferred_element_type=F32) * 64.0 + jnp.dot(
            low, hot, preferred_element_type=F32
        )
        found = jnp.sum(jnp.where(row_id == entity // LANES, value, 0.0), axis=0, keepdims=True)
        pt[POS + m : POS + m + 1, :] = found
        where = found.astype(I32)
        here = (where // SHARD) % COLS == c
        tgt[m : m + 1, :] = jnp.where(here, (where // BLOCK) * SHARD + where % SHARD, -1)

    def turn(d):
        a_wait(0, d, every, d - 1)
        for e in (2, 1, 3):
            a_send(from_plane(0, d), top, e, 0, 6 + 3 * (d - 1) + e - 1)
        a_wait(d, 0, every, d + 2)
        for e in (2, 1, 3):
            a_send(from_plane(d, 0), low_half, 0, e, 15 + 3 * (d - 1) + e - 1)

    turn(1)
    turn(3)
    z_wait(2, every, 2)
    z_send(4, from_z(2), top, 2, 4)
    z_send(3, from_z(2), every, 1, 3)
    z_wait(-2, every, 6)
    z_send(-4, from_z(-2), low_half, -2, 8)
    z_send(-3, from_z(-2), every, -1, 5)
    turn(2)
    for d, slot in ((2, 2), (-2, 6)):
        sib_send(d, every, slot)
    for d, slot in ((1, 1), (-1, 7)):
        z_wait(d, every, slot)
        sib_send(d, every, slot)
    for d, slot in ((3, 3), (-3, 5)):
        z_wait(d, every, slot)
        sib_send(d, every, slot)
    z_wait(4, top, 4)
    sib_send(4, top, 4)
    z_wait(-4, low_half, 8)
    sib_send(-4, low_half, 8)
    for d in (1, 3, 2):
        for e in (1, 3, 2):
            a_wait(e, d, top, 6 + 3 * (d - 1) + e - 1)
            a_wait(d, e, low_half, 15 + 3 * (d - 1) + e - 1)
    for d, slot in ((0, 0), (1, 1), (-1, 7), (2, 2), (-2, 6), (3, 3), (-3, 5)):
        sib_wait(d, every, slot)
    sib_wait(4, top, 4)
    sib_wait(-4, low_half, 8)

    anchors = a_buf[...].reshape(BLOCK, WIDTH)
    for h in range(2):
        cand = c_buf[8 * h : 8 * h + 8].reshape(BLOCK // 2, WIDTH)
        s_ref[256 * h : 256 * h + 256, :] = HALF * lax.dot_general(
            cand, anchors, (((1,), (1,)), ((), ())), preferred_element_type=F32
        )
    tile = s_ref[pl.ds(pl.multiple_of(r * SHARD, SHARD), SHARD), pl.ds(pl.multiple_of(y * LANES, LANES), LANES)]
    me_row = lax.broadcasted_iota(I32, (SHARD, LANES), 0)
    me_lane = lax.broadcasted_iota(I32, (SHARD, LANES), 1)
    s_ref[pl.ds(pl.multiple_of(r * SHARD, SHARD), SHARD), pl.ds(pl.multiple_of(y * LANES, LANES), LANES)] = (
        jnp.where(me_lane - x * SHARD == me_row, -1e30, tile)
    )

    iota_k = lax.broadcasted_iota(I32, (STEP, LANES), 0)
    iota_a = lax.broadcasted_iota(I32, (STEP, LANES), 1)
    steps = BLOCK // STEP

    def fold(value):
        return jnp.sum(value.reshape(STEP // 8, 8, LANES), axis=0)

    def cut(q):
        return slice(q * LANES, (q + 1) * LANES)

    for q in range(4):
        rows = [tgt[m : m + 1, cut(q)] for m in range(POS)]

        def pick(i, acc, q=q, rows=rows):
            k0 = pl.multiple_of(i * STEP, STEP)
            score = s_ref[pl.ds(k0, STEP), cut(q)]
            return tuple(
                acc[m] + fold(jnp.where(iota_k == rows[m] - k0, score, 0.0)) for m in range(POS)
            )

        acc = lax.fori_loop(0, steps, pick, (jnp.zeros((8, LANES), F32),) * POS)
        for m in range(POS):
            half, lane = q // 2, (q % 2) * LANES
            x1s[half * POS + m : half * POS + m + 1, lane : lane + LANES] = jnp.sum(
                acc[m], axis=0, keepdims=True
            )

    def exchange(src, dst, ss, rs, peer):
        def start(o, carry):
            remote(src, dst, ss.at[o], rs.at[o], peer(o)).start()
            return carry

        lax.fori_loop(1, 16, start, 0)

    def arrive(src, dst, ss, rs, peer, index):
        def wait(o, carry):
            remote(src, dst.at[index ^ o], ss.at[o], rs.at[o], peer(o)).wait_recv()
            return carry

        lax.fori_loop(1, 16, wait, 0)

    def leave(src, dst, ss, rs, peer):
        def wait(o, carry):
            remote(src, dst, ss.at[o], rs.at[o], peer(o)).wait_send()
            return carry

        lax.fori_loop(1, 16, wait, 0)

    def peer_c(o):
        return (r, c ^ o)

    def peer_r(o):
        return (r ^ o, c)

    exchange(x1s, x1r.at[c], x1_ss, x1_rs, peer_c)
    x1r[c] = x1s[...]
    arrive(x1s, x1r, x1_ss, x1_rs, peer_c, c)
    total = jnp.sum(x1r[...], axis=0)
    pt[0:POS, 0:256] = total[0:POS]
    pt[0:POS, 256:512] = total[POS : 2 * POS]

    group = pl.ds(pl.multiple_of(y * LANES, LANES), LANES)
    def line_copy(i, part_ref, landed_ref, ss, rs):
        o = LINE[i]
        to = ((z + o[0]) % ZS) * 2 + (core + o[1]) % 2
        return remote(part_ref.at[to], landed_ref.at[r], ss.at[i], rs.at[i], (to, c))

    def line_start(part_ref, landed_ref, ss, rs):
        for i in range(15):
            line_copy(i, part_ref, landed_ref, ss, rs).start()

    def line_sum(part_ref, landed_ref, ss, rs, first):
        for i in reversed(range(15)):
            frm = from_z(*LINE[i])
            remote(part_ref.at[frm], landed_ref.at[frm], ss.at[i], rs.at[i], (frm, c)).wait_recv()
            out[:, first : first + NARROW] += landed_ref[frm].astype(F32)

    def line_sent(part_ref, landed_ref, ss, rs):
        for i in range(15):
            line_copy(i, part_ref, landed_ref, ss, rs).wait_send()

    for q in range(4):
        rows = [pt[m : m + 1, cut(q)] for m in range(POS)]

        def count(i, acc, q=q, rows=rows):
            k0 = pl.multiple_of(i * STEP, STEP)
            score = s_ref[pl.ds(k0, STEP), cut(q)]
            new = []
            for m in range(POS):
                t = jnp.tanh(score - rows[m])
                u = 1.0 + t
                v = 1.0 - t * t
                vi[m, pl.ds(k0, STEP), cut(q)] = v
                new.append(acc[2 * m] + fold(u))
                new.append(acc[2 * m + 1] + fold(v))
            return tuple(new)

        acc = lax.fori_loop(0, steps, count, (jnp.zeros((8, LANES), F32),) * (2 * POS))
        for m in range(POS):
            x2s[m : m + 1, cut(q)] = jnp.sum(acc[2 * m], axis=0, keepdims=True)
            x2s[POS + m : POS + m + 1, cut(q)] = jnp.sum(acc[2 * m + 1], axis=0, keepdims=True)
    exchange(x2s, x2r.at[c], x2_ss, x2_rs, peer_c)
    x2r[c] = x2s[...]
    exchange(pt.at[:, group], jp.at[r], p_ss, p_rs, peer_r)
    jp[r] = pt[:, group]

    def columns(src, first):
        jt[...] = jnp.transpose(src[...].reshape(ROWS * 8, LANES))
        mine_cols = jt[pl.ds(pl.multiple_of(x * SHARD, SHARD), SHARD), :]
        for b in range(ROWS):
            for n in range(8):
                jc[first + n, b * SHARD : (b + 1) * SHARD, :] = jnp.broadcast_to(
                    mine_cols[:, b * 8 + n : b * 8 + n + 1], (SHARD, LANES)
                )

    arrive(x2s, x2r, x2_ss, x2_rs, peer_c, c)
    total = jnp.sum(x2r[...], axis=0)
    factor = 1.0 / (POS * SHARD * ROWS * COLS)
    p = [pt[m : m + 1, :] for m in range(POS)]
    rank = [0.5 + 0.5 * total[m : m + 1] for m in range(POS)]
    slope = [0.25 * total[POS + m : POS + m + 1] for m in range(POS)]
    prank = [jnp.full((1, BLOCK), 1.0, F32) for _ in range(POS)]
    grad = [-factor / rank[m] for m in range(POS)]
    pulled = [jnp.zeros((1, BLOCK), F32) for _ in range(POS)]
    for m in range(POS):
        for n in range(m + 1, POS):
            t = jnp.tanh(p[n] - p[m])
            prank[m] = prank[m] + 0.5 * (1.0 + t)
            prank[n] = prank[n] + 0.5 * (1.0 - t)
            pair = (0.25 / TAU) * (1.0 - t) * (1.0 + t) * (grad[n] - grad[m])
            pulled[m] = pulled[m] + pair
            pulled[n] = pulled[n] - pair
    for m in range(POS):
        weight = prank[m] / (rank[m] * rank[m]) * factor / TAU
        we[m : m + 1, :] = 0.25 * weight
        we[POS + m : POS + m + 1, :] = pulled[m] - weight * slope[m]

    exchange(we.at[:, group], jw.at[r], w_ss, w_rs, peer_r)
    jw[r] = we[:, group]

    for q in range(4):
        rows = [tgt[m : m + 1, cut(q)] for m in range(POS)]
        weights = [we[m : m + 1, cut(q)] for m in range(POS)]
        extras = [we[POS + m : POS + m + 1, cut(q)] for m in range(POS)]

        def tile_i(i, carry, q=q, rows=rows, weights=weights, extras=extras):
            k0 = pl.multiple_of(i * STEP, STEP)
            dense = weights[0] * vi[0, pl.ds(k0, STEP), cut(q)]
            for m in range(1, POS):
                dense = dense + weights[m] * vi[m, pl.ds(k0, STEP), cut(q)]
            for m in range(POS):
                dense = dense + jnp.where(iota_k == rows[m] - k0, extras[m], 0.0)
            gi[pl.ds(k0, STEP), cut(q)] = dense.astype(BF16)
            return carry

        lax.fori_loop(0, steps, tile_i, 0)

    early_line = a_buf[:, :, BOTH_AT:].reshape(BLOCK, NARROW)
    early_plane = c_buf[:, :, BOTH_AT:].reshape(BLOCK, NARROW)
    over_rows = (((0,), (0,)), ((), ()))
    for h in range(2):
        rows = slice(256 * h, 256 * h + 256)
        product = jnp.dot(gi[rows, :], early_line, preferred_element_type=F32)
        ez_part[8 * h : 8 * h + 8] = product.astype(BF16).reshape(8, SHARD, NARROW)

        @pl.when(r // 8 == h)
        def _(product=product):
            z_mine[...] = product.reshape(8, SHARD, NARROW)

    line_start(ez_part, ez_landed, e_ss, e_rs)
    out[:, BOTH_AT:] = z_mine[r % 8]
    for h in range(2):
        rows = slice(256 * h, 256 * h + 256)
        product = lax.dot_general(gi[:, rows], early_plane, over_rows, preferred_element_type=F32)
        ep_part[8 * h : 8 * h + 8] = product.astype(BF16).reshape(8, SHARD, NARROW)

        @pl.when(c // 8 == h)
        def _(product=product):
            z_mine[...] = product.reshape(8, SHARD, NARROW)

    def early_push(n, carry):
        to = c ^ (16 - n)
        remote(ep_part.at[to], ep_landed.at[c], f_ss.at[16 - n], f_rs.at[16 - n], (r, to)).start()
        return carry

    lax.fori_loop(1, 16, early_push, 0)
    out[:, BOTH_AT:] += z_mine[c % 8]

    arrive(pt.at[:, group], jp, p_ss, p_rs, peer_r, r)
    columns(jp, 0)

    def slopes(i, carry):
        k0 = pl.multiple_of(i * STEP, STEP)
        for m in range(POS):
            col = jc[m, pl.ds(k0, STEP), :]
            for q in range(4):
                t = jnp.tanh(s_ref[pl.ds(k0, STEP), cut(q)] - col)
                vj[m, pl.ds(k0, STEP), cut(q)] = 1.0 - t * t
            where = jc[POS + m, pl.ds(k0, STEP), :].astype(I32)
            jc[POS + m, pl.ds(k0, STEP), :] = jnp.where(
                where // BLOCK == r, where % BLOCK, -1
            ).astype(F32)
        return carry

    lax.fori_loop(0, steps, slopes, 0)

    arrive(we.at[:, group], jw, w_ss, w_rs, peer_r, r)
    columns(jw, 2 * POS)

    def tile_j(i, carry):
        k0 = pl.multiple_of(i * STEP, STEP)
        for q in range(4):
            dense = jc[2 * POS, pl.ds(k0, STEP), :] * vj[0, pl.ds(k0, STEP), cut(q)]
            for m in range(1, POS):
                dense = dense + jc[2 * POS + m, pl.ds(k0, STEP), :] * vj[m, pl.ds(k0, STEP), cut(q)]
            lane = (iota_a + q * LANES).astype(F32)
            for m in range(POS):
                dense = dense + jnp.where(
                    jc[POS + m, pl.ds(k0, STEP), :] == lane,
                    jc[3 * POS + m, pl.ds(k0, STEP), :],
                    0.0,
                )
            gj[pl.ds(k0, STEP), cut(q)] = dense.astype(BF16)
        return carry

    lax.fori_loop(0, steps, tile_j, 0)

    right = a_buf[:, :, LINE_AT:BOTH_AT].reshape(BLOCK, NARROW)
    for h in range(2):
        rows = slice(256 * h, 256 * h + 256)
        product = jnp.dot(gi[rows, :], right, preferred_element_type=F32)
        product = product + jnp.dot(gj[rows, :], right, preferred_element_type=F32)
        z_part[8 * h : 8 * h + 8] = product.astype(BF16).reshape(8, SHARD, NARROW)

        @pl.when(r // 8 == h)
        def _(product=product):
            z_mine[...] = product.reshape(8, SHARD, NARROW)

    line_start(z_part, z_landed, h_ss, h_rs)

    left = c_buf[:, :, :BROAD].reshape(BLOCK, BROAD)
    wide = 2 * LANES
    for turn_id in range(2):
        h = (c // 8) ^ (1 - turn_id)
        half = pl.ds(pl.multiple_of(h * wide, wide), wide)
        product = lax.dot_general(gi[:, half], left, over_rows, preferred_element_type=F32)
        product = product + lax.dot_general(gj[:, half], left, over_rows, preferred_element_type=F32)
        part[pl.ds(h * 8, 8)] = product.astype(BF16).reshape(8, SHARD, BROAD)
        if turn_id == 1:
            mine[...] = product.reshape(8, SHARD, BROAD)

        def push(n, carry):
            to = c ^ n
            remote(part.at[to], landed.at[c], g_ss.at[n], g_rs.at[n], (r, to)).start()
            return carry

        lax.fori_loop(*((8, 16) if turn_id == 0 else (1, 8)), push, 0)

    out[:, :BROAD] = mine[c % 8]
    out[:, LINE_AT:BOTH_AT] = z_mine[r % 8]

    def plane_sum(part_ref, landed_ref, ss, rs, first, width):
        def add(o, carry):
            frm = c ^ o
            remote(part_ref.at[frm], landed_ref.at[frm], ss.at[o], rs.at[o], (r, frm)).wait_recv()
            out[:, first : first + width] += landed_ref[frm].astype(F32)
            return carry

        lax.fori_loop(1, 16, add, 0)

    def plane_sent(part_ref, landed_ref, ss, rs):
        def wait(o, carry):
            frm = c ^ o
            remote(part_ref.at[frm], landed_ref.at[frm], ss.at[o], rs.at[o], (r, frm)).wait_send()
            return carry

        lax.fori_loop(1, 16, wait, 0)

    line_sum(ez_part, ez_landed, e_ss, e_rs, BOTH_AT)
    plane_sum(ep_part, ep_landed, f_ss, f_rs, BOTH_AT, NARROW)
    line_sent(ez_part, ez_landed, e_ss, e_rs)
    plane_sent(ep_part, ep_landed, f_ss, f_rs)
    leave(x1s, x1r.at[c], x1_ss, x1_rs, peer_c)
    leave(x2s, x2r.at[c], x2_ss, x2_rs, peer_c)
    leave(pt.at[:, group], jp.at[r], p_ss, p_rs, peer_r)
    leave(we.at[:, group], jw.at[r], w_ss, w_rs, peer_r)
    for copy in sent:
        copy.wait_send()
    line_sum(z_part, z_landed, h_ss, h_rs, LINE_AT)
    plane_sum(part, landed, g_ss, g_rs, 0, BROAD)
    line_sent(z_part, z_landed, h_ss, h_rs)
    plane_sent(part, landed, g_ss, g_rs)


def body(embed, positives, placement):
    dma = pltpu.SemaphoreType.DMA
    return pl.pallas_call(
        kernel,
        out_shape=jax.ShapeDtypeStruct((SHARD, WIDTH), F32),
        in_specs=[pl.BlockSpec(memory_space=pl.ANY)] * 3,
        out_specs=pl.BlockSpec(memory_space=pltpu.VMEM),
        scratch_shapes=[
            pltpu.VMEM((COLS, SHARD, WIDTH), BF16),
            pltpu.VMEM((ROWS, SHARD, WIDTH), BF16),
            pltpu.VMEM((BLOCK, BLOCK), F32),
            pltpu.VMEM((POS, BLOCK, BLOCK), F32),
            pltpu.VMEM((POS, BLOCK, BLOCK), F32),
            pltpu.VMEM((BLOCK, BLOCK), BF16),
            pltpu.VMEM((BLOCK, BLOCK), BF16),
            pltpu.VMEM((COLS, SHARD, BROAD), BF16),
            pltpu.VMEM((COLS, SHARD, BROAD), BF16),
            pltpu.VMEM((8, SHARD, BROAD), F32),
            pltpu.VMEM((ROWS, SHARD, NARROW), BF16),
            pltpu.VMEM((ROWS, SHARD, NARROW), BF16),
            pltpu.VMEM((8, SHARD, NARROW), F32),
            pltpu.VMEM((ROWS, SHARD, NARROW), BF16),
            pltpu.VMEM((ROWS, SHARD, NARROW), BF16),
            pltpu.VMEM((COLS, SHARD, NARROW), BF16),
            pltpu.VMEM((COLS, SHARD, NARROW), BF16),
            pltpu.VMEM((POS, BLOCK), I32),
            pltpu.VMEM((64, LANES), I32),
            pltpu.VMEM((8, BLOCK), I32),
            pltpu.VMEM((8, BLOCK), F32),
            pltpu.VMEM((8, BLOCK), F32),
            pltpu.VMEM((8, BLOCK // 2), F32),
            pltpu.VMEM((COLS, 8, BLOCK // 2), F32),
            pltpu.VMEM((8, BLOCK), F32),
            pltpu.VMEM((COLS, 8, BLOCK), F32),
            pltpu.VMEM((ROWS, 8, LANES), F32),
            pltpu.VMEM((ROWS, 8, LANES), F32),
            pltpu.VMEM((LANES, LANES), F32),
            pltpu.VMEM((4 * POS, BLOCK, LANES), F32),
            dma((4,)),
            dma((24,)),
            dma((24,)),
        ]
        + [dma((16,))] * 20,
        compiler_params=pltpu.CompilerParams(
            collective_id=0, has_side_effects=True, vmem_limit_bytes=60 * 1024 * 1024
        ),
        cost_estimate=pl.CostEstimate(flops=1 << 31, bytes_accessed=1 << 22, transcendentals=1 << 21),
        name="smooth_ap",
    )(embed, positives.T, placement.reshape(64, LANES))


def solution(mesh):
    return jax.shard_map(
        body,
        mesh=mesh,
        in_specs=(P(("row", "col"), None), P("row", None), P()),
        out_specs=P(("row", "col"), None),
        check_vma=False,
    )
```

```python
import functools

import jax
import jax.numpy as jnp
from jax import lax
from jax.experimental import pallas as pl
from jax.experimental.pallas import tpu as pltpu
from jax.sharding import PartitionSpec as P

MESH = pl.DeviceIdType.MESH
TAU = 0.02
HALF = 0.5 / TAU
F32, BF16, I32 = jnp.float32, jnp.bfloat16, jnp.int32

ROWS, COLS, ZS = 16, 16, 8
SHARD, WIDTH, POS = 32, 1024, 4
BLOCK = SHARD * COLS
LANES = 128
STEP = 64

BROAD, NARROW, EARLY = 384, 256, 384
LINE_AT, BOTH_AT = BROAD, BROAD + NARROW

DEPTHS = (4, 3, 5, 2, 6, 1, 7)
PLANE = (10, 11, 14, 9, 6, 8, 2, 15, 13, 7, 5, 12, 4, 3, 1)
LINE = (8, 9, 10, 11, 6, 7, 14, 15, 12, 13, 4, 5, 2, 3, 1)


def remote(src, dst, send, recv, device):
    return pltpu.make_async_remote_copy(
        src_ref=src, dst_ref=dst, send_sem=send, recv_sem=recv,
        device_id=device, device_id_type=MESH,
    )


def kernel(
    embed, positives, placement, out,
    a_buf, c_buf, s_ref, vi, vj, gi, gj, part, landed, mine, z_part, z_landed, z_whole, z_other,
    ez_part, ez_landed, e_whole, e_other, ep_part, ep_landed,
    pos_in, place_in, tgt, pt, we, x1s, x1r, x2s, x2r, jp, jw, jt, jc,
    in_sem, z_sem, e_sem, plane_s, plane_r, z_s, z_r, sib_s, sib_r,
    x1_ss, x1_rs, x2_ss, x2_rs, p_ss, p_rs, w_ss, w_rs, g_ss, g_rs, h_ss, h_rs,
    e_ss, e_rs, f_ss, f_rs,
):
    r, c = lax.axis_index("row"), lax.axis_index("col")
    z, core = r // 2, r % 2
    y, x = c // 4, c % 4

    def in_plane(o):
        return (r, ((y + o[0]) % 4) * 4 + (x + o[1]) % 4)

    def in_line(d, k=0):
        return (((z + d) % ZS) * 2 + (core + k) % 2, c)

    loads = [
        pltpu.make_async_copy(embed, a_buf.at[c], in_sem.at[0]),
        pltpu.make_async_copy(embed, c_buf.at[r], in_sem.at[1]),
        pltpu.make_async_copy(positives, pos_in, in_sem.at[2]),
        pltpu.make_async_copy(placement, place_in, in_sem.at[3]),
    ]
    for load in loads:
        load.start()
    barrier = pltpu.get_barrier_semaphore()

    def greet(o, carry):
        pl.semaphore_signal(barrier, inc=1, device_id=(r, c ^ o), device_id_type=MESH)
        pl.semaphore_signal(barrier, inc=1, device_id=(r ^ o, c), device_id_type=MESH)
        return carry

    lax.fori_loop(1, 16, greet, 0)
    for load in loads:
        load.wait()
    pl.semaphore_wait(barrier, 30)

    sent = []

    def go(src, dst, ss, rs, device):
        copy = remote(src, dst, ss, rs, device)
        copy.start()
        sent.append(copy)

    def z_send(d, block, rows, step, slot):
        view = c_buf.at[block, rows]
        go(view, view, z_s.at[slot], z_r.at[slot], in_line(step % ZS))

    def z_wait(d, rows, slot):
        view = c_buf.at[from_z(d), rows]
        remote(view, view, z_s.at[slot], z_r.at[slot], in_line(d % ZS)).wait_recv()

    def from_z(d, k=0):
        return ((z + ZS - d) % ZS) * 2 + (core + k) % 2

    def from_plane(dy, dx):
        return ((y + 4 - dy) % 4) * 4 + (x + 4 - dx) % 4

    def a_send(block, rows, dy, dx, slot):
        view = a_buf.at[block, rows]
        go(view, view, plane_s.at[slot], plane_r.at[slot], in_plane((dy, dx)))

    def a_wait(dy, dx, rows, slot):
        view = a_buf.at[from_plane(dy, dx), rows]
        remote(view, view, plane_s.at[slot], plane_r.at[slot], in_plane((dy, dx))).wait_recv()

    def sib_send(d, rows, slot):
        view = c_buf.at[from_z(d), rows]
        go(view, view, sib_s.at[slot], sib_r.at[slot], in_line(0, 1))

    def sib_wait(d, rows, slot):
        view = c_buf.at[from_z(d, 1), rows]
        remote(view, view, sib_s.at[slot], sib_r.at[slot], in_line(0, 1)).wait_recv()

    every, top, low_half = pl.ds(0, SHARD), pl.ds(0, SHARD // 2), pl.ds(SHARD // 2, SHARD // 2)
    z_send(2, r, every, 2, 2)
    z_send(-2, r, every, -2, 6)
    a_send(c, every, 0, 2, 1)
    a_send(c, every, 2, 0, 4)
    z_send(1, r, every, 1, 1)
    z_send(-1, r, every, -1, 7)
    for d in (1, 3):
        a_send(c, every, 0, d, d - 1)
        a_send(c, every, d, 0, d + 2)
    sib_send(0, every, 0)

    table = place_in[...]
    high = (table // 64).astype(F32).astype(BF16)
    low = (table % 64).astype(F32).astype(BF16)
    lane_id = lax.broadcasted_iota(I32, (LANES, BLOCK), 0)
    row_id = lax.broadcasted_iota(I32, (64, BLOCK), 0)
    for m in range(POS):
        entity = pos_in[m : m + 1, :]
        hot = jnp.where(lane_id == entity % LANES, 1.0, 0.0).astype(BF16)
        value = jnp.dot(high, hot, preferred_element_type=F32) * 64.0 + jnp.dot(
            low, hot, preferred_element_type=F32
        )
        found = jnp.sum(jnp.where(row_id == entity // LANES, value, 0.0), axis=0, keepdims=True)
        pt[POS + m : POS + m + 1, :] = found
        where = found.astype(I32)
        here = (where // SHARD) % COLS == c
        tgt[m : m + 1, :] = jnp.where(here, (where // BLOCK) * SHARD + where % SHARD, -1)

    def turn(d):
        a_wait(0, d, every, d - 1)
        for e in (2, 1, 3):
            a_send(from_plane(0, d), top, e, 0, 6 + 3 * (d - 1) + e - 1)
        a_wait(d, 0, every, d + 2)
        for e in (2, 1, 3):
            a_send(from_plane(d, 0), low_half, 0, e, 15 + 3 * (d - 1) + e - 1)

    turn(1)
    turn(3)
    z_wait(2, every, 2)
    z_send(4, from_z(2), top, 2, 4)
    z_send(3, from_z(2), every, 1, 3)
    z_wait(-2, every, 6)
    z_send(-4, from_z(-2), low_half, -2, 8)
    z_send(-3, from_z(-2), every, -1, 5)
    turn(2)
    for d, slot in ((2, 2), (-2, 6)):
        sib_send(d, every, slot)
    for d, slot in ((1, 1), (-1, 7)):
        z_wait(d, every, slot)
        sib_send(d, every, slot)
    for d, slot in ((3, 3), (-3, 5)):
        z_wait(d, every, slot)
        sib_send(d, every, slot)
    z_wait(4, top, 4)
    sib_send(4, top, 4)
    z_wait(-4, low_half, 8)
    sib_send(-4, low_half, 8)
    for d in (1, 3, 2):
        for e in (1, 3, 2):
            a_wait(e, d, top, 6 + 3 * (d - 1) + e - 1)
            a_wait(d, e, low_half, 15 + 3 * (d - 1) + e - 1)
    for d, slot in ((0, 0), (1, 1), (-1, 7), (2, 2), (-2, 6), (3, 3), (-3, 5)):
        sib_wait(d, every, slot)
    sib_wait(4, top, 4)
    sib_wait(-4, low_half, 8)

    anchors = a_buf[...].reshape(BLOCK, WIDTH)
    for h in range(2):
        cand = c_buf[8 * h : 8 * h + 8].reshape(BLOCK // 2, WIDTH)
        s_ref[256 * h : 256 * h + 256, :] = HALF * lax.dot_general(
            cand, anchors, (((1,), (1,)), ((), ())), preferred_element_type=F32
        )
    tile = s_ref[pl.ds(pl.multiple_of(r * SHARD, SHARD), SHARD), pl.ds(pl.multiple_of(y * LANES, LANES), LANES)]
    me_row = lax.broadcasted_iota(I32, (SHARD, LANES), 0)
    me_lane = lax.broadcasted_iota(I32, (SHARD, LANES), 1)
    s_ref[pl.ds(pl.multiple_of(r * SHARD, SHARD), SHARD), pl.ds(pl.multiple_of(y * LANES, LANES), LANES)] = (
        jnp.where(me_lane - x * SHARD == me_row, -1e30, tile)
    )

    iota_k = lax.broadcasted_iota(I32, (STEP, LANES), 0)
    iota_a = lax.broadcasted_iota(I32, (STEP, LANES), 1)
    steps = BLOCK // STEP

    def fold(value):
        return jnp.sum(value.reshape(STEP // 8, 8, LANES), axis=0)

    def cut(q):
        return slice(q * LANES, (q + 1) * LANES)

    for q in range(4):
        rows = [tgt[m : m + 1, cut(q)] for m in range(POS)]

        def pick(i, acc, q=q, rows=rows):
            k0 = pl.multiple_of(i * STEP, STEP)
            score = s_ref[pl.ds(k0, STEP), cut(q)]
            return tuple(
                acc[m] + fold(jnp.where(iota_k == rows[m] - k0, score, 0.0)) for m in range(POS)
            )

        acc = lax.fori_loop(0, steps, pick, (jnp.zeros((8, LANES), F32),) * POS)
        for m in range(POS):
            half, lane = q // 2, (q % 2) * LANES
            x1s[half * POS + m : half * POS + m + 1, lane : lane + LANES] = jnp.sum(
                acc[m], axis=0, keepdims=True
            )

    def exchange(src, dst, ss, rs, peer, order):
        for o in order:
            remote(src, dst, ss.at[o], rs.at[o], peer(o)).start()

    def arrive(src, dst, ss, rs, peer, index):
        def wait(o, carry):
            remote(src, dst.at[index ^ o], ss.at[o], rs.at[o], peer(o)).wait_recv()
            return carry

        lax.fori_loop(1, 16, wait, 0)

    def leave(src, dst, ss, rs, peer):
        def wait(o, carry):
            remote(src, dst, ss.at[o], rs.at[o], peer(o)).wait_send()
            return carry

        lax.fori_loop(1, 16, wait, 0)

    def peer_c(o):
        return (r, c ^ o)

    def peer_r(o):
        return (r ^ o, c)

    exchange(x1s, x1r.at[c], x1_ss, x1_rs, peer_c, PLANE)
    x1r[c] = x1s[...]
    arrive(x1s, x1r, x1_ss, x1_rs, peer_c, c)
    total = jnp.sum(x1r[...], axis=0)
    pt[0:POS, 0:256] = total[0:POS]
    pt[0:POS, 256:512] = total[POS : 2 * POS]

    group = pl.ds(pl.multiple_of(y * LANES, LANES), LANES)
    def line_meet(tiles, columns, whole, other, sem):
        for h in range(2):
            rows = slice(256 * h, 256 * h + 256)
            product = sum(jnp.dot(g[rows, :], columns, preferred_element_type=F32) for g in tiles)
            whole[4 * h : 4 * h + 4] = product.reshape(4, 2, SHARD, product.shape[1])
        remote(whole.at[:, 1 - core], other, sem.at[0], sem.at[1], (r ^ 1, c)).start()

    def line_go(whole, other, part_ref, landed_ref, sem, ss, rs):
        meet = remote(whole.at[:, 1 - core], other, sem.at[0], sem.at[1], (r ^ 1, c))
        meet.wait_recv()
        part_ref[...] = (whole[:, core] + other[...]).astype(BF16)
        for d in DEPTHS:
            to = (z + d) % ZS
            remote(part_ref.at[to], landed_ref.at[z], ss.at[d], rs.at[d], in_line(d)).start()
        meet.wait_send()
        return whole[z, core] + other[z]

    def line_sum(landed_ref, ss, rs, first, width):
        for d in reversed(DEPTHS):
            frm = (z + ZS - d) % ZS
            remote(landed_ref.at[frm], landed_ref.at[frm], ss.at[d], rs.at[d], in_line(d)).wait_recv()
            out[:, first : first + width] += landed_ref[frm].astype(F32)

    def line_sent(part_ref, landed_ref, ss, rs):
        for d in DEPTHS:
            to = (z + d) % ZS
            remote(part_ref.at[to], landed_ref.at[z], ss.at[d], rs.at[d], in_line(d)).wait_send()

    for q in range(4):
        rows = [pt[m : m + 1, cut(q)] for m in range(POS)]

        def count(i, acc, q=q, rows=rows):
            k0 = pl.multiple_of(i * STEP, STEP)
            score = s_ref[pl.ds(k0, STEP), cut(q)]
            new = []
            for m in range(POS):
                t = jnp.tanh(score - rows[m])
                u = 1.0 + t
                v = 1.0 - t * t
                vi[m, pl.ds(k0, STEP), cut(q)] = v
                new.append(acc[2 * m] + fold(u))
                new.append(acc[2 * m + 1] + fold(v))
            return tuple(new)

        acc = lax.fori_loop(0, steps, count, (jnp.zeros((8, LANES), F32),) * (2 * POS))
        for m in range(POS):
            x2s[m : m + 1, cut(q)] = jnp.sum(acc[2 * m], axis=0, keepdims=True)
            x2s[POS + m : POS + m + 1, cut(q)] = jnp.sum(acc[2 * m + 1], axis=0, keepdims=True)
    exchange(x2s, x2r.at[c], x2_ss, x2_rs, peer_c, PLANE)
    x2r[c] = x2s[...]
    exchange(pt.at[:, group], jp.at[r], p_ss, p_rs, peer_r, LINE)
    jp[r] = pt[:, group]

    def columns(src, first):
        jt[...] = jnp.transpose(src[...].reshape(ROWS * 8, LANES))
        mine_cols = jt[pl.ds(pl.multiple_of(x * SHARD, SHARD), SHARD), :]
        for b in range(ROWS):
            for n in range(8):
                jc[first + n, b * SHARD : (b + 1) * SHARD, :] = jnp.broadcast_to(
                    mine_cols[:, b * 8 + n : b * 8 + n + 1], (SHARD, LANES)
                )

    arrive(x2s, x2r, x2_ss, x2_rs, peer_c, c)
    total = jnp.sum(x2r[...], axis=0)
    factor = 1.0 / (POS * SHARD * ROWS * COLS)
    p = [pt[m : m + 1, :] for m in range(POS)]
    rank = [0.5 + 0.5 * total[m : m + 1] for m in range(POS)]
    slope = [0.25 * total[POS + m : POS + m + 1] for m in range(POS)]
    prank = [jnp.full((1, BLOCK), 1.0, F32) for _ in range(POS)]
    grad = [-factor / rank[m] for m in range(POS)]
    pulled = [jnp.zeros((1, BLOCK), F32) for _ in range(POS)]
    for m in range(POS):
        for n in range(m + 1, POS):
            t = jnp.tanh(p[n] - p[m])
            prank[m] = prank[m] + 0.5 * (1.0 + t)
            prank[n] = prank[n] + 0.5 * (1.0 - t)
            pair = (0.25 / TAU) * (1.0 - t) * (1.0 + t) * (grad[n] - grad[m])
            pulled[m] = pulled[m] + pair
            pulled[n] = pulled[n] - pair
    for m in range(POS):
        weight = prank[m] / (rank[m] * rank[m]) * factor / TAU
        we[m : m + 1, :] = 0.25 * weight
        we[POS + m : POS + m + 1, :] = pulled[m] - weight * slope[m]

    exchange(we.at[:, group], jw.at[r], w_ss, w_rs, peer_r, LINE)
    jw[r] = we[:, group]

    for q in range(4):
        rows = [tgt[m : m + 1, cut(q)] for m in range(POS)]
        weights = [we[m : m + 1, cut(q)] for m in range(POS)]
        extras = [we[POS + m : POS + m + 1, cut(q)] for m in range(POS)]

        def tile_i(i, carry, q=q, rows=rows, weights=weights, extras=extras):
            k0 = pl.multiple_of(i * STEP, STEP)
            dense = weights[0] * vi[0, pl.ds(k0, STEP), cut(q)]
            for m in range(1, POS):
                dense = dense + weights[m] * vi[m, pl.ds(k0, STEP), cut(q)]
            for m in range(POS):
                dense = dense + jnp.where(iota_k == rows[m] - k0, extras[m], 0.0)
            gi[pl.ds(k0, STEP), cut(q)] = dense.astype(BF16)
            return carry

        lax.fori_loop(0, steps, tile_i, 0)

    over_rows = (((0,), (0,)), ((), ()))
    line_meet((gi,), a_buf[:, :, BOTH_AT:].reshape(BLOCK, EARLY), e_whole, e_other, e_sem)
    early_plane = c_buf[:, :, BOTH_AT:].reshape(BLOCK, EARLY)
    for h in range(2):
        rows = slice(256 * h, 256 * h + 256)
        product = lax.dot_general(gi[:, rows], early_plane, over_rows, preferred_element_type=F32)
        ep_part[8 * h : 8 * h + 8] = product.astype(BF16).reshape(8, SHARD, EARLY)

        @pl.when(c // 8 == h)
        def _(product=product):
            mine[...] = product.reshape(8, SHARD, EARLY)

    for o in PLANE:
        remote(ep_part.at[c ^ o], ep_landed.at[c], f_ss.at[o], f_rs.at[o], (r, c ^ o)).start()
    out[:, BOTH_AT:] = mine[c % 8]
    out[:, BOTH_AT:] += line_go(e_whole, e_other, ez_part, ez_landed, e_sem, e_ss, e_rs)

    arrive(pt.at[:, group], jp, p_ss, p_rs, peer_r, r)
    columns(jp, 0)

    def slopes(i, carry):
        k0 = pl.multiple_of(i * STEP, STEP)
        for m in range(POS):
            col = jc[m, pl.ds(k0, STEP), :]
            for q in range(4):
                t = jnp.tanh(s_ref[pl.ds(k0, STEP), cut(q)] - col)
                vj[m, pl.ds(k0, STEP), cut(q)] = 1.0 - t * t
            where = jc[POS + m, pl.ds(k0, STEP), :].astype(I32)
            jc[POS + m, pl.ds(k0, STEP), :] = jnp.where(
                where // BLOCK == r, where % BLOCK, -1
            ).astype(F32)
        return carry

    lax.fori_loop(0, steps, slopes, 0)

    arrive(we.at[:, group], jw, w_ss, w_rs, peer_r, r)
    columns(jw, 2 * POS)

    def tile_j(i, carry):
        k0 = pl.multiple_of(i * STEP, STEP)
        for q in range(4):
            dense = jc[2 * POS, pl.ds(k0, STEP), :] * vj[0, pl.ds(k0, STEP), cut(q)]
            for m in range(1, POS):
                dense = dense + jc[2 * POS + m, pl.ds(k0, STEP), :] * vj[m, pl.ds(k0, STEP), cut(q)]
            lane = (iota_a + q * LANES).astype(F32)
            for m in range(POS):
                dense = dense + jnp.where(
                    jc[POS + m, pl.ds(k0, STEP), :] == lane,
                    jc[3 * POS + m, pl.ds(k0, STEP), :],
                    0.0,
                )
            gj[pl.ds(k0, STEP), cut(q)] = dense.astype(BF16)
        return carry

    lax.fori_loop(0, steps, tile_j, 0)

    line_meet((gi, gj), a_buf[:, :, LINE_AT:BOTH_AT].reshape(BLOCK, NARROW), z_whole, z_other, z_sem)

    left = c_buf[:, :, :BROAD].reshape(BLOCK, BROAD)
    wide = 2 * LANES
    for turn_id in range(2):
        h = (c // 8) ^ (1 - turn_id)
        half = pl.ds(pl.multiple_of(h * wide, wide), wide)
        product = lax.dot_general(gi[:, half], left, over_rows, preferred_element_type=F32)
        product = product + lax.dot_general(gj[:, half], left, over_rows, preferred_element_type=F32)
        part[pl.ds(h * 8, 8)] = product.astype(BF16).reshape(8, SHARD, BROAD)
        if turn_id == 1:
            mine[...] = product.reshape(8, SHARD, BROAD)

        for o in PLANE:
            if (o < 8) == (turn_id == 1):
                remote(part.at[c ^ o], landed.at[c], g_ss.at[o], g_rs.at[o], (r, c ^ o)).start()

    out[:, :BROAD] = mine[c % 8]
    out[:, LINE_AT:BOTH_AT] = line_go(z_whole, z_other, z_part, z_landed, z_sem, h_ss, h_rs)

    def plane_sum(part_ref, landed_ref, ss, rs, first, width):
        def add(o, carry):
            frm = c ^ o
            remote(part_ref.at[frm], landed_ref.at[frm], ss.at[o], rs.at[o], (r, frm)).wait_recv()
            out[:, first : first + width] += landed_ref[frm].astype(F32)
            return carry

        lax.fori_loop(1, 16, add, 0)

    def plane_sent(part_ref, landed_ref, ss, rs):
        def wait(o, carry):
            frm = c ^ o
            remote(part_ref.at[frm], landed_ref.at[frm], ss.at[o], rs.at[o], (r, frm)).wait_send()
            return carry

        lax.fori_loop(1, 16, wait, 0)

    line_sum(ez_landed, e_ss, e_rs, BOTH_AT, EARLY)
    plane_sum(ep_part, ep_landed, f_ss, f_rs, BOTH_AT, EARLY)
    line_sent(ez_part, ez_landed, e_ss, e_rs)
    plane_sent(ep_part, ep_landed, f_ss, f_rs)
    leave(x1s, x1r.at[c], x1_ss, x1_rs, peer_c)
    leave(x2s, x2r.at[c], x2_ss, x2_rs, peer_c)
    leave(pt.at[:, group], jp.at[r], p_ss, p_rs, peer_r)
    leave(we.at[:, group], jw.at[r], w_ss, w_rs, peer_r)
    for copy in sent:
        copy.wait_send()
    line_sum(z_landed, h_ss, h_rs, LINE_AT, NARROW)
    plane_sum(part, landed, g_ss, g_rs, 0, BROAD)
    line_sent(z_part, z_landed, h_ss, h_rs)
    plane_sent(part, landed, g_ss, g_rs)


def body(embed, positives, placement):
    dma = pltpu.SemaphoreType.DMA
    return pl.pallas_call(
        kernel,
        out_shape=jax.ShapeDtypeStruct((SHARD, WIDTH), F32),
        in_specs=[pl.BlockSpec(memory_space=pl.ANY)] * 3,
        out_specs=pl.BlockSpec(memory_space=pltpu.VMEM),
        scratch_shapes=[
            pltpu.VMEM((COLS, SHARD, WIDTH), BF16),
            pltpu.VMEM((ROWS, SHARD, WIDTH), BF16),
            pltpu.VMEM((BLOCK, BLOCK), F32),
            pltpu.VMEM((POS, BLOCK, BLOCK), F32),
            pltpu.VMEM((POS, BLOCK, BLOCK), F32),
            pltpu.VMEM((BLOCK, BLOCK), BF16),
            pltpu.VMEM((BLOCK, BLOCK), BF16),
            pltpu.VMEM((COLS, SHARD, BROAD), BF16),
            pltpu.VMEM((COLS, SHARD, BROAD), BF16),
            pltpu.VMEM((8, SHARD, BROAD), F32),
            pltpu.VMEM((ZS, SHARD, NARROW), BF16),
            pltpu.VMEM((ZS, SHARD, NARROW), BF16),
            pltpu.VMEM((ZS, 2, SHARD, NARROW), F32),
            pltpu.VMEM((ZS, SHARD, NARROW), F32),
            pltpu.VMEM((ZS, SHARD, EARLY), BF16),
            pltpu.VMEM((ZS, SHARD, EARLY), BF16),
            pltpu.VMEM((ZS, 2, SHARD, EARLY), F32),
            pltpu.VMEM((ZS, SHARD, EARLY), F32),
            pltpu.VMEM((COLS, SHARD, EARLY), BF16),
            pltpu.VMEM((COLS, SHARD, EARLY), BF16),
            pltpu.VMEM((POS, BLOCK), I32),
            pltpu.VMEM((64, LANES), I32),
            pltpu.VMEM((8, BLOCK), I32),
            pltpu.VMEM((8, BLOCK), F32),
            pltpu.VMEM((8, BLOCK), F32),
            pltpu.VMEM((8, BLOCK // 2), F32),
            pltpu.VMEM((COLS, 8, BLOCK // 2), F32),
            pltpu.VMEM((8, BLOCK), F32),
            pltpu.VMEM((COLS, 8, BLOCK), F32),
            pltpu.VMEM((ROWS, 8, LANES), F32),
            pltpu.VMEM((ROWS, 8, LANES), F32),
            pltpu.VMEM((LANES, LANES), F32),
            pltpu.VMEM((4 * POS, BLOCK, LANES), F32),
            dma((4,)),
            dma((2,)),
            dma((2,)),
            dma((24,)),
            dma((24,)),
        ]
        + [dma((16,))] * 20,
        compiler_params=pltpu.CompilerParams(
            collective_id=0, has_side_effects=True, vmem_limit_bytes=60 * 1024 * 1024
        ),
        cost_estimate=pl.CostEstimate(flops=1 << 31, bytes_accessed=1 << 22, transcendentals=1 << 21),
        name="smooth_ap",
    )(embed, positives.T, placement.reshape(64, LANES))


def solution(mesh):
    return jax.shard_map(
        body,
        mesh=mesh,
        in_specs=(P(("row", "col"), None), P("row", None), P()),
        out_specs=P(("row", "col"), None),
        check_vma=False,
    )
```

```python
import functools

import jax
import jax.numpy as jnp
from jax import lax
from jax.experimental import pallas as pl
from jax.experimental.pallas import tpu as pltpu
from jax.sharding import PartitionSpec as P

MESH = pl.DeviceIdType.MESH
TAU = 0.02
HALF = 0.5 / TAU
F32, BF16, I32 = jnp.float32, jnp.bfloat16, jnp.int32

ROWS, COLS, ZS = 16, 16, 8
SHARD, WIDTH, POS = 32, 1024, 4
BLOCK = SHARD * COLS
LANES = 128
STEP = 64

BROAD, NARROW, EARLY = 384, 256, 384
LINE_AT, BOTH_AT = BROAD, BROAD + NARROW

DEPTHS = (4, 3, 5, 2, 6, 1, 7)
PLANE = (10, 11, 14, 9, 6, 8, 2, 15, 13, 7, 5, 12, 4, 3, 1)
LINE = (8, 9, 10, 11, 6, 7, 14, 15, 12, 13, 4, 5, 2, 3, 1)


def remote(src, dst, send, recv, device):
    return pltpu.make_async_remote_copy(
        src_ref=src, dst_ref=dst, send_sem=send, recv_sem=recv,
        device_id=device, device_id_type=MESH,
    )


def kernel(
    embed, positives, placement, out,
    a_buf, c_buf, s_ref, vi, vj, gi, gj, part, landed, mine, z_part, z_landed, z_whole, z_other,
    ez_part, ez_landed, e_whole, e_other, ep_part, ep_landed,
    pos_in, place_in, tgt, pt, we, x1s, x1r, x2s, x2r, jp, jw, jt, jc,
    in_sem, z_sem, e_sem, plane_s, plane_r, z_s, z_r, sib_s, sib_r,
    x1_ss, x1_rs, x2_ss, x2_rs, p_ss, p_rs, w_ss, w_rs, g_ss, g_rs, h_ss, h_rs,
    e_ss, e_rs, f_ss, f_rs,
):
    r, c = lax.axis_index("row"), lax.axis_index("col")
    z, core = r // 2, r % 2
    y, x = c // 4, c % 4

    def in_plane(o):
        return (r, ((y + o[0]) % 4) * 4 + (x + o[1]) % 4)

    def in_line(d, k=0):
        return (((z + d) % ZS) * 2 + (core + k) % 2, c)

    loads = [
        pltpu.make_async_copy(embed, a_buf.at[c], in_sem.at[0]),
        pltpu.make_async_copy(embed, c_buf.at[r], in_sem.at[1]),
        pltpu.make_async_copy(positives, pos_in, in_sem.at[2]),
        pltpu.make_async_copy(placement, place_in, in_sem.at[3]),
    ]
    for load in loads:
        load.start()
    barrier = pltpu.get_barrier_semaphore()

    near = [in_line(2), in_line(6), in_plane((0, 2)), in_plane((2, 0)), in_line(1), in_line(7)]
    near += [in_plane((0, 1)), in_plane((1, 0)), in_plane((0, 3)), in_plane((3, 0)), in_line(0, 1)]
    for peer in near:
        pl.semaphore_signal(barrier, inc=1, device_id=peer, device_id_type=MESH)
    for load in loads:
        load.wait()
    pl.semaphore_wait(barrier, len(near))

    sent = []

    def go(src, dst, ss, rs, device):
        copy = remote(src, dst, ss, rs, device)
        copy.start()
        sent.append(copy)

    def z_send(d, block, rows, step, slot):
        view = c_buf.at[block, rows]
        go(view, view, z_s.at[slot], z_r.at[slot], in_line(step % ZS))

    def z_wait(d, rows, slot):
        view = c_buf.at[from_z(d), rows]
        remote(view, view, z_s.at[slot], z_r.at[slot], in_line(d % ZS)).wait_recv()

    def from_z(d, k=0):
        return ((z + ZS - d) % ZS) * 2 + (core + k) % 2

    def from_plane(dy, dx):
        return ((y + 4 - dy) % 4) * 4 + (x + 4 - dx) % 4

    def a_send(block, rows, dy, dx, slot):
        view = a_buf.at[block, rows]
        go(view, view, plane_s.at[slot], plane_r.at[slot], in_plane((dy, dx)))

    def a_wait(dy, dx, rows, slot):
        view = a_buf.at[from_plane(dy, dx), rows]
        remote(view, view, plane_s.at[slot], plane_r.at[slot], in_plane((dy, dx))).wait_recv()

    def sib_send(d, rows, slot):
        view = c_buf.at[from_z(d), rows]
        go(view, view, sib_s.at[slot], sib_r.at[slot], in_line(0, 1))

    def sib_wait(d, rows, slot):
        view = c_buf.at[from_z(d, 1), rows]
        remote(view, view, sib_s.at[slot], sib_r.at[slot], in_line(0, 1)).wait_recv()

    every, top, low_half = pl.ds(0, SHARD), pl.ds(0, SHARD // 2), pl.ds(SHARD // 2, SHARD // 2)
    z_send(2, r, every, 2, 2)
    z_send(-2, r, every, -2, 6)
    a_send(c, every, 0, 2, 1)
    a_send(c, every, 2, 0, 4)
    z_send(1, r, every, 1, 1)
    z_send(-1, r, every, -1, 7)
    for d in (1, 3):
        a_send(c, every, 0, d, d - 1)
        a_send(c, every, d, 0, d + 2)
    sib_send(0, every, 0)

    table = place_in[...]
    high = (table // 64).astype(F32).astype(BF16)
    low = (table % 64).astype(F32).astype(BF16)
    lane_id = lax.broadcasted_iota(I32, (LANES, BLOCK), 0)
    row_id = lax.broadcasted_iota(I32, (64, BLOCK), 0)
    for m in range(POS):
        entity = pos_in[m : m + 1, :]
        hot = jnp.where(lane_id == entity % LANES, 1.0, 0.0).astype(BF16)
        value = jnp.dot(high, hot, preferred_element_type=F32) * 64.0 + jnp.dot(
            low, hot, preferred_element_type=F32
        )
        found = jnp.sum(jnp.where(row_id == entity // LANES, value, 0.0), axis=0, keepdims=True)
        pt[POS + m : POS + m + 1, :] = found
        where = found.astype(I32)
        here = (where // SHARD) % COLS == c
        tgt[m : m + 1, :] = jnp.where(here, (where // BLOCK) * SHARD + where % SHARD, -1)

    def turn(d):
        a_wait(0, d, every, d - 1)
        for e in (2, 1, 3):
            a_send(from_plane(0, d), top, e, 0, 6 + 3 * (d - 1) + e - 1)
        a_wait(d, 0, every, d + 2)
        for e in (2, 1, 3):
            a_send(from_plane(d, 0), low_half, 0, e, 15 + 3 * (d - 1) + e - 1)

    turn(1)
    turn(3)
    z_wait(2, every, 2)
    z_send(4, from_z(2), top, 2, 4)
    z_send(3, from_z(2), every, 1, 3)
    z_wait(-2, every, 6)
    z_send(-4, from_z(-2), low_half, -2, 8)
    z_send(-3, from_z(-2), every, -1, 5)
    turn(2)
    for d, slot in ((2, 2), (-2, 6)):
        sib_send(d, every, slot)
    for d, slot in ((1, 1), (-1, 7)):
        z_wait(d, every, slot)
        sib_send(d, every, slot)
    for d, slot in ((3, 3), (-3, 5)):
        z_wait(d, every, slot)
        sib_send(d, every, slot)
    z_wait(4, top, 4)
    sib_send(4, top, 4)
    z_wait(-4, low_half, 8)
    sib_send(-4, low_half, 8)
    for d in (1, 3, 2):
        for e in (1, 3, 2):
            a_wait(e, d, top, 6 + 3 * (d - 1) + e - 1)
            a_wait(d, e, low_half, 15 + 3 * (d - 1) + e - 1)
    for d, slot in ((0, 0), (1, 1), (-1, 7), (2, 2), (-2, 6), (3, 3), (-3, 5)):
        sib_wait(d, every, slot)
    sib_wait(4, top, 4)
    sib_wait(-4, low_half, 8)

    anchors = a_buf[...].reshape(BLOCK, WIDTH)
    for h in range(2):
        cand = c_buf[8 * h : 8 * h + 8].reshape(BLOCK // 2, WIDTH)
        s_ref[256 * h : 256 * h + 256, :] = HALF * lax.dot_general(
            cand, anchors, (((1,), (1,)), ((), ())), preferred_element_type=F32
        )
    tile = s_ref[pl.ds(pl.multiple_of(r * SHARD, SHARD), SHARD), pl.ds(pl.multiple_of(y * LANES, LANES), LANES)]
    me_row = lax.broadcasted_iota(I32, (SHARD, LANES), 0)
    me_lane = lax.broadcasted_iota(I32, (SHARD, LANES), 1)
    s_ref[pl.ds(pl.multiple_of(r * SHARD, SHARD), SHARD), pl.ds(pl.multiple_of(y * LANES, LANES), LANES)] = (
        jnp.where(me_lane - x * SHARD == me_row, -1e30, tile)
    )

    iota_k = lax.broadcasted_iota(I32, (STEP, LANES), 0)
    iota_a = lax.broadcasted_iota(I32, (STEP, LANES), 1)
    steps = BLOCK // STEP

    def fold(value):
        return jnp.sum(value.reshape(STEP // 8, 8, LANES), axis=0)

    def cut(q):
        return slice(q * LANES, (q + 1) * LANES)

    for q in range(4):
        rows = [tgt[m : m + 1, cut(q)] for m in range(POS)]

        def pick(i, acc, q=q, rows=rows):
            k0 = pl.multiple_of(i * STEP, STEP)
            score = s_ref[pl.ds(k0, STEP), cut(q)]
            return tuple(
                acc[m] + fold(jnp.where(iota_k == rows[m] - k0, score, 0.0)) for m in range(POS)
            )

        acc = lax.fori_loop(0, steps, pick, (jnp.zeros((8, LANES), F32),) * POS)
        for m in range(POS):
            half, lane = q // 2, (q % 2) * LANES
            x1s[half * POS + m : half * POS + m + 1, lane : lane + LANES] = jnp.sum(
                acc[m], axis=0, keepdims=True
            )

    def exchange(src, dst, ss, rs, peer, order):
        for o in order:
            remote(src, dst, ss.at[o], rs.at[o], peer(o)).start()

    def arrive(src, dst, ss, rs, peer, index):
        def wait(o, carry):
            remote(src, dst.at[index ^ o], ss.at[o], rs.at[o], peer(o)).wait_recv()
            return carry

        lax.fori_loop(1, 16, wait, 0)

    def leave(src, dst, ss, rs, peer):
        def wait(o, carry):
            remote(src, dst, ss.at[o], rs.at[o], peer(o)).wait_send()
            return carry

        lax.fori_loop(1, 16, wait, 0)

    def peer_c(o):
        return (r, c ^ o)

    def peer_r(o):
        return (r ^ o, c)

    exchange(x1s, x1r.at[c], x1_ss, x1_rs, peer_c, PLANE)
    x1r[c] = x1s[...]
    arrive(x1s, x1r, x1_ss, x1_rs, peer_c, c)
    total = jnp.sum(x1r[...], axis=0)
    pt[0:POS, 0:256] = total[0:POS]
    pt[0:POS, 256:512] = total[POS : 2 * POS]

    group = pl.ds(pl.multiple_of(y * LANES, LANES), LANES)
    def line_meet(tiles, columns, whole, other, sem):
        for h in range(2):
            rows = slice(256 * h, 256 * h + 256)
            product = sum(jnp.dot(g[rows, :], columns, preferred_element_type=F32) for g in tiles)
            whole[4 * h : 4 * h + 4] = product.reshape(4, 2, SHARD, product.shape[1])
        remote(whole.at[:, 1 - core], other, sem.at[0], sem.at[1], (r ^ 1, c)).start()

    def line_go(whole, other, part_ref, landed_ref, sem, ss, rs):
        meet = remote(whole.at[:, 1 - core], other, sem.at[0], sem.at[1], (r ^ 1, c))
        meet.wait_recv()
        part_ref[...] = (whole[:, core] + other[...]).astype(BF16)
        for d in DEPTHS:
            to = (z + d) % ZS
            remote(part_ref.at[to], landed_ref.at[z], ss.at[d], rs.at[d], in_line(d)).start()
        meet.wait_send()
        return whole[z, core] + other[z]

    def line_sum(landed_ref, ss, rs, first, width):
        for d in reversed(DEPTHS):
            frm = (z + ZS - d) % ZS
            remote(landed_ref.at[frm], landed_ref.at[frm], ss.at[d], rs.at[d], in_line(d)).wait_recv()
            out[:, first : first + width] += landed_ref[frm].astype(F32)

    def line_sent(part_ref, landed_ref, ss, rs):
        for d in DEPTHS:
            to = (z + d) % ZS
            remote(part_ref.at[to], landed_ref.at[z], ss.at[d], rs.at[d], in_line(d)).wait_send()

    for q in range(4):
        rows = [pt[m : m + 1, cut(q)] for m in range(POS)]

        def count(i, acc, q=q, rows=rows):
            k0 = pl.multiple_of(i * STEP, STEP)
            score = s_ref[pl.ds(k0, STEP), cut(q)]
            new = []
            for m in range(POS):
                t = jnp.tanh(score - rows[m])
                u = 1.0 + t
                v = 1.0 - t * t
                vi[m, pl.ds(k0, STEP), cut(q)] = v
                new.append(acc[2 * m] + fold(u))
                new.append(acc[2 * m + 1] + fold(v))
            return tuple(new)

        acc = lax.fori_loop(0, steps, count, (jnp.zeros((8, LANES), F32),) * (2 * POS))
        for m in range(POS):
            x2s[m : m + 1, cut(q)] = jnp.sum(acc[2 * m], axis=0, keepdims=True)
            x2s[POS + m : POS + m + 1, cut(q)] = jnp.sum(acc[2 * m + 1], axis=0, keepdims=True)
    exchange(x2s, x2r.at[c], x2_ss, x2_rs, peer_c, PLANE)
    x2r[c] = x2s[...]
    exchange(pt.at[:, group], jp.at[r], p_ss, p_rs, peer_r, LINE)
    jp[r] = pt[:, group]

    def columns(src, first):
        jt[...] = jnp.transpose(src[...].reshape(ROWS * 8, LANES))
        mine_cols = jt[pl.ds(pl.multiple_of(x * SHARD, SHARD), SHARD), :]
        for b in range(ROWS):
            for n in range(8):
                jc[first + n, b * SHARD : (b + 1) * SHARD, :] = jnp.broadcast_to(
                    mine_cols[:, b * 8 + n : b * 8 + n + 1], (SHARD, LANES)
                )

    arrive(x2s, x2r, x2_ss, x2_rs, peer_c, c)
    total = jnp.sum(x2r[...], axis=0)
    factor = 1.0 / (POS * SHARD * ROWS * COLS)
    p = [pt[m : m + 1, :] for m in range(POS)]
    rank = [0.5 + 0.5 * total[m : m + 1] for m in range(POS)]
    slope = [0.25 * total[POS + m : POS + m + 1] for m in range(POS)]
    prank = [jnp.full((1, BLOCK), 1.0, F32) for _ in range(POS)]
    grad = [-factor / rank[m] for m in range(POS)]
    pulled = [jnp.zeros((1, BLOCK), F32) for _ in range(POS)]
    for m in range(POS):
        for n in range(m + 1, POS):
            t = jnp.tanh(p[n] - p[m])
            prank[m] = prank[m] + 0.5 * (1.0 + t)
            prank[n] = prank[n] + 0.5 * (1.0 - t)
            pair = (0.25 / TAU) * (1.0 - t) * (1.0 + t) * (grad[n] - grad[m])
            pulled[m] = pulled[m] + pair
            pulled[n] = pulled[n] - pair
    for m in range(POS):
        weight = prank[m] / (rank[m] * rank[m]) * factor / TAU
        we[m : m + 1, :] = 0.25 * weight
        we[POS + m : POS + m + 1, :] = pulled[m] - weight * slope[m]

    exchange(we.at[:, group], jw.at[r], w_ss, w_rs, peer_r, LINE)
    jw[r] = we[:, group]

    for q in range(4):
        rows = [tgt[m : m + 1, cut(q)] for m in range(POS)]
        weights = [we[m : m + 1, cut(q)] for m in range(POS)]
        extras = [we[POS + m : POS + m + 1, cut(q)] for m in range(POS)]

        def tile_i(i, carry, q=q, rows=rows, weights=weights, extras=extras):
            k0 = pl.multiple_of(i * STEP, STEP)
            dense = weights[0] * vi[0, pl.ds(k0, STEP), cut(q)]
            for m in range(1, POS):
                dense = dense + weights[m] * vi[m, pl.ds(k0, STEP), cut(q)]
            for m in range(POS):
                dense = dense + jnp.where(iota_k == rows[m] - k0, extras[m], 0.0)
            gi[pl.ds(k0, STEP), cut(q)] = dense.astype(BF16)
            return carry

        lax.fori_loop(0, steps, tile_i, 0)

    over_rows = (((0,), (0,)), ((), ()))
    line_meet((gi,), a_buf[:, :, BOTH_AT:].reshape(BLOCK, EARLY), e_whole, e_other, e_sem)
    early_plane = c_buf[:, :, BOTH_AT:].reshape(BLOCK, EARLY)
    for h in range(2):
        rows = slice(256 * h, 256 * h + 256)
        product = lax.dot_general(gi[:, rows], early_plane, over_rows, preferred_element_type=F32)
        ep_part[8 * h : 8 * h + 8] = product.astype(BF16).reshape(8, SHARD, EARLY)

        @pl.when(c // 8 == h)
        def _(product=product):
            mine[...] = product.reshape(8, SHARD, EARLY)

    for o in PLANE:
        remote(ep_part.at[c ^ o], ep_landed.at[c], f_ss.at[o], f_rs.at[o], (r, c ^ o)).start()
    out[:, BOTH_AT:] = mine[c % 8]
    out[:, BOTH_AT:] += line_go(e_whole, e_other, ez_part, ez_landed, e_sem, e_ss, e_rs)

    arrive(pt.at[:, group], jp, p_ss, p_rs, peer_r, r)
    columns(jp, 0)

    def slopes(i, carry):
        k0 = pl.multiple_of(i * STEP, STEP)
        for m in range(POS):
            col = jc[m, pl.ds(k0, STEP), :]
            for q in range(4):
                t = jnp.tanh(s_ref[pl.ds(k0, STEP), cut(q)] - col)
                vj[m, pl.ds(k0, STEP), cut(q)] = 1.0 - t * t
            where = jc[POS + m, pl.ds(k0, STEP), :].astype(I32)
            jc[POS + m, pl.ds(k0, STEP), :] = jnp.where(
                where // BLOCK == r, where % BLOCK, -1
            ).astype(F32)
        return carry

    lax.fori_loop(0, steps, slopes, 0)

    arrive(we.at[:, group], jw, w_ss, w_rs, peer_r, r)
    columns(jw, 2 * POS)

    def tile_j(i, carry):
        k0 = pl.multiple_of(i * STEP, STEP)
        for q in range(4):
            dense = jc[2 * POS, pl.ds(k0, STEP), :] * vj[0, pl.ds(k0, STEP), cut(q)]
            for m in range(1, POS):
                dense = dense + jc[2 * POS + m, pl.ds(k0, STEP), :] * vj[m, pl.ds(k0, STEP), cut(q)]
            lane = (iota_a + q * LANES).astype(F32)
            for m in range(POS):
                dense = dense + jnp.where(
                    jc[POS + m, pl.ds(k0, STEP), :] == lane,
                    jc[3 * POS + m, pl.ds(k0, STEP), :],
                    0.0,
                )
            gj[pl.ds(k0, STEP), cut(q)] = dense.astype(BF16)
        return carry

    lax.fori_loop(0, steps, tile_j, 0)

    line_meet((gi, gj), a_buf[:, :, LINE_AT:BOTH_AT].reshape(BLOCK, NARROW), z_whole, z_other, z_sem)

    left = c_buf[:, :, :BROAD].reshape(BLOCK, BROAD)
    wide = 2 * LANES
    for turn_id in range(2):
        h = (c // 8) ^ (1 - turn_id)
        half = pl.ds(pl.multiple_of(h * wide, wide), wide)
        product = lax.dot_general(gi[:, half], left, over_rows, preferred_element_type=F32)
        product = product + lax.dot_general(gj[:, half], left, over_rows, preferred_element_type=F32)
        part[pl.ds(h * 8, 8)] = product.astype(BF16).reshape(8, SHARD, BROAD)
        if turn_id == 1:
            mine[...] = product.reshape(8, SHARD, BROAD)

        for o in PLANE:
            if (o < 8) == (turn_id == 1):
                remote(part.at[c ^ o], landed.at[c], g_ss.at[o], g_rs.at[o], (r, c ^ o)).start()

    out[:, :BROAD] = mine[c % 8]
    out[:, LINE_AT:BOTH_AT] = line_go(z_whole, z_other, z_part, z_landed, z_sem, h_ss, h_rs)

    def plane_sum(part_ref, landed_ref, ss, rs, first, width):
        def add(o, carry):
            frm = c ^ o
            remote(part_ref.at[frm], landed_ref.at[frm], ss.at[o], rs.at[o], (r, frm)).wait_recv()
            out[:, first : first + width] += landed_ref[frm].astype(F32)
            return carry

        lax.fori_loop(1, 16, add, 0)

    def plane_sent(part_ref, landed_ref, ss, rs):
        def wait(o, carry):
            frm = c ^ o
            remote(part_ref.at[frm], landed_ref.at[frm], ss.at[o], rs.at[o], (r, frm)).wait_send()
            return carry

        lax.fori_loop(1, 16, wait, 0)

    line_sum(ez_landed, e_ss, e_rs, BOTH_AT, EARLY)
    plane_sum(ep_part, ep_landed, f_ss, f_rs, BOTH_AT, EARLY)
    line_sent(ez_part, ez_landed, e_ss, e_rs)
    plane_sent(ep_part, ep_landed, f_ss, f_rs)
    leave(x1s, x1r.at[c], x1_ss, x1_rs, peer_c)
    leave(x2s, x2r.at[c], x2_ss, x2_rs, peer_c)
    leave(pt.at[:, group], jp.at[r], p_ss, p_rs, peer_r)
    leave(we.at[:, group], jw.at[r], w_ss, w_rs, peer_r)
    for copy in sent:
        copy.wait_send()
    line_sum(z_landed, h_ss, h_rs, LINE_AT, NARROW)
    plane_sum(part, landed, g_ss, g_rs, 0, BROAD)
    line_sent(z_part, z_landed, h_ss, h_rs)
    plane_sent(part, landed, g_ss, g_rs)


def body(embed, positives, placement):
    dma = pltpu.SemaphoreType.DMA
    return pl.pallas_call(
        kernel,
        out_shape=jax.ShapeDtypeStruct((SHARD, WIDTH), F32),
        in_specs=[pl.BlockSpec(memory_space=pl.ANY)] * 3,
        out_specs=pl.BlockSpec(memory_space=pltpu.VMEM),
        scratch_shapes=[
            pltpu.VMEM((COLS, SHARD, WIDTH), BF16),
            pltpu.VMEM((ROWS, SHARD, WIDTH), BF16),
            pltpu.VMEM((BLOCK, BLOCK), F32),
            pltpu.VMEM((POS, BLOCK, BLOCK), F32),
            pltpu.VMEM((POS, BLOCK, BLOCK), F32),
            pltpu.VMEM((BLOCK, BLOCK), BF16),
            pltpu.VMEM((BLOCK, BLOCK), BF16),
            pltpu.VMEM((COLS, SHARD, BROAD), BF16),
            pltpu.VMEM((COLS, SHARD, BROAD), BF16),
            pltpu.VMEM((8, SHARD, BROAD), F32),
            pltpu.VMEM((ZS, SHARD, NARROW), BF16),
            pltpu.VMEM((ZS, SHARD, NARROW), BF16),
            pltpu.VMEM((ZS, 2, SHARD, NARROW), F32),
            pltpu.VMEM((ZS, SHARD, NARROW), F32),
            pltpu.VMEM((ZS, SHARD, EARLY), BF16),
            pltpu.VMEM((ZS, SHARD, EARLY), BF16),
            pltpu.VMEM((ZS, 2, SHARD, EARLY), F32),
            pltpu.VMEM((ZS, SHARD, EARLY), F32),
            pltpu.VMEM((COLS, SHARD, EARLY), BF16),
            pltpu.VMEM((COLS, SHARD, EARLY), BF16),
            pltpu.VMEM((POS, BLOCK), I32),
            pltpu.VMEM((64, LANES), I32),
            pltpu.VMEM((8, BLOCK), I32),
            pltpu.VMEM((8, BLOCK), F32),
            pltpu.VMEM((8, BLOCK), F32),
            pltpu.VMEM((8, BLOCK // 2), F32),
            pltpu.VMEM((COLS, 8, BLOCK // 2), F32),
            pltpu.VMEM((8, BLOCK), F32),
            pltpu.VMEM((COLS, 8, BLOCK), F32),
            pltpu.VMEM((ROWS, 8, LANES), F32),
            pltpu.VMEM((ROWS, 8, LANES), F32),
            pltpu.VMEM((LANES, LANES), F32),
            pltpu.VMEM((4 * POS, BLOCK, LANES), F32),
            dma((4,)),
            dma((2,)),
            dma((2,)),
            dma((24,)),
            dma((24,)),
        ]
        + [dma((16,))] * 20,
        compiler_params=pltpu.CompilerParams(
            collective_id=0, has_side_effects=True, vmem_limit_bytes=60 * 1024 * 1024
        ),
        cost_estimate=pl.CostEstimate(flops=1 << 31, bytes_accessed=1 << 22, transcendentals=1 << 21),
        name="smooth_ap",
    )(embed, positives.T, placement.reshape(64, LANES))


def solution(mesh):
    return jax.shard_map(
        body,
        mesh=mesh,
        in_specs=(P(("row", "col"), None), P("row", None), P()),
        out_specs=P(("row", "col"), None),
        check_vma=False,
    )
```

```python
import functools

import jax
import jax.numpy as jnp
from jax import lax
from jax.experimental import pallas as pl
from jax.experimental.pallas import tpu as pltpu
from jax.sharding import PartitionSpec as P

MESH = pl.DeviceIdType.MESH
TAU = 0.02
HALF = 0.5 / TAU
F32, BF16, I32 = jnp.float32, jnp.bfloat16, jnp.int32

ROWS, COLS, ZS = 16, 16, 8
SHARD, WIDTH, POS = 32, 1024, 4
BLOCK = SHARD * COLS
LANES = 128
STEP = 64

BROAD, NARROW, EARLY = 256, 256, 512
LINE_AT, BOTH_AT = BROAD, BROAD + NARROW

DEPTHS = (4, 3, 5, 2, 6, 1, 7)
PLANE = (10, 11, 14, 9, 6, 8, 2, 15, 13, 7, 5, 12, 4, 3, 1)
LINE = (8, 9, 10, 11, 6, 7, 14, 15, 12, 13, 4, 5, 2, 3, 1)


def remote(src, dst, send, recv, device):
    return pltpu.make_async_remote_copy(
        src_ref=src, dst_ref=dst, send_sem=send, recv_sem=recv,
        device_id=device, device_id_type=MESH,
    )


def kernel(
    embed, positives, placement, out,
    a_buf, c_buf, s_ref, vi, vj, gi, gj, part, landed, mine, z_part, z_landed, z_whole, z_other,
    ez_part, ez_landed, e_whole, e_other, ep_part, ep_landed, e_mine,
    pos_in, place_in, tgt, pt, we, x1s, x1r, x2s, x2r, jp, jw, jt, jc,
    in_sem, z_sem, e_sem, plane_s, plane_r, z_s, z_r, sib_s, sib_r,
    x1_ss, x1_rs, x2_ss, x2_rs, p_ss, p_rs, w_ss, w_rs, g_ss, g_rs, h_ss, h_rs,
    e_ss, e_rs, f_ss, f_rs,
):
    r, c = lax.axis_index("row"), lax.axis_index("col")
    z, core = r // 2, r % 2
    y, x = c // 4, c % 4

    def in_plane(o):
        return (r, ((y + o[0]) % 4) * 4 + (x + o[1]) % 4)

    def in_line(d, k=0):
        return (((z + d) % ZS) * 2 + (core + k) % 2, c)

    loads = [
        pltpu.make_async_copy(embed, a_buf.at[c], in_sem.at[0]),
        pltpu.make_async_copy(embed, c_buf.at[r], in_sem.at[1]),
        pltpu.make_async_copy(positives, pos_in, in_sem.at[2]),
        pltpu.make_async_copy(placement, place_in, in_sem.at[3]),
    ]
    for load in loads:
        load.start()
    barrier = pltpu.get_barrier_semaphore()

    near = [in_line(2), in_line(6), in_plane((0, 2)), in_plane((2, 0)), in_line(1), in_line(7)]
    near += [in_plane((0, 1)), in_plane((1, 0)), in_plane((0, 3)), in_plane((3, 0)), in_line(0, 1)]
    for peer in near:
        pl.semaphore_signal(barrier, inc=1, device_id=peer, device_id_type=MESH)
    for load in loads:
        load.wait()
    pl.semaphore_wait(barrier, len(near))

    sent = []

    def go(src, dst, ss, rs, device):
        copy = remote(src, dst, ss, rs, device)
        copy.start()
        sent.append(copy)

    def z_send(d, block, rows, step, slot):
        view = c_buf.at[block, rows]
        go(view, view, z_s.at[slot], z_r.at[slot], in_line(step % ZS))

    def z_wait(d, rows, slot):
        view = c_buf.at[from_z(d), rows]
        remote(view, view, z_s.at[slot], z_r.at[slot], in_line(d % ZS)).wait_recv()

    def from_z(d, k=0):
        return ((z + ZS - d) % ZS) * 2 + (core + k) % 2

    def from_plane(dy, dx):
        return ((y + 4 - dy) % 4) * 4 + (x + 4 - dx) % 4

    def a_send(block, rows, dy, dx, slot):
        view = a_buf.at[block, rows]
        go(view, view, plane_s.at[slot], plane_r.at[slot], in_plane((dy, dx)))

    def a_wait(dy, dx, rows, slot):
        view = a_buf.at[from_plane(dy, dx), rows]
        remote(view, view, plane_s.at[slot], plane_r.at[slot], in_plane((dy, dx))).wait_recv()

    def sib_send(d, rows, slot):
        view = c_buf.at[from_z(d), rows]
        go(view, view, sib_s.at[slot], sib_r.at[slot], in_line(0, 1))

    def sib_wait(d, rows, slot):
        view = c_buf.at[from_z(d, 1), rows]
        remote(view, view, sib_s.at[slot], sib_r.at[slot], in_line(0, 1)).wait_recv()

    every, top, low_half = pl.ds(0, SHARD), pl.ds(0, SHARD // 2), pl.ds(SHARD // 2, SHARD // 2)
    halves = (top, low_half)

    def x_first(d, h):
        a_send(c, halves[h], 0, d, 4 * d - 4 + h)

    def y_first(d, h):
        a_send(c, halves[h], d, 0, 4 * d - 2 + h)

    for d in (2, 1, 3):
        x_first(d, 0)
        y_first(d, 1)
    z_send(2, r, top, 2, 0)
    z_send(-2, r, low_half, -2, 1)
    z_send(2, r, low_half, 2, 2)
    z_send(-2, r, top, -2, 3)
    z_send(1, r, every, 1, 4)
    z_send(-1, r, every, -1, 5)
    for d in (2, 1, 3):
        x_first(d, 1)
        y_first(d, 0)
    sib_send(0, every, 0)

    table = place_in[...]
    high = (table // 64).astype(F32).astype(BF16)
    low = (table % 64).astype(F32).astype(BF16)
    lane_id = lax.broadcasted_iota(I32, (LANES, BLOCK), 0)
    row_id = lax.broadcasted_iota(I32, (64, BLOCK), 0)
    for m in range(POS):
        entity = pos_in[m : m + 1, :]
        hot = jnp.where(lane_id == entity % LANES, 1.0, 0.0).astype(BF16)
        value = jnp.dot(high, hot, preferred_element_type=F32) * 64.0 + jnp.dot(
            low, hot, preferred_element_type=F32
        )
        found = jnp.sum(jnp.where(row_id == entity // LANES, value, 0.0), axis=0, keepdims=True)
        pt[POS + m : POS + m + 1, :] = found
        where = found.astype(I32)
        here = (where // SHARD) % COLS == c
        tgt[m : m + 1, :] = jnp.where(here, (where // BLOCK) * SHARD + where % SHARD, -1)

    def turn(d):
        a_wait(0, d, top, 4 * d - 4)
        for e in (2, 1, 3):
            a_send(from_plane(0, d), top, e, 0, 12 + 3 * (d - 1) + e - 1)
        a_wait(d, 0, low_half, 4 * d - 1)
        for e in (2, 1, 3):
            a_send(from_plane(d, 0), low_half, 0, e, 21 + 3 * (d - 1) + e - 1)

    turn(1)
    turn(3)
    z_wait(2, top, 0)
    z_send(4, from_z(2), top, 2, 6)
    z_send(3, from_z(2), top, 1, 7)
    z_wait(-2, low_half, 1)
    z_send(-4, from_z(-2), low_half, -2, 8)
    z_send(-3, from_z(-2), low_half, -1, 9)
    z_wait(2, low_half, 2)
    z_send(3, from_z(2), low_half, 1, 10)
    z_wait(-2, top, 3)
    z_send(-3, from_z(-2), top, -1, 11)
    turn(2)
    for d, slot in ((2, 2), (-2, 6)):
        sib_send(d, every, slot)
    for d, slot in ((1, 4), (-1, 5)):
        z_wait(d, every, slot)
        sib_send(d, every, 1 if d == 1 else 7)
    z_wait(4, top, 6)
    sib_send(4, top, 4)
    z_wait(-4, low_half, 8)
    sib_send(-4, low_half, 8)
    z_wait(3, top, 7)
    z_wait(3, low_half, 10)
    sib_send(3, every, 3)
    z_wait(-3, low_half, 9)
    z_wait(-3, top, 11)
    sib_send(-3, every, 5)
    for d in (1, 3, 2):
        a_wait(0, d, low_half, 4 * d - 3)
        a_wait(d, 0, top, 4 * d - 2)
    for d in (1, 3, 2):
        for e in (1, 3, 2):
            a_wait(e, d, top, 12 + 3 * (d - 1) + e - 1)
            a_wait(d, e, low_half, 21 + 3 * (d - 1) + e - 1)
    for d, slot in ((0, 0), (1, 1), (-1, 7), (2, 2), (-2, 6), (3, 3), (-3, 5)):
        sib_wait(d, every, slot)
    sib_wait(4, top, 4)
    sib_wait(-4, low_half, 8)

    anchors = a_buf[...].reshape(BLOCK, WIDTH)
    for h in range(2):
        cand = c_buf[8 * h : 8 * h + 8].reshape(BLOCK // 2, WIDTH)
        s_ref[256 * h : 256 * h + 256, :] = HALF * lax.dot_general(
            cand, anchors, (((1,), (1,)), ((), ())), preferred_element_type=F32
        )
    tile = s_ref[pl.ds(pl.multiple_of(r * SHARD, SHARD), SHARD), pl.ds(pl.multiple_of(y * LANES, LANES), LANES)]
    me_row = lax.broadcasted_iota(I32, (SHARD, LANES), 0)
    me_lane = lax.broadcasted_iota(I32, (SHARD, LANES), 1)
    s_ref[pl.ds(pl.multiple_of(r * SHARD, SHARD), SHARD), pl.ds(pl.multiple_of(y * LANES, LANES), LANES)] = (
        jnp.where(me_lane - x * SHARD == me_row, -1e30, tile)
    )

    iota_k = lax.broadcasted_iota(I32, (STEP, LANES), 0)
    iota_a = lax.broadcasted_iota(I32, (STEP, LANES), 1)
    steps = BLOCK // STEP

    def fold(value):
        return jnp.sum(value.reshape(STEP // 8, 8, LANES), axis=0)

    def cut(q):
        return slice(q * LANES, (q + 1) * LANES)

    for q in range(4):
        rows = [tgt[m : m + 1, cut(q)] for m in range(POS)]

        def pick(i, acc, q=q, rows=rows):
            k0 = pl.multiple_of(i * STEP, STEP)
            score = s_ref[pl.ds(k0, STEP), cut(q)]
            return tuple(
                acc[m] + fold(jnp.where(iota_k == rows[m] - k0, score, 0.0)) for m in range(POS)
            )

        acc = lax.fori_loop(0, steps, pick, (jnp.zeros((8, LANES), F32),) * POS)
        for m in range(POS):
            half, lane = q // 2, (q % 2) * LANES
            x1s[half * POS + m : half * POS + m + 1, lane : lane + LANES] = jnp.sum(
                acc[m], axis=0, keepdims=True
            )

    def exchange(src, dst, ss, rs, peer, order):
        for o in order:
            remote(src, dst, ss.at[o], rs.at[o], peer(o)).start()

    def arrive(src, dst, ss, rs, peer, index):
        def wait(o, carry):
            remote(src, dst.at[index ^ o], ss.at[o], rs.at[o], peer(o)).wait_recv()
            return carry

        lax.fori_loop(1, 16, wait, 0)

    def leave(src, dst, ss, rs, peer):
        def wait(o, carry):
            remote(src, dst, ss.at[o], rs.at[o], peer(o)).wait_send()
            return carry

        lax.fori_loop(1, 16, wait, 0)

    def peer_c(o):
        return (r, c ^ o)

    def peer_r(o):
        return (r ^ o, c)

    exchange(x1s, x1r.at[c], x1_ss, x1_rs, peer_c, PLANE)
    x1r[c] = x1s[...]
    arrive(x1s, x1r, x1_ss, x1_rs, peer_c, c)
    total = jnp.sum(x1r[...], axis=0)
    pt[0:POS, 0:256] = total[0:POS]
    pt[0:POS, 256:512] = total[POS : 2 * POS]

    group = pl.ds(pl.multiple_of(y * LANES, LANES), LANES)
    def line_meet(tiles, columns, whole, other, sem):
        for h in range(2):
            rows = slice(256 * h, 256 * h + 256)
            product = sum(jnp.dot(g[rows, :], columns, preferred_element_type=F32) for g in tiles)
            whole[4 * h : 4 * h + 4] = product.reshape(4, 2, SHARD, product.shape[1])
        remote(whole.at[:, 1 - core], other, sem.at[0], sem.at[1], (r ^ 1, c)).start()

    def line_go(whole, other, part_ref, landed_ref, sem, ss, rs):
        meet = remote(whole.at[:, 1 - core], other, sem.at[0], sem.at[1], (r ^ 1, c))
        meet.wait_recv()
        part_ref[...] = (whole[:, core] + other[...]).astype(BF16)
        for d in DEPTHS:
            to = (z + d) % ZS
            remote(part_ref.at[to], landed_ref.at[z], ss.at[d], rs.at[d], in_line(d)).start()
        meet.wait_send()
        return whole[z, core] + other[z]

    def line_sum(landed_ref, ss, rs, first, width):
        for d in reversed(DEPTHS):
            frm = (z + ZS - d) % ZS
            remote(landed_ref.at[frm], landed_ref.at[frm], ss.at[d], rs.at[d], in_line(d)).wait_recv()
            out[:, first : first + width] += landed_ref[frm].astype(F32)

    def line_sent(part_ref, landed_ref, ss, rs):
        for d in DEPTHS:
            to = (z + d) % ZS
            remote(part_ref.at[to], landed_ref.at[z], ss.at[d], rs.at[d], in_line(d)).wait_send()

    for q in range(4):
        rows = [pt[m : m + 1, cut(q)] for m in range(POS)]

        def count(i, acc, q=q, rows=rows):
            k0 = pl.multiple_of(i * STEP, STEP)
            score = s_ref[pl.ds(k0, STEP), cut(q)]
            new = []
            for m in range(POS):
                t = jnp.tanh(score - rows[m])
                u = 1.0 + t
                v = 1.0 - t * t
                vi[m, pl.ds(k0, STEP), cut(q)] = v
                new.append(acc[2 * m] + fold(u))
                new.append(acc[2 * m + 1] + fold(v))
            return tuple(new)

        acc = lax.fori_loop(0, steps, count, (jnp.zeros((8, LANES), F32),) * (2 * POS))
        for m in range(POS):
            x2s[m : m + 1, cut(q)] = jnp.sum(acc[2 * m], axis=0, keepdims=True)
            x2s[POS + m : POS + m + 1, cut(q)] = jnp.sum(acc[2 * m + 1], axis=0, keepdims=True)
    exchange(x2s, x2r.at[c], x2_ss, x2_rs, peer_c, PLANE)
    x2r[c] = x2s[...]
    exchange(pt.at[:, group], jp.at[r], p_ss, p_rs, peer_r, LINE)
    jp[r] = pt[:, group]

    def columns(src, first):
        jt[...] = jnp.transpose(src[...].reshape(ROWS * 8, LANES))
        mine_cols = jt[pl.ds(pl.multiple_of(x * SHARD, SHARD), SHARD), :]
        for b in range(ROWS):
            for n in range(8):
                jc[first + n, b * SHARD : (b + 1) * SHARD, :] = jnp.broadcast_to(
                    mine_cols[:, b * 8 + n : b * 8 + n + 1], (SHARD, LANES)
                )

    arrive(x2s, x2r, x2_ss, x2_rs, peer_c, c)
    total = jnp.sum(x2r[...], axis=0)
    factor = 1.0 / (POS * SHARD * ROWS * COLS)
    p = [pt[m : m + 1, :] for m in range(POS)]
    rank = [0.5 + 0.5 * total[m : m + 1] for m in range(POS)]
    slope = [0.25 * total[POS + m : POS + m + 1] for m in range(POS)]
    prank = [jnp.full((1, BLOCK), 1.0, F32) for _ in range(POS)]
    grad = [-factor / rank[m] for m in range(POS)]
    pulled = [jnp.zeros((1, BLOCK), F32) for _ in range(POS)]
    for m in range(POS):
        for n in range(m + 1, POS):
            t = jnp.tanh(p[n] - p[m])
            prank[m] = prank[m] + 0.5 * (1.0 + t)
            prank[n] = prank[n] + 0.5 * (1.0 - t)
            pair = (0.25 / TAU) * (1.0 - t) * (1.0 + t) * (grad[n] - grad[m])
            pulled[m] = pulled[m] + pair
            pulled[n] = pulled[n] - pair
    for m in range(POS):
        weight = prank[m] / (rank[m] * rank[m]) * factor / TAU
        we[m : m + 1, :] = 0.25 * weight
        we[POS + m : POS + m + 1, :] = pulled[m] - weight * slope[m]

    exchange(we.at[:, group], jw.at[r], w_ss, w_rs, peer_r, LINE)
    jw[r] = we[:, group]

    for q in range(4):
        rows = [tgt[m : m + 1, cut(q)] for m in range(POS)]
        weights = [we[m : m + 1, cut(q)] for m in range(POS)]
        extras = [we[POS + m : POS + m + 1, cut(q)] for m in range(POS)]

        def tile_i(i, carry, q=q, rows=rows, weights=weights, extras=extras):
            k0 = pl.multiple_of(i * STEP, STEP)
            dense = weights[0] * vi[0, pl.ds(k0, STEP), cut(q)]
            for m in range(1, POS):
                dense = dense + weights[m] * vi[m, pl.ds(k0, STEP), cut(q)]
            for m in range(POS):
                dense = dense + jnp.where(iota_k == rows[m] - k0, extras[m], 0.0)
            gi[pl.ds(k0, STEP), cut(q)] = dense.astype(BF16)
            return carry

        lax.fori_loop(0, steps, tile_i, 0)

    over_rows = (((0,), (0,)), ((), ()))
    line_meet((gi,), a_buf[:, :, BOTH_AT:].reshape(BLOCK, EARLY), e_whole, e_other, e_sem)
    early_plane = c_buf[:, :, BOTH_AT:].reshape(BLOCK, EARLY)
    for h in range(2):
        rows = slice(256 * h, 256 * h + 256)
        product = lax.dot_general(gi[:, rows], early_plane, over_rows, preferred_element_type=F32)
        ep_part[8 * h : 8 * h + 8] = product.astype(BF16).reshape(8, SHARD, EARLY)

        @pl.when(c // 8 == h)
        def _(product=product):
            e_mine[...] = product.reshape(8, SHARD, EARLY)

    for o in PLANE:
        remote(ep_part.at[c ^ o], ep_landed.at[c], f_ss.at[o], f_rs.at[o], (r, c ^ o)).start()
    out[:, BOTH_AT:] = e_mine[c % 8]

    arrive(pt.at[:, group], jp, p_ss, p_rs, peer_r, r)
    columns(jp, 0)
    out[:, BOTH_AT:] += line_go(e_whole, e_other, ez_part, ez_landed, e_sem, e_ss, e_rs)

    def slopes(i, carry):
        k0 = pl.multiple_of(i * STEP, STEP)
        for m in range(POS):
            col = jc[m, pl.ds(k0, STEP), :]
            for q in range(4):
                t = jnp.tanh(s_ref[pl.ds(k0, STEP), cut(q)] - col)
                vj[m, pl.ds(k0, STEP), cut(q)] = 1.0 - t * t
            where = jc[POS + m, pl.ds(k0, STEP), :].astype(I32)
            jc[POS + m, pl.ds(k0, STEP), :] = jnp.where(
                where // BLOCK == r, where % BLOCK, -1
            ).astype(F32)
        return carry

    lax.fori_loop(0, steps, slopes, 0)

    arrive(we.at[:, group], jw, w_ss, w_rs, peer_r, r)
    columns(jw, 2 * POS)

    def tile_j(i, carry):
        for part_id in range(2):
            k0 = pl.ds(pl.multiple_of(i * 32 + part_id * 16, 16), 16)
            weights = [jc[2 * POS + m, k0, :] for m in range(POS)]
            extras = [jc[3 * POS + m, k0, :] for m in range(POS)]
            at = [jc[POS + m, k0, :] for m in range(POS)]
            for q in range(4):
                dense = weights[0] * vj[0, k0, cut(q)]
                for m in range(1, POS):
                    dense = dense + weights[m] * vj[m, k0, cut(q)]
                lane = (iota_a[0:16, :] + q * LANES).astype(F32)
                for m in range(POS):
                    dense = dense + jnp.where(at[m] == lane, extras[m], 0.0)
                gj[k0, cut(q)] = dense.astype(BF16)
        return carry

    lax.fori_loop(0, BLOCK // 32, tile_j, 0)

    line_meet((gi, gj), a_buf[:, :, LINE_AT:BOTH_AT].reshape(BLOCK, NARROW), z_whole, z_other, z_sem)

    left = c_buf[:, :, :BROAD].reshape(BLOCK, BROAD)
    wide = 2 * LANES
    for turn_id in range(2):
        h = (c // 8) ^ (1 - turn_id)
        half = pl.ds(pl.multiple_of(h * wide, wide), wide)
        product = lax.dot_general(gi[:, half], left, over_rows, preferred_element_type=F32)
        product = product + lax.dot_general(gj[:, half], left, over_rows, preferred_element_type=F32)
        part[pl.ds(h * 8, 8)] = product.astype(BF16).reshape(8, SHARD, BROAD)
        if turn_id == 1:
            mine[...] = product.reshape(8, SHARD, BROAD)

        for o in PLANE:
            if (o < 8) == (turn_id == 1):
                remote(part.at[c ^ o], landed.at[c], g_ss.at[o], g_rs.at[o], (r, c ^ o)).start()

    out[:, :BROAD] = mine[c % 8]
    out[:, LINE_AT:BOTH_AT] = line_go(z_whole, z_other, z_part, z_landed, z_sem, h_ss, h_rs)

    def plane_sum(part_ref, landed_ref, ss, rs, first, width):
        def add(o, carry):
            frm = c ^ o
            remote(part_ref.at[frm], landed_ref.at[frm], ss.at[o], rs.at[o], (r, frm)).wait_recv()
            out[:, first : first + width] += landed_ref[frm].astype(F32)
            return carry

        lax.fori_loop(1, 16, add, 0)

    def plane_sent(part_ref, landed_ref, ss, rs):
        def wait(o, carry):
            frm = c ^ o
            remote(part_ref.at[frm], landed_ref.at[frm], ss.at[o], rs.at[o], (r, frm)).wait_send()
            return carry

        lax.fori_loop(1, 16, wait, 0)

    line_sum(ez_landed, e_ss, e_rs, BOTH_AT, EARLY)
    plane_sum(ep_part, ep_landed, f_ss, f_rs, BOTH_AT, EARLY)
    line_sent(ez_part, ez_landed, e_ss, e_rs)
    plane_sent(ep_part, ep_landed, f_ss, f_rs)
    leave(x1s, x1r.at[c], x1_ss, x1_rs, peer_c)
    leave(x2s, x2r.at[c], x2_ss, x2_rs, peer_c)
    leave(pt.at[:, group], jp.at[r], p_ss, p_rs, peer_r)
    leave(we.at[:, group], jw.at[r], w_ss, w_rs, peer_r)
    for copy in sent:
        copy.wait_send()
    line_sum(z_landed, h_ss, h_rs, LINE_AT, NARROW)
    plane_sum(part, landed, g_ss, g_rs, 0, BROAD)
    line_sent(z_part, z_landed, h_ss, h_rs)
    plane_sent(part, landed, g_ss, g_rs)


def body(embed, positives, placement):
    dma = pltpu.SemaphoreType.DMA
    return pl.pallas_call(
        kernel,
        out_shape=jax.ShapeDtypeStruct((SHARD, WIDTH), F32),
        in_specs=[pl.BlockSpec(memory_space=pl.ANY)] * 3,
        out_specs=pl.BlockSpec(memory_space=pltpu.VMEM),
        scratch_shapes=[
            pltpu.VMEM((COLS, SHARD, WIDTH), BF16),
            pltpu.VMEM((ROWS, SHARD, WIDTH), BF16),
            pltpu.VMEM((BLOCK, BLOCK), F32),
            pltpu.VMEM((POS, BLOCK, BLOCK), F32),
            pltpu.VMEM((POS, BLOCK, BLOCK), F32),
            pltpu.VMEM((BLOCK, BLOCK), BF16),
            pltpu.VMEM((BLOCK, BLOCK), BF16),
            pltpu.VMEM((COLS, SHARD, BROAD), BF16),
            pltpu.VMEM((COLS, SHARD, BROAD), BF16),
            pltpu.VMEM((8, SHARD, BROAD), F32),
            pltpu.VMEM((ZS, SHARD, NARROW), BF16),
            pltpu.VMEM((ZS, SHARD, NARROW), BF16),
            pltpu.VMEM((ZS, 2, SHARD, NARROW), F32),
            pltpu.VMEM((ZS, SHARD, NARROW), F32),
            pltpu.VMEM((ZS, SHARD, EARLY), BF16),
            pltpu.VMEM((ZS, SHARD, EARLY), BF16),
            pltpu.VMEM((ZS, 2, SHARD, EARLY), F32),
            pltpu.VMEM((ZS, SHARD, EARLY), F32),
            pltpu.VMEM((COLS, SHARD, EARLY), BF16),
            pltpu.VMEM((COLS, SHARD, EARLY), BF16),
            pltpu.VMEM((8, SHARD, EARLY), F32),
            pltpu.VMEM((POS, BLOCK), I32),
            pltpu.VMEM((64, LANES), I32),
            pltpu.VMEM((8, BLOCK), I32),
            pltpu.VMEM((8, BLOCK), F32),
            pltpu.VMEM((8, BLOCK), F32),
            pltpu.VMEM((8, BLOCK // 2), F32),
            pltpu.VMEM((COLS, 8, BLOCK // 2), F32),
            pltpu.VMEM((8, BLOCK), F32),
            pltpu.VMEM((COLS, 8, BLOCK), F32),
            pltpu.VMEM((ROWS, 8, LANES), F32),
            pltpu.VMEM((ROWS, 8, LANES), F32),
            pltpu.VMEM((LANES, LANES), F32),
            pltpu.VMEM((4 * POS, BLOCK, LANES), F32),
            dma((4,)),
            dma((2,)),
            dma((2,)),
            dma((32,)),
            dma((32,)),
        ]
        + [dma((16,))] * 20,
        compiler_params=pltpu.CompilerParams(
            collective_id=0, has_side_effects=True, vmem_limit_bytes=60 * 1024 * 1024
        ),
        cost_estimate=pl.CostEstimate(flops=1 << 31, bytes_accessed=1 << 22, transcendentals=1 << 21),
        name="smooth_ap",
    )(embed, positives.T, placement.reshape(64, LANES))


def solution(mesh):
    return jax.shard_map(
        body,
        mesh=mesh,
        in_specs=(P(("row", "col"), None), P("row", None), P()),
        out_specs=P(("row", "col"), None),
        check_vma=False,
    )
```

```python
import functools

import jax
import jax.numpy as jnp
from jax import lax
from jax.experimental import pallas as pl
from jax.experimental.pallas import tpu as pltpu
from jax.sharding import PartitionSpec as P

MESH = pl.DeviceIdType.MESH
TAU = 0.02
HALF = 0.5 / TAU
F32, BF16, I32 = jnp.float32, jnp.bfloat16, jnp.int32

ROWS, COLS, ZS = 16, 16, 8
SHARD, WIDTH, POS = 32, 1024, 4
BLOCK = SHARD * COLS
LANES = 128
STEP = 64

BROAD, NARROW, EARLY = 256, 256, 512
LINE_AT, BOTH_AT = BROAD, BROAD + NARROW

DEPTHS = (4, 3, 5, 2, 6, 1, 7)
PLANE = (10, 11, 14, 9, 6, 8, 2, 15, 13, 7, 5, 12, 4, 3, 1)
LINE = (8, 9, 10, 11, 6, 7, 14, 15, 12, 13, 4, 5, 2, 3, 1)


def remote(src, dst, send, recv, device):
    return pltpu.make_async_remote_copy(
        src_ref=src, dst_ref=dst, send_sem=send, recv_sem=recv,
        device_id=device, device_id_type=MESH,
    )


def kernel(
    embed, positives, placement, out,
    a_buf, c_buf, s_ref, vi, vj, gi, gj, part, landed, mine, z_part, z_landed, z_whole, z_other,
    ez_part, ez_landed, e_whole, e_other, ep_part, ep_landed, e_mine,
    pos_in, place_in, tgt, pt, we, x1s, x1r, x2s, x2r, jp, jw, jt, jc,
    in_sem, z_sem, e_sem, plane_s, plane_r, z_s, z_r, sib_s, sib_r,
    x1_ss, x1_rs, x2_ss, x2_rs, p_ss, p_rs, w_ss, w_rs, g_ss, g_rs, h_ss, h_rs,
    e_ss, e_rs, f_ss, f_rs,
):
    r, c = lax.axis_index("row"), lax.axis_index("col")
    z, core = r // 2, r % 2
    y, x = c // 4, c % 4

    def in_plane(o):
        return (r, ((y + o[0]) % 4) * 4 + (x + o[1]) % 4)

    def in_line(d, k=0):
        return (((z + d) % ZS) * 2 + (core + k) % 2, c)

    loads = [
        pltpu.make_async_copy(embed, a_buf.at[c], in_sem.at[0]),
        pltpu.make_async_copy(embed, c_buf.at[r], in_sem.at[1]),
        pltpu.make_async_copy(positives, pos_in, in_sem.at[2]),
        pltpu.make_async_copy(placement, place_in, in_sem.at[3]),
    ]
    for load in loads:
        load.start()
    barrier = pltpu.get_barrier_semaphore()

    near = [in_line(2), in_line(6), in_plane((0, 2)), in_plane((2, 0)), in_line(1), in_line(7)]
    near += [in_plane((0, 1)), in_plane((1, 0)), in_plane((0, 3)), in_plane((3, 0)), in_line(0, 1)]
    for peer in near:
        pl.semaphore_signal(barrier, inc=1, device_id=peer, device_id_type=MESH)
    for load in loads:
        load.wait()
    pl.semaphore_wait(barrier, len(near))

    sent = []

    def go(src, dst, ss, rs, device):
        copy = remote(src, dst, ss, rs, device)
        copy.start()
        sent.append(copy)

    def z_send(d, block, rows, step, slot):
        view = c_buf.at[block, rows]
        go(view, view, z_s.at[slot], z_r.at[slot], in_line(step % ZS))

    def z_wait(d, rows, slot):
        view = c_buf.at[from_z(d), rows]
        remote(view, view, z_s.at[slot], z_r.at[slot], in_line(d % ZS)).wait_recv()

    def from_z(d, k=0):
        return ((z + ZS - d) % ZS) * 2 + (core + k) % 2

    def from_plane(dy, dx):
        return ((y + 4 - dy) % 4) * 4 + (x + 4 - dx) % 4

    def a_send(block, rows, dy, dx, slot):
        view = a_buf.at[block, rows]
        go(view, view, plane_s.at[slot], plane_r.at[slot], in_plane((dy, dx)))

    def a_wait(dy, dx, rows, slot):
        view = a_buf.at[from_plane(dy, dx), rows]
        remote(view, view, plane_s.at[slot], plane_r.at[slot], in_plane((dy, dx))).wait_recv()

    def sib_send(d, rows, slot):
        view = c_buf.at[from_z(d), rows]
        go(view, view, sib_s.at[slot], sib_r.at[slot], in_line(0, 1))

    def sib_wait(d, rows, slot):
        view = c_buf.at[from_z(d, 1), rows]
        remote(view, view, sib_s.at[slot], sib_r.at[slot], in_line(0, 1)).wait_recv()

    every, top, low_half = pl.ds(0, SHARD), pl.ds(0, SHARD // 2), pl.ds(SHARD // 2, SHARD // 2)
    halves = (top, low_half)

    def x_first(d, h):
        a_send(c, halves[h], 0, d, 4 * d - 4 + h)

    def y_first(d, h):
        a_send(c, halves[h], d, 0, 4 * d - 2 + h)

    for d in (2, 1, 3):
        x_first(d, 0)
        y_first(d, 1)
    z_send(2, r, top, 2, 0)
    z_send(-2, r, low_half, -2, 1)
    z_send(2, r, low_half, 2, 2)
    z_send(-2, r, top, -2, 3)
    z_send(1, r, every, 1, 4)
    z_send(-1, r, every, -1, 5)
    for d in (2, 1, 3):
        x_first(d, 1)
        y_first(d, 0)
    sib_send(0, every, 0)

    table = place_in[...]
    high = (table // 64).astype(F32).astype(BF16)
    low = (table % 64).astype(F32).astype(BF16)
    lane_id = lax.broadcasted_iota(I32, (LANES, BLOCK), 0)
    row_id = lax.broadcasted_iota(I32, (64, BLOCK), 0)
    for m in range(POS):
        entity = pos_in[m : m + 1, :]
        hot = jnp.where(lane_id == entity % LANES, 1.0, 0.0).astype(BF16)
        value = jnp.dot(high, hot, preferred_element_type=F32) * 64.0 + jnp.dot(
            low, hot, preferred_element_type=F32
        )
        found = jnp.sum(jnp.where(row_id == entity // LANES, value, 0.0), axis=0, keepdims=True)
        pt[POS + m : POS + m + 1, :] = found
        where = found.astype(I32)
        here = (where // SHARD) % COLS == c
        tgt[m : m + 1, :] = jnp.where(here, (where // BLOCK) * SHARD + where % SHARD, -1)

    def turn(d):
        a_wait(0, d, top, 4 * d - 4)
        for e in (2, 1, 3):
            a_send(from_plane(0, d), top, e, 0, 12 + 3 * (d - 1) + e - 1)
        a_wait(d, 0, low_half, 4 * d - 1)
        for e in (2, 1, 3):
            a_send(from_plane(d, 0), low_half, 0, e, 21 + 3 * (d - 1) + e - 1)

    turn(1)
    turn(3)
    z_wait(2, top, 0)
    z_send(4, from_z(2), top, 2, 6)
    z_send(3, from_z(2), top, 1, 7)
    z_wait(-2, low_half, 1)
    z_send(-4, from_z(-2), low_half, -2, 8)
    z_send(-3, from_z(-2), low_half, -1, 9)
    z_wait(2, low_half, 2)
    z_send(3, from_z(2), low_half, 1, 10)
    z_wait(-2, top, 3)
    z_send(-3, from_z(-2), top, -1, 11)
    turn(2)
    for d, slot in ((2, 2), (-2, 6)):
        sib_send(d, every, slot)
    for d, slot in ((1, 4), (-1, 5)):
        z_wait(d, every, slot)
        sib_send(d, every, 1 if d == 1 else 7)
    z_wait(4, top, 6)
    sib_send(4, top, 4)
    z_wait(-4, low_half, 8)
    sib_send(-4, low_half, 8)
    z_wait(3, top, 7)
    z_wait(3, low_half, 10)
    sib_send(3, every, 3)
    z_wait(-3, low_half, 9)
    z_wait(-3, top, 11)
    sib_send(-3, every, 5)
    for d in (1, 3, 2):
        a_wait(0, d, low_half, 4 * d - 3)
        a_wait(d, 0, top, 4 * d - 2)
    for d in (1, 3, 2):
        for e in (1, 3, 2):
            a_wait(e, d, top, 12 + 3 * (d - 1) + e - 1)
            a_wait(d, e, low_half, 21 + 3 * (d - 1) + e - 1)
    for d, slot in ((0, 0), (1, 1), (-1, 7), (2, 2), (-2, 6), (3, 3), (-3, 5)):
        sib_wait(d, every, slot)
    sib_wait(4, top, 4)
    sib_wait(-4, low_half, 8)

    anchors = a_buf[...].reshape(BLOCK, WIDTH)
    for h in range(2):
        cand = c_buf[8 * h : 8 * h + 8].reshape(BLOCK // 2, WIDTH)
        s_ref[256 * h : 256 * h + 256, :] = HALF * lax.dot_general(
            cand, anchors, (((1,), (1,)), ((), ())), preferred_element_type=F32
        )
    tile = s_ref[pl.ds(pl.multiple_of(r * SHARD, SHARD), SHARD), pl.ds(pl.multiple_of(y * LANES, LANES), LANES)]
    me_row = lax.broadcasted_iota(I32, (SHARD, LANES), 0)
    me_lane = lax.broadcasted_iota(I32, (SHARD, LANES), 1)
    s_ref[pl.ds(pl.multiple_of(r * SHARD, SHARD), SHARD), pl.ds(pl.multiple_of(y * LANES, LANES), LANES)] = (
        jnp.where(me_lane - x * SHARD == me_row, -1e30, tile)
    )

    iota_k = lax.broadcasted_iota(I32, (STEP, LANES), 0)
    iota_a = lax.broadcasted_iota(I32, (STEP, LANES), 1)
    steps = BLOCK // STEP

    def fold(value):
        return jnp.sum(value.reshape(STEP // 8, 8, LANES), axis=0)

    def cut(q):
        return slice(q * LANES, (q + 1) * LANES)

    for q in range(4):
        rows = [tgt[m : m + 1, cut(q)] for m in range(POS)]

        def pick(i, acc, q=q, rows=rows):
            k0 = pl.multiple_of(i * STEP, STEP)
            score = s_ref[pl.ds(k0, STEP), cut(q)]
            return tuple(
                acc[m] + fold(jnp.where(iota_k == rows[m] - k0, score, 0.0)) for m in range(POS)
            )

        acc = lax.fori_loop(0, steps, pick, (jnp.zeros((8, LANES), F32),) * POS)
        for m in range(POS):
            x1s[m * POS + q : m * POS + q + 1, :] = jnp.sum(acc[m], axis=0, keepdims=True)

    def exchange(src, dst, ss, rs, peer, order):
        for o in order:
            remote(src, dst, ss.at[o], rs.at[o], peer(o)).start()

    def arrive(src, dst, ss, rs, peer, index):
        def wait(o, carry):
            remote(src, dst.at[index ^ o], ss.at[o], rs.at[o], peer(o)).wait_recv()
            return carry

        lax.fori_loop(1, 16, wait, 0)

    def leave(src, dst, ss, rs, peer):
        def wait(o, carry):
            remote(src, dst, ss.at[o], rs.at[o], peer(o)).wait_send()
            return carry

        lax.fori_loop(1, 16, wait, 0)

    def peer_c(o):
        return (r, c ^ o)

    def peer_r(o):
        return (r ^ o, c)

    exchange(x1s, x1r.at[c], x1_ss, x1_rs, peer_c, PLANE)
    x1r[c] = x1s[...]
    arrive(x1s, x1r, x1_ss, x1_rs, peer_c, c)
    scores = jnp.sum(x1r[...], axis=0)
    for m in range(POS):
        for q in range(4):
            pt[m : m + 1, cut(q)] = scores[m * POS + q : m * POS + q + 1, :]

    group = pl.ds(pl.multiple_of(y * LANES, LANES), LANES)
    def line_meet(tiles, columns, whole, other, sem):
        for h in range(2):
            rows = slice(256 * h, 256 * h + 256)
            product = sum(jnp.dot(g[rows, :], columns, preferred_element_type=F32) for g in tiles)
            whole[4 * h : 4 * h + 4] = product.reshape(4, 2, SHARD, product.shape[1])
        remote(whole.at[:, 1 - core], other, sem.at[0], sem.at[1], (r ^ 1, c)).start()

    def line_go(whole, other, part_ref, landed_ref, sem, ss, rs):
        meet = remote(whole.at[:, 1 - core], other, sem.at[0], sem.at[1], (r ^ 1, c))
        meet.wait_recv()
        part_ref[...] = (whole[:, core] + other[...]).astype(BF16)
        for d in DEPTHS:
            to = (z + d) % ZS
            remote(part_ref.at[to], landed_ref.at[z], ss.at[d], rs.at[d], in_line(d)).start()
        meet.wait_send()
        return whole[z, core] + other[z]

    def line_sum(landed_ref, ss, rs, first, width):
        for d in reversed(DEPTHS):
            frm = (z + ZS - d) % ZS
            remote(landed_ref.at[frm], landed_ref.at[frm], ss.at[d], rs.at[d], in_line(d)).wait_recv()
            out[:, first : first + width] += landed_ref[frm].astype(F32)

    def line_sent(part_ref, landed_ref, ss, rs):
        for d in DEPTHS:
            to = (z + d) % ZS
            remote(part_ref.at[to], landed_ref.at[z], ss.at[d], rs.at[d], in_line(d)).wait_send()

    for q in range(4):
        rows = [pt[m : m + 1, cut(q)] for m in range(POS)]

        def count(i, acc, q=q, rows=rows):
            k0 = pl.multiple_of(i * STEP, STEP)
            score = s_ref[pl.ds(k0, STEP), cut(q)]
            new = []
            for m in range(POS):
                t = jnp.tanh(score - rows[m])
                u = 1.0 + t
                v = 1.0 - t * t
                vi[m, pl.ds(k0, STEP), cut(q)] = v
                new.append(acc[2 * m] + fold(u))
                new.append(acc[2 * m + 1] + fold(v))
            return tuple(new)

        acc = lax.fori_loop(0, steps, count, (jnp.zeros((8, LANES), F32),) * (2 * POS))
        for m in range(POS):
            at = m * POS + q
            x2s[at : at + 1, :] = jnp.sum(acc[2 * m], axis=0, keepdims=True)
            x2s[16 + at : 17 + at, :] = jnp.sum(acc[2 * m + 1], axis=0, keepdims=True)
    exchange(x2s, x2r.at[c], x2_ss, x2_rs, peer_c, PLANE)
    x2r[c] = x2s[...]
    exchange(pt.at[:, group], jp.at[r], p_ss, p_rs, peer_r, LINE)
    jp[r] = pt[:, group]

    def columns(src, first):
        jt[...] = jnp.transpose(src[...].reshape(ROWS * 8, LANES))
        mine_cols = jt[pl.ds(pl.multiple_of(x * SHARD, SHARD), SHARD), :]
        for b in range(ROWS):
            for n in range(8):
                jc[first + n, b * SHARD : (b + 1) * SHARD, :] = jnp.broadcast_to(
                    mine_cols[:, b * 8 + n : b * 8 + n + 1], (SHARD, LANES)
                )

    arrive(x2s, x2r, x2_ss, x2_rs, peer_c, c)
    total = jnp.sum(x2r[...], axis=0)
    factor = 1.0 / (POS * SHARD * ROWS * COLS)

    def of(value, m):
        return value[m * POS : (m + 1) * POS]

    p = [of(scores, m) for m in range(POS)]
    rank = [0.5 + 0.5 * of(total[0:16], m) for m in range(POS)]
    slope = [0.25 * of(total[16:32], m) for m in range(POS)]
    prank = [jnp.full((POS, LANES), 1.0, F32) for _ in range(POS)]
    grad = [-factor / rank[m] for m in range(POS)]
    pulled = [jnp.zeros((POS, LANES), F32) for _ in range(POS)]
    for m in range(POS):
        for n in range(m + 1, POS):
            t = jnp.tanh(p[n] - p[m])
            prank[m] = prank[m] + 0.5 * (1.0 + t)
            prank[n] = prank[n] + 0.5 * (1.0 - t)
            pair = (0.25 / TAU) * (1.0 - t) * (1.0 + t) * (grad[n] - grad[m])
            pulled[m] = pulled[m] + pair
            pulled[n] = pulled[n] - pair
    for m in range(POS):
        weight = prank[m] / (rank[m] * rank[m]) * factor / TAU
        quarter, extra = 0.25 * weight, pulled[m] - weight * slope[m]
        for q in range(4):
            we[m : m + 1, cut(q)] = quarter[q : q + 1, :]
            we[POS + m : POS + m + 1, cut(q)] = extra[q : q + 1, :]

    exchange(we.at[:, group], jw.at[r], w_ss, w_rs, peer_r, LINE)
    jw[r] = we[:, group]

    for q in range(4):
        rows = [tgt[m : m + 1, cut(q)] for m in range(POS)]
        weights = [we[m : m + 1, cut(q)] for m in range(POS)]
        extras = [we[POS + m : POS + m + 1, cut(q)] for m in range(POS)]

        def tile_i(i, carry, q=q, rows=rows, weights=weights, extras=extras):
            k0 = pl.multiple_of(i * STEP, STEP)
            dense = weights[0] * vi[0, pl.ds(k0, STEP), cut(q)]
            for m in range(1, POS):
                dense = dense + weights[m] * vi[m, pl.ds(k0, STEP), cut(q)]
            for m in range(POS):
                dense = dense + jnp.where(iota_k == rows[m] - k0, extras[m], 0.0)
            gi[pl.ds(k0, STEP), cut(q)] = dense.astype(BF16)
            return carry

        lax.fori_loop(0, steps, tile_i, 0)

    over_rows = (((0,), (0,)), ((), ()))
    line_meet((gi,), a_buf[:, :, BOTH_AT:].reshape(BLOCK, EARLY), e_whole, e_other, e_sem)
    early_plane = c_buf[:, :, BOTH_AT:].reshape(BLOCK, EARLY)
    for h in range(2):
        rows = slice(256 * h, 256 * h + 256)
        product = lax.dot_general(gi[:, rows], early_plane, over_rows, preferred_element_type=F32)
        ep_part[8 * h : 8 * h + 8] = product.astype(BF16).reshape(8, SHARD, EARLY)

        @pl.when(c // 8 == h)
        def _(product=product):
            e_mine[...] = product.reshape(8, SHARD, EARLY)

    for o in PLANE:
        remote(ep_part.at[c ^ o], ep_landed.at[c], f_ss.at[o], f_rs.at[o], (r, c ^ o)).start()
    out[:, BOTH_AT:] = e_mine[c % 8]

    arrive(pt.at[:, group], jp, p_ss, p_rs, peer_r, r)
    columns(jp, 0)
    out[:, BOTH_AT:] += line_go(e_whole, e_other, ez_part, ez_landed, e_sem, e_ss, e_rs)

    def slopes(i, carry):
        k0 = pl.multiple_of(i * STEP, STEP)
        for m in range(POS):
            col = jc[m, pl.ds(k0, STEP), :]
            for q in range(4):
                t = jnp.tanh(s_ref[pl.ds(k0, STEP), cut(q)] - col)
                vj[m, pl.ds(k0, STEP), cut(q)] = 1.0 - t * t
            where = jc[POS + m, pl.ds(k0, STEP), :].astype(I32)
            jc[POS + m, pl.ds(k0, STEP), :] = jnp.where(
                where // BLOCK == r, where % BLOCK, -1
            ).astype(F32)
        return carry

    lax.fori_loop(0, steps, slopes, 0)

    arrive(we.at[:, group], jw, w_ss, w_rs, peer_r, r)
    columns(jw, 2 * POS)

    def tile_j(i, carry):
        for part_id in range(2):
            k0 = pl.ds(pl.multiple_of(i * 32 + part_id * 16, 16), 16)
            weights = [jc[2 * POS + m, k0, :] for m in range(POS)]
            extras = [jc[3 * POS + m, k0, :] for m in range(POS)]
            at = [jc[POS + m, k0, :] for m in range(POS)]
            for q in range(4):
                dense = weights[0] * vj[0, k0, cut(q)]
                for m in range(1, POS):
                    dense = dense + weights[m] * vj[m, k0, cut(q)]
                lane = (iota_a[0:16, :] + q * LANES).astype(F32)
                for m in range(POS):
                    dense = dense + jnp.where(at[m] == lane, extras[m], 0.0)
                gj[k0, cut(q)] = dense.astype(BF16)
        return carry

    lax.fori_loop(0, BLOCK // 32, tile_j, 0)

    line_meet((gi, gj), a_buf[:, :, LINE_AT:BOTH_AT].reshape(BLOCK, NARROW), z_whole, z_other, z_sem)

    left = c_buf[:, :, :BROAD].reshape(BLOCK, BROAD)
    wide = 2 * LANES
    for turn_id in range(2):
        h = (c // 8) ^ (1 - turn_id)
        half = pl.ds(pl.multiple_of(h * wide, wide), wide)
        product = lax.dot_general(gi[:, half], left, over_rows, preferred_element_type=F32)
        product = product + lax.dot_general(gj[:, half], left, over_rows, preferred_element_type=F32)
        part[pl.ds(h * 8, 8)] = product.astype(BF16).reshape(8, SHARD, BROAD)
        if turn_id == 1:
            mine[...] = product.reshape(8, SHARD, BROAD)

        for o in PLANE:
            if (o < 8) == (turn_id == 1):
                remote(part.at[c ^ o], landed.at[c], g_ss.at[o], g_rs.at[o], (r, c ^ o)).start()

    out[:, :BROAD] = mine[c % 8]
    out[:, LINE_AT:BOTH_AT] = line_go(z_whole, z_other, z_part, z_landed, z_sem, h_ss, h_rs)

    def plane_sum(part_ref, landed_ref, ss, rs, first, width):
        def add(o, carry):
            frm = c ^ o
            remote(part_ref.at[frm], landed_ref.at[frm], ss.at[o], rs.at[o], (r, frm)).wait_recv()
            out[:, first : first + width] += landed_ref[frm].astype(F32)
            return carry

        lax.fori_loop(1, 16, add, 0)

    def plane_sent(part_ref, landed_ref, ss, rs):
        def wait(o, carry):
            frm = c ^ o
            remote(part_ref.at[frm], landed_ref.at[frm], ss.at[o], rs.at[o], (r, frm)).wait_send()
            return carry

        lax.fori_loop(1, 16, wait, 0)

    line_sum(ez_landed, e_ss, e_rs, BOTH_AT, EARLY)
    plane_sum(ep_part, ep_landed, f_ss, f_rs, BOTH_AT, EARLY)
    line_sent(ez_part, ez_landed, e_ss, e_rs)
    plane_sent(ep_part, ep_landed, f_ss, f_rs)
    leave(x1s, x1r.at[c], x1_ss, x1_rs, peer_c)
    leave(x2s, x2r.at[c], x2_ss, x2_rs, peer_c)
    leave(pt.at[:, group], jp.at[r], p_ss, p_rs, peer_r)
    leave(we.at[:, group], jw.at[r], w_ss, w_rs, peer_r)
    for copy in sent:
        copy.wait_send()
    line_sum(z_landed, h_ss, h_rs, LINE_AT, NARROW)
    plane_sum(part, landed, g_ss, g_rs, 0, BROAD)
    line_sent(z_part, z_landed, h_ss, h_rs)
    plane_sent(part, landed, g_ss, g_rs)


def body(embed, positives, placement):
    dma = pltpu.SemaphoreType.DMA
    return pl.pallas_call(
        kernel,
        out_shape=pltpu.VMEM((SHARD, WIDTH), F32),
        in_specs=[pl.BlockSpec(memory_space=pl.ANY)] * 3,
        out_specs=pl.BlockSpec(memory_space=pltpu.VMEM),
        scratch_shapes=[
            pltpu.VMEM((COLS, SHARD, WIDTH), BF16),
            pltpu.VMEM((ROWS, SHARD, WIDTH), BF16),
            pltpu.VMEM((BLOCK, BLOCK), F32),
            pltpu.VMEM((POS, BLOCK, BLOCK), F32),
            pltpu.VMEM((POS, BLOCK, BLOCK), F32),
            pltpu.VMEM((BLOCK, BLOCK), BF16),
            pltpu.VMEM((BLOCK, BLOCK), BF16),
            pltpu.VMEM((COLS, SHARD, BROAD), BF16),
            pltpu.VMEM((COLS, SHARD, BROAD), BF16),
            pltpu.VMEM((8, SHARD, BROAD), F32),
            pltpu.VMEM((ZS, SHARD, NARROW), BF16),
            pltpu.VMEM((ZS, SHARD, NARROW), BF16),
            pltpu.VMEM((ZS, 2, SHARD, NARROW), F32),
            pltpu.VMEM((ZS, SHARD, NARROW), F32),
            pltpu.VMEM((ZS, SHARD, EARLY), BF16),
            pltpu.VMEM((ZS, SHARD, EARLY), BF16),
            pltpu.VMEM((ZS, 2, SHARD, EARLY), F32),
            pltpu.VMEM((ZS, SHARD, EARLY), F32),
            pltpu.VMEM((COLS, SHARD, EARLY), BF16),
            pltpu.VMEM((COLS, SHARD, EARLY), BF16),
            pltpu.VMEM((8, SHARD, EARLY), F32),
            pltpu.VMEM((POS, BLOCK), I32),
            pltpu.VMEM((64, LANES), I32),
            pltpu.VMEM((8, BLOCK), I32),
            pltpu.VMEM((8, BLOCK), F32),
            pltpu.VMEM((8, BLOCK), F32),
            pltpu.VMEM((16, LANES), F32),
            pltpu.VMEM((COLS, 16, LANES), F32),
            pltpu.VMEM((32, LANES), F32),
            pltpu.VMEM((COLS, 32, LANES), F32),
            pltpu.VMEM((ROWS, 8, LANES), F32),
            pltpu.VMEM((ROWS, 8, LANES), F32),
            pltpu.VMEM((LANES, LANES), F32),
            pltpu.VMEM((4 * POS, BLOCK, LANES), F32),
            dma((4,)),
            dma((2,)),
            dma((2,)),
            dma((32,)),
            dma((32,)),
        ]
        + [dma((16,))] * 20,
        compiler_params=pltpu.CompilerParams(
            collective_id=0, has_side_effects=True, vmem_limit_bytes=60 * 1024 * 1024
        ),
        cost_estimate=pl.CostEstimate(flops=1 << 31, bytes_accessed=1 << 22, transcendentals=1 << 21),
        name="smooth_ap",
    )(embed, positives.T, placement.reshape(64, LANES))


def solution(mesh):
    return jax.shard_map(
        body,
        mesh=mesh,
        in_specs=(P(("row", "col"), None), P("row", None), P()),
        out_specs=P(("row", "col"), None),
        check_vma=False,
    )
```

```python
import functools

import jax
import jax.numpy as jnp
from jax import lax
from jax.experimental import pallas as pl
from jax.experimental.pallas import tpu as pltpu
from jax.sharding import PartitionSpec as P

MESH = pl.DeviceIdType.MESH
TAU = 0.02
HALF = 0.5 / TAU
F32, BF16, I32 = jnp.float32, jnp.bfloat16, jnp.int32

ROWS, COLS, ZS = 16, 16, 8
SHARD, WIDTH, POS = 32, 1024, 4
BLOCK = SHARD * COLS
LANES = 128
STEP = 64

BROAD, NARROW, EARLY = 256, 256, 512
LINE_AT, BOTH_AT = BROAD, BROAD + NARROW

DEPTHS = (4, 3, 5, 2, 6, 1, 7)
PLANE = (10, 11, 14, 9, 6, 8, 2, 15, 13, 7, 5, 12, 4, 3, 1)
LINE = (8, 9, 10, 11, 6, 7, 14, 15, 12, 13, 4, 5, 2, 3, 1)


def remote(src, dst, send, recv, device):
    return pltpu.make_async_remote_copy(
        src_ref=src, dst_ref=dst, send_sem=send, recv_sem=recv,
        device_id=device, device_id_type=MESH,
    )


def kernel(
    embed, positives, placement, out,
    a_buf, c_buf, s_ref, vi, vj, gi, gj, part, landed, mine, z_part, z_landed, z_whole, z_other,
    ez_part, ez_landed, e_whole, e_other, ep_part, ep_landed, e_mine,
    pos_in, place_in, tgt, pt, we, x1s, x1r, x2s, x2r, jp, jw, jt, jc,
    in_sem, z_sem, e_sem, plane_s, plane_r, z_s, z_r, sib_s, sib_r,
    x1_ss, x1_rs, x2_ss, x2_rs, p_ss, p_rs, w_ss, w_rs, g_ss, g_rs, h_ss, h_rs,
    e_ss, e_rs, f_ss, f_rs,
):
    r, c = lax.axis_index("row"), lax.axis_index("col")
    z, core = r // 2, r % 2
    y, x = c // 4, c % 4

    def in_plane(o):
        return (r, ((y + o[0]) % 4) * 4 + (x + o[1]) % 4)

    def in_line(d, k=0):
        return (((z + d) % ZS) * 2 + (core + k) % 2, c)

    loads = [
        pltpu.make_async_copy(embed, a_buf.at[c], in_sem.at[0]),
        pltpu.make_async_copy(embed, c_buf.at[r], in_sem.at[1]),
        pltpu.make_async_copy(positives, pos_in, in_sem.at[2]),
        pltpu.make_async_copy(placement, place_in, in_sem.at[3]),
    ]
    barrier = pltpu.get_barrier_semaphore()

    near = [in_line(2), in_line(6), in_plane((0, 2)), in_plane((2, 0)), in_line(1), in_line(7)]
    near += [in_plane((0, 1)), in_plane((1, 0)), in_plane((0, 3)), in_plane((3, 0)), in_line(0, 1)]
    for peer in near:
        pl.semaphore_signal(barrier, inc=1, device_id=peer, device_id_type=MESH)
    for load in loads:
        load.start()
    for load in loads:
        load.wait()
    pl.semaphore_wait(barrier, len(near))

    sent = []

    def go(src, dst, ss, rs, device):
        copy = remote(src, dst, ss, rs, device)
        copy.start()
        sent.append(copy)

    def z_send(d, block, rows, step, slot):
        view = c_buf.at[block, rows]
        go(view, view, z_s.at[slot], z_r.at[slot], in_line(step % ZS))

    def z_wait(d, rows, slot):
        view = c_buf.at[from_z(d), rows]
        remote(view, view, z_s.at[slot], z_r.at[slot], in_line(d % ZS)).wait_recv()

    def from_z(d, k=0):
        return ((z + ZS - d) % ZS) * 2 + (core + k) % 2

    def from_plane(dy, dx):
        return ((y + 4 - dy) % 4) * 4 + (x + 4 - dx) % 4

    def a_send(block, rows, dy, dx, slot):
        view = a_buf.at[block, rows]
        go(view, view, plane_s.at[slot], plane_r.at[slot], in_plane((dy, dx)))

    def a_wait(dy, dx, rows, slot):
        view = a_buf.at[from_plane(dy, dx), rows]
        remote(view, view, plane_s.at[slot], plane_r.at[slot], in_plane((dy, dx))).wait_recv()

    def sib_send(d, rows, slot):
        view = c_buf.at[from_z(d), rows]
        go(view, view, sib_s.at[slot], sib_r.at[slot], in_line(0, 1))

    def sib_wait(d, rows, slot):
        view = c_buf.at[from_z(d, 1), rows]
        remote(view, view, sib_s.at[slot], sib_r.at[slot], in_line(0, 1)).wait_recv()

    every, top, low_half = pl.ds(0, SHARD), pl.ds(0, SHARD // 2), pl.ds(SHARD // 2, SHARD // 2)
    halves = (top, low_half)

    def x_first(d, h):
        a_send(c, halves[h], 0, d, 4 * d - 4 + h)

    def y_first(d, h):
        a_send(c, halves[h], d, 0, 4 * d - 2 + h)

    for d in (2, 1, 3):
        x_first(d, 0)
        y_first(d, 1)
    z_send(2, r, top, 2, 0)
    z_send(-2, r, low_half, -2, 1)
    z_send(2, r, low_half, 2, 2)
    z_send(-2, r, top, -2, 3)
    z_send(1, r, every, 1, 4)
    z_send(-1, r, every, -1, 5)
    for d in (2, 1, 3):
        x_first(d, 1)
        y_first(d, 0)
    sib_send(0, every, 0)

    table = place_in[...]
    high = (table // 64).astype(F32).astype(BF16)
    low = (table % 64).astype(F32).astype(BF16)
    lane_id = lax.broadcasted_iota(I32, (LANES, BLOCK), 0)
    row_id = lax.broadcasted_iota(I32, (64, BLOCK), 0)
    for m in range(POS):
        entity = pos_in[m : m + 1, :]
        hot = jnp.where(lane_id == entity % LANES, 1.0, 0.0).astype(BF16)
        value = jnp.dot(high, hot, preferred_element_type=F32) * 64.0 + jnp.dot(
            low, hot, preferred_element_type=F32
        )
        found = jnp.sum(jnp.where(row_id == entity // LANES, value, 0.0), axis=0, keepdims=True)
        pt[POS + m : POS + m + 1, :] = found
        where = found.astype(I32)
        here = (where // SHARD) % COLS == c
        tgt[m : m + 1, :] = jnp.where(here, (where // BLOCK) * SHARD + where % SHARD, -1)

    def turn(d):
        a_wait(0, d, top, 4 * d - 4)
        for e in (2, 1, 3):
            a_send(from_plane(0, d), top, e, 0, 12 + 3 * (d - 1) + e - 1)
        a_wait(d, 0, low_half, 4 * d - 1)
        for e in (2, 1, 3):
            a_send(from_plane(d, 0), low_half, 0, e, 21 + 3 * (d - 1) + e - 1)

    turn(1)
    turn(3)
    z_wait(2, top, 0)
    z_send(4, from_z(2), top, 2, 6)
    z_send(3, from_z(2), top, 1, 7)
    z_wait(-2, low_half, 1)
    z_send(-4, from_z(-2), low_half, -2, 8)
    z_send(-3, from_z(-2), low_half, -1, 9)
    z_wait(2, low_half, 2)
    z_send(3, from_z(2), low_half, 1, 10)
    z_wait(-2, top, 3)
    z_send(-3, from_z(-2), top, -1, 11)
    turn(2)
    for d, slot in ((2, 2), (-2, 6)):
        sib_send(d, every, slot)
    for d, slot in ((1, 4), (-1, 5)):
        z_wait(d, every, slot)
        sib_send(d, every, 1 if d == 1 else 7)
    z_wait(4, top, 6)
    sib_send(4, top, 4)
    z_wait(-4, low_half, 8)
    sib_send(-4, low_half, 8)
    z_wait(3, top, 7)
    z_wait(3, low_half, 10)
    sib_send(3, every, 3)
    z_wait(-3, low_half, 9)
    z_wait(-3, top, 11)
    sib_send(-3, every, 5)
    for d in (1, 3, 2):
        a_wait(0, d, low_half, 4 * d - 3)
        a_wait(d, 0, top, 4 * d - 2)
    for d in (1, 3, 2):
        for e in (1, 3, 2):
            a_wait(e, d, top, 12 + 3 * (d - 1) + e - 1)
            a_wait(d, e, low_half, 21 + 3 * (d - 1) + e - 1)
    anchors = a_buf[...].reshape(BLOCK, WIDTH)
    iota_k = lax.broadcasted_iota(I32, (STEP, LANES), 0)
    iota_a = lax.broadcasted_iota(I32, (STEP, LANES), 1)
    steps = BLOCK // STEP

    def fold(value):
        return jnp.sum(value.reshape(STEP // 8, 8, LANES), axis=0)

    def cut(q):
        return slice(q * LANES, (q + 1) * LANES)

    def score(first, last):
        chips = [(z + i) % ZS for i in range(first, last)]
        cand = jnp.concatenate([c_buf[pl.ds(2 * chip, 2)].reshape(STEP, WIDTH) for chip in chips], axis=0)
        product = HALF * lax.dot_general(
            cand, anchors, (((1,), (1,)), ((), ())), preferred_element_type=F32
        )
        for i, chip in enumerate(chips):
            s_ref[pl.ds(pl.multiple_of(chip * STEP, STEP), STEP), :] = product[i * STEP : (i + 1) * STEP]

    def pick(first, last, sums):
        new = []
        for q in range(4):
            rows = [tgt[m : m + 1, cut(q)] for m in range(POS)]

            def step(i, acc, q=q, rows=rows):
                k0 = pl.multiple_of(((z + i) % ZS) * STEP, STEP)
                tile = s_ref[pl.ds(k0, STEP), cut(q)]
                return tuple(
                    acc[m] + fold(jnp.where(iota_k == rows[m] - k0, tile, 0.0)) for m in range(POS)
                )

            new.append(lax.fori_loop(first, last, step, sums[q]))
        return new

    for d, slot in ((0, 0), (1, 1), (-1, 7), (2, 2), (-2, 6)):
        sib_wait(d, every, slot)
    score(6, 11)
    own_rows = pl.ds(pl.multiple_of(r * SHARD, SHARD), SHARD)
    own_lanes = pl.ds(pl.multiple_of(y * LANES, LANES), LANES)
    me_row = lax.broadcasted_iota(I32, (SHARD, LANES), 0)
    me_lane = lax.broadcasted_iota(I32, (SHARD, LANES), 1)
    s_ref[own_rows, own_lanes] = jnp.where(me_lane - x * SHARD == me_row, -1e30, s_ref[own_rows, own_lanes])
    sums = pick(6, 11, [(jnp.zeros((8, LANES), F32),) * POS] * 4)
    for d, slot in ((3, 3), (-3, 5)):
        sib_wait(d, every, slot)
    sib_wait(4, top, 4)
    sib_wait(-4, low_half, 8)
    score(3, 6)
    sums = pick(3, 6, sums)
    for q in range(4):
        for m in range(POS):
            x1s[m * POS + q : m * POS + q + 1, :] = jnp.sum(sums[q][m], axis=0, keepdims=True)

    def exchange(src, dst, ss, rs, peer, order):
        for o in order:
            remote(src, dst, ss.at[o], rs.at[o], peer(o)).start()

    def arrive(src, dst, ss, rs, peer, index):
        def wait(o, carry):
            remote(src, dst.at[index ^ o], ss.at[o], rs.at[o], peer(o)).wait_recv()
            return carry

        lax.fori_loop(1, 16, wait, 0)

    def leave(src, dst, ss, rs, peer):
        def wait(o, carry):
            remote(src, dst, ss.at[o], rs.at[o], peer(o)).wait_send()
            return carry

        lax.fori_loop(1, 16, wait, 0)

    def peer_c(o):
        return (r, c ^ o)

    def peer_r(o):
        return (r ^ o, c)

    exchange(x1s, x1r.at[c], x1_ss, x1_rs, peer_c, PLANE)
    x1r[c] = x1s[...]
    arrive(x1s, x1r, x1_ss, x1_rs, peer_c, c)
    scores = jnp.sum(x1r[...], axis=0)
    for m in range(POS):
        for q in range(4):
            pt[m : m + 1, cut(q)] = scores[m * POS + q : m * POS + q + 1, :]

    group = pl.ds(pl.multiple_of(y * LANES, LANES), LANES)
    def line_meet(tiles, columns, whole, other, sem):
        for h in range(2):
            rows = slice(256 * h, 256 * h + 256)
            product = sum(jnp.dot(g[rows, :], columns, preferred_element_type=F32) for g in tiles)
            whole[4 * h : 4 * h + 4] = product.reshape(4, 2, SHARD, product.shape[1])
        remote(whole.at[:, 1 - core], other, sem.at[0], sem.at[1], (r ^ 1, c)).start()

    def line_go(whole, other, part_ref, landed_ref, sem, ss, rs):
        meet = remote(whole.at[:, 1 - core], other, sem.at[0], sem.at[1], (r ^ 1, c))
        meet.wait_recv()
        part_ref[...] = (whole[:, core] + other[...]).astype(BF16)
        for d in DEPTHS:
            to = (z + d) % ZS
            remote(part_ref.at[to], landed_ref.at[z], ss.at[d], rs.at[d], in_line(d)).start()
        meet.wait_send()
        return whole[z, core] + other[z]

    def line_sum(landed_ref, ss, rs, first, width):
        for d in reversed(DEPTHS):
            frm = (z + ZS - d) % ZS
            remote(landed_ref.at[frm], landed_ref.at[frm], ss.at[d], rs.at[d], in_line(d)).wait_recv()
            out[:, first : first + width] += landed_ref[frm].astype(F32)

    def line_sent(part_ref, landed_ref, ss, rs):
        for d in DEPTHS:
            to = (z + d) % ZS
            remote(part_ref.at[to], landed_ref.at[z], ss.at[d], rs.at[d], in_line(d)).wait_send()

    for q in range(4):
        rows = [pt[m : m + 1, cut(q)] for m in range(POS)]

        def count(i, acc, q=q, rows=rows):
            k0 = pl.multiple_of(i * STEP, STEP)
            score = s_ref[pl.ds(k0, STEP), cut(q)]
            new = []
            for m in range(POS):
                t = jnp.tanh(score - rows[m])
                u = 1.0 + t
                v = 1.0 - t * t
                vi[m, pl.ds(k0, STEP), cut(q)] = v
                new.append(acc[2 * m] + fold(u))
                new.append(acc[2 * m + 1] + fold(v))
            return tuple(new)

        acc = lax.fori_loop(0, steps, count, (jnp.zeros((8, LANES), F32),) * (2 * POS))
        for m in range(POS):
            at = m * POS + q
            x2s[at : at + 1, :] = jnp.sum(acc[2 * m], axis=0, keepdims=True)
            x2s[16 + at : 17 + at, :] = jnp.sum(acc[2 * m + 1], axis=0, keepdims=True)
    exchange(x2s, x2r.at[c], x2_ss, x2_rs, peer_c, PLANE)
    x2r[c] = x2s[...]
    exchange(pt.at[:, group], jp.at[r], p_ss, p_rs, peer_r, LINE)
    jp[r] = pt[:, group]

    def columns(src, first):
        jt[...] = jnp.transpose(src[...].reshape(ROWS * 8, LANES))
        mine_cols = jt[pl.ds(pl.multiple_of(x * SHARD, SHARD), SHARD), :]
        for b in range(ROWS):
            for n in range(8):
                jc[first + n, b * SHARD : (b + 1) * SHARD, :] = jnp.broadcast_to(
                    mine_cols[:, b * 8 + n : b * 8 + n + 1], (SHARD, LANES)
                )

    arrive(x2s, x2r, x2_ss, x2_rs, peer_c, c)
    total = jnp.sum(x2r[...], axis=0)
    factor = 1.0 / (POS * SHARD * ROWS * COLS)

    def of(value, m):
        return value[m * POS : (m + 1) * POS]

    p = [of(scores, m) for m in range(POS)]
    rank = [0.5 + 0.5 * of(total[0:16], m) for m in range(POS)]
    slope = [0.25 * of(total[16:32], m) for m in range(POS)]
    prank = [jnp.full((POS, LANES), 1.0, F32) for _ in range(POS)]
    grad = [-factor / rank[m] for m in range(POS)]
    pulled = [jnp.zeros((POS, LANES), F32) for _ in range(POS)]
    for m in range(POS):
        for n in range(m + 1, POS):
            t = jnp.tanh(p[n] - p[m])
            prank[m] = prank[m] + 0.5 * (1.0 + t)
            prank[n] = prank[n] + 0.5 * (1.0 - t)
            pair = (0.25 / TAU) * (1.0 - t) * (1.0 + t) * (grad[n] - grad[m])
            pulled[m] = pulled[m] + pair
            pulled[n] = pulled[n] - pair
    for m in range(POS):
        weight = prank[m] / (rank[m] * rank[m]) * factor / TAU
        quarter, extra = 0.25 * weight, pulled[m] - weight * slope[m]
        for q in range(4):
            we[m : m + 1, cut(q)] = quarter[q : q + 1, :]
            we[POS + m : POS + m + 1, cut(q)] = extra[q : q + 1, :]

    exchange(we.at[:, group], jw.at[r], w_ss, w_rs, peer_r, LINE)
    jw[r] = we[:, group]

    for q in range(4):
        rows = [tgt[m : m + 1, cut(q)] for m in range(POS)]
        weights = [we[m : m + 1, cut(q)] for m in range(POS)]
        extras = [we[POS + m : POS + m + 1, cut(q)] for m in range(POS)]

        def tile_i(i, carry, q=q, rows=rows, weights=weights, extras=extras):
            k0 = pl.multiple_of(i * STEP, STEP)
            dense = weights[0] * vi[0, pl.ds(k0, STEP), cut(q)]
            for m in range(1, POS):
                dense = dense + weights[m] * vi[m, pl.ds(k0, STEP), cut(q)]
            extra = jnp.where(iota_k == rows[0] - k0, extras[0], 0.0)
            for m in range(1, POS):
                extra = jnp.where(iota_k == rows[m] - k0, extras[m], extra)
            dense = dense + extra
            gi[pl.ds(k0, STEP), cut(q)] = dense.astype(BF16)
            return carry

        lax.fori_loop(0, steps, tile_i, 0)

    over_rows = (((0,), (0,)), ((), ()))
    line_meet((gi,), a_buf[:, :, BOTH_AT:].reshape(BLOCK, EARLY), e_whole, e_other, e_sem)
    early_plane = c_buf[:, :, BOTH_AT:].reshape(BLOCK, EARLY)
    for h in range(2):
        rows = slice(256 * h, 256 * h + 256)
        product = lax.dot_general(gi[:, rows], early_plane, over_rows, preferred_element_type=F32)
        ep_part[8 * h : 8 * h + 8] = product.astype(BF16).reshape(8, SHARD, EARLY)

        @pl.when(c // 8 == h)
        def _(product=product):
            e_mine[...] = product.reshape(8, SHARD, EARLY)

    for o in PLANE:
        remote(ep_part.at[c ^ o], ep_landed.at[c], f_ss.at[o], f_rs.at[o], (r, c ^ o)).start()
    out[:, BOTH_AT:] = e_mine[c % 8]

    arrive(pt.at[:, group], jp, p_ss, p_rs, peer_r, r)
    columns(jp, 0)
    out[:, BOTH_AT:] += line_go(e_whole, e_other, ez_part, ez_landed, e_sem, e_ss, e_rs)

    def slopes(i, carry):
        k0 = pl.multiple_of(i * STEP, STEP)
        for m in range(POS):
            col = jc[m, pl.ds(k0, STEP), :]
            for q in range(4):
                t = jnp.tanh(s_ref[pl.ds(k0, STEP), cut(q)] - col)
                vj[m, pl.ds(k0, STEP), cut(q)] = 1.0 - t * t
            where = jc[POS + m, pl.ds(k0, STEP), :].astype(I32)
            jc[POS + m, pl.ds(k0, STEP), :] = jnp.where(
                where // BLOCK == r, where % BLOCK, -1
            ).astype(F32)
        return carry

    lax.fori_loop(0, steps, slopes, 0)

    arrive(we.at[:, group], jw, w_ss, w_rs, peer_r, r)
    columns(jw, 2 * POS)

    def tile_j(i, carry):
        for part_id in range(2):
            k0 = pl.ds(pl.multiple_of(i * 32 + part_id * 16, 16), 16)
            weights = [jc[2 * POS + m, k0, :] for m in range(POS)]
            extras = [jc[3 * POS + m, k0, :] for m in range(POS)]
            at = [jc[POS + m, k0, :] for m in range(POS)]
            for q in range(4):
                dense = weights[0] * vj[0, k0, cut(q)]
                for m in range(1, POS):
                    dense = dense + weights[m] * vj[m, k0, cut(q)]
                lane = (iota_a[0:16, :] + q * LANES).astype(F32)
                extra = jnp.where(at[0] == lane, extras[0], 0.0)
                for m in range(1, POS):
                    extra = jnp.where(at[m] == lane, extras[m], extra)
                dense = dense + extra
                gj[k0, cut(q)] = dense.astype(BF16)
        return carry

    lax.fori_loop(0, BLOCK // 32, tile_j, 0)

    line_meet((gi, gj), a_buf[:, :, LINE_AT:BOTH_AT].reshape(BLOCK, NARROW), z_whole, z_other, z_sem)

    left = c_buf[:, :, :BROAD].reshape(BLOCK, BROAD)
    wide = 2 * LANES
    for turn_id in range(2):
        h = (c // 8) ^ (1 - turn_id)
        half = pl.ds(pl.multiple_of(h * wide, wide), wide)
        product = lax.dot_general(gi[:, half], left, over_rows, preferred_element_type=F32)
        product = product + lax.dot_general(gj[:, half], left, over_rows, preferred_element_type=F32)
        part[pl.ds(h * 8, 8)] = product.astype(BF16).reshape(8, SHARD, BROAD)
        if turn_id == 1:
            mine[...] = product.reshape(8, SHARD, BROAD)

        for o in PLANE:
            if (o < 8) == (turn_id == 1):
                remote(part.at[c ^ o], landed.at[c], g_ss.at[o], g_rs.at[o], (r, c ^ o)).start()

    out[:, :BROAD] = mine[c % 8]
    out[:, LINE_AT:BOTH_AT] = line_go(z_whole, z_other, z_part, z_landed, z_sem, h_ss, h_rs)

    def plane_sum(part_ref, landed_ref, ss, rs, first, width):
        def add(o, carry):
            frm = c ^ o
            remote(part_ref.at[frm], landed_ref.at[frm], ss.at[o], rs.at[o], (r, frm)).wait_recv()
            out[:, first : first + width] += landed_ref[frm].astype(F32)
            return carry

        lax.fori_loop(1, 16, add, 0)

    def plane_sent(part_ref, landed_ref, ss, rs):
        def wait(o, carry):
            frm = c ^ o
            remote(part_ref.at[frm], landed_ref.at[frm], ss.at[o], rs.at[o], (r, frm)).wait_send()
            return carry

        lax.fori_loop(1, 16, wait, 0)

    line_sum(ez_landed, e_ss, e_rs, BOTH_AT, EARLY)
    plane_sum(ep_part, ep_landed, f_ss, f_rs, BOTH_AT, EARLY)
    line_sent(ez_part, ez_landed, e_ss, e_rs)
    plane_sent(ep_part, ep_landed, f_ss, f_rs)
    leave(x1s, x1r.at[c], x1_ss, x1_rs, peer_c)
    leave(x2s, x2r.at[c], x2_ss, x2_rs, peer_c)
    leave(pt.at[:, group], jp.at[r], p_ss, p_rs, peer_r)
    leave(we.at[:, group], jw.at[r], w_ss, w_rs, peer_r)
    for copy in sent:
        copy.wait_send()
    line_sum(z_landed, h_ss, h_rs, LINE_AT, NARROW)
    plane_sum(part, landed, g_ss, g_rs, 0, BROAD)
    line_sent(z_part, z_landed, h_ss, h_rs)
    plane_sent(part, landed, g_ss, g_rs)


def body(embed, positives, placement):
    dma = pltpu.SemaphoreType.DMA
    return pl.pallas_call(
        kernel,
        out_shape=pltpu.VMEM((SHARD, WIDTH), F32),
        in_specs=[pl.BlockSpec(memory_space=pl.ANY)] * 3,
        out_specs=pl.BlockSpec(memory_space=pltpu.VMEM),
        scratch_shapes=[
            pltpu.VMEM((COLS, SHARD, WIDTH), BF16),
            pltpu.VMEM((ROWS, SHARD, WIDTH), BF16),
            pltpu.VMEM((BLOCK, BLOCK), F32),
            pltpu.VMEM((POS, BLOCK, BLOCK), F32),
            pltpu.VMEM((POS, BLOCK, BLOCK), F32),
            pltpu.VMEM((BLOCK, BLOCK), BF16),
            pltpu.VMEM((BLOCK, BLOCK), BF16),
            pltpu.VMEM((COLS, SHARD, BROAD), BF16),
            pltpu.VMEM((COLS, SHARD, BROAD), BF16),
            pltpu.VMEM((8, SHARD, BROAD), F32),
            pltpu.VMEM((ZS, SHARD, NARROW), BF16),
            pltpu.VMEM((ZS, SHARD, NARROW), BF16),
            pltpu.VMEM((ZS, 2, SHARD, NARROW), F32),
            pltpu.VMEM((ZS, SHARD, NARROW), F32),
            pltpu.VMEM((ZS, SHARD, EARLY), BF16),
            pltpu.VMEM((ZS, SHARD, EARLY), BF16),
            pltpu.VMEM((ZS, 2, SHARD, EARLY), F32),
            pltpu.VMEM((ZS, SHARD, EARLY), F32),
            pltpu.VMEM((COLS, SHARD, EARLY), BF16),
            pltpu.VMEM((COLS, SHARD, EARLY), BF16),
            pltpu.VMEM((8, SHARD, EARLY), F32),
            pltpu.VMEM((POS, BLOCK), I32),
            pltpu.VMEM((64, LANES), I32),
            pltpu.VMEM((8, BLOCK), I32),
            pltpu.VMEM((8, BLOCK), F32),
            pltpu.VMEM((8, BLOCK), F32),
            pltpu.VMEM((16, LANES), F32),
            pltpu.VMEM((COLS, 16, LANES), F32),
            pltpu.VMEM((32, LANES), F32),
            pltpu.VMEM((COLS, 32, LANES), F32),
            pltpu.VMEM((ROWS, 8, LANES), F32),
            pltpu.VMEM((ROWS, 8, LANES), F32),
            pltpu.VMEM((LANES, LANES), F32),
            pltpu.VMEM((4 * POS, BLOCK, LANES), F32),
            dma((4,)),
            dma((2,)),
            dma((2,)),
            dma((32,)),
            dma((32,)),
        ]
        + [dma((16,))] * 20,
        compiler_params=pltpu.CompilerParams(
            collective_id=0, has_side_effects=True, vmem_limit_bytes=60 * 1024 * 1024
        ),
        cost_estimate=pl.CostEstimate(flops=1 << 31, bytes_accessed=1 << 22, transcendentals=1 << 21),
        name="smooth_ap",
    )(embed, positives.T, placement.reshape(64, LANES))


def solution(mesh):
    return jax.shard_map(
        body,
        mesh=mesh,
        in_specs=(P(("row", "col"), None), P("row", None), P()),
        out_specs=P(("row", "col"), None),
        check_vma=False,
    )
```

```python
import functools

import jax
import jax.numpy as jnp
from jax import lax
from jax.experimental import pallas as pl
from jax.experimental.pallas import tpu as pltpu
from jax.sharding import PartitionSpec as P

MESH = pl.DeviceIdType.MESH
TAU = 0.02
HALF = 0.5 / TAU
F32, BF16, I32 = jnp.float32, jnp.bfloat16, jnp.int32

ROWS, COLS, ZS = 16, 16, 8
SHARD, WIDTH, POS = 32, 1024, 4
BLOCK = SHARD * COLS
LANES = 128
STEP = 64

BROAD, NARROW, EARLY = 384, 256, 384
LINE_AT, BOTH_AT = BROAD, BROAD + NARROW

DEPTHS = (4, 3, 5, 2, 6, 1, 7)
PLANE = (10, 11, 14, 9, 6, 8, 2, 15, 13, 7, 5, 12, 4, 3, 1)
LINE = (8, 9, 10, 11, 6, 7, 14, 15, 12, 13, 4, 5, 2, 3, 1)


def remote(src, dst, send, recv, device):
    return pltpu.make_async_remote_copy(
        src_ref=src, dst_ref=dst, send_sem=send, recv_sem=recv,
        device_id=device, device_id_type=MESH,
    )


def kernel(
    embed, positives, placement, out,
    a_buf, c_buf, s_ref, vi, vj, gi, gj, part, landed, mine, z_part, z_landed, z_whole, z_other,
    ez_part, ez_landed, e_whole, e_other, ep_part, ep_landed, e_mine,
    pos_in, place_in, tgt, pt, we, x1s, x1r, x2s, x2r, jp, jw, jt, jc,
    in_sem, z_sem, e_sem, plane_s, plane_r, z_s, z_r, sib_s, sib_r,
    x1_ss, x1_rs, x2_ss, x2_rs, p_ss, p_rs, w_ss, w_rs, g_ss, g_rs, h_ss, h_rs,
    e_ss, e_rs, f_ss, f_rs,
):
    r, c = lax.axis_index("row"), lax.axis_index("col")
    z, core = r // 2, r % 2
    y, x = c // 4, c % 4

    def in_plane(o):
        return (r, ((y + o[0]) % 4) * 4 + (x + o[1]) % 4)

    def in_line(d, k=0):
        return (((z + d) % ZS) * 2 + (core + k) % 2, c)

    loads = [
        pltpu.make_async_copy(embed, a_buf.at[c], in_sem.at[0]),
        pltpu.make_async_copy(embed, c_buf.at[r], in_sem.at[1]),
        pltpu.make_async_copy(positives, pos_in, in_sem.at[2]),
        pltpu.make_async_copy(placement, place_in, in_sem.at[3]),
    ]
    barrier = pltpu.get_barrier_semaphore()

    near = [in_line(2), in_line(6), in_plane((0, 2)), in_plane((2, 0)), in_line(1), in_line(7)]
    near += [in_plane((0, 1)), in_plane((1, 0)), in_plane((0, 3)), in_plane((3, 0)), in_line(0, 1)]
    for peer in near:
        pl.semaphore_signal(barrier, inc=1, device_id=peer, device_id_type=MESH)
    for load in loads:
        load.start()
    for load in loads:
        load.wait()
    pl.semaphore_wait(barrier, len(near))

    sent = []

    def go(src, dst, ss, rs, device):
        copy = remote(src, dst, ss, rs, device)
        copy.start()
        sent.append(copy)

    def z_send(d, block, rows, step, slot):
        view = c_buf.at[block, rows]
        go(view, view, z_s.at[slot], z_r.at[slot], in_line(step % ZS))

    def z_wait(d, rows, slot):
        view = c_buf.at[from_z(d), rows]
        remote(view, view, z_s.at[slot], z_r.at[slot], in_line(d % ZS)).wait_recv()

    def from_z(d, k=0):
        return ((z + ZS - d) % ZS) * 2 + (core + k) % 2

    def from_plane(dy, dx):
        return ((y + 4 - dy) % 4) * 4 + (x + 4 - dx) % 4

    def a_send(block, rows, dy, dx, slot):
        view = a_buf.at[block, rows]
        go(view, view, plane_s.at[slot], plane_r.at[slot], in_plane((dy, dx)))

    def a_wait(dy, dx, rows, slot):
        view = a_buf.at[from_plane(dy, dx), rows]
        remote(view, view, plane_s.at[slot], plane_r.at[slot], in_plane((dy, dx))).wait_recv()

    def sib_send(d, rows, slot):
        view = c_buf.at[from_z(d), rows]
        go(view, view, sib_s.at[slot], sib_r.at[slot], in_line(0, 1))

    def sib_wait(d, rows, slot):
        view = c_buf.at[from_z(d, 1), rows]
        remote(view, view, sib_s.at[slot], sib_r.at[slot], in_line(0, 1)).wait_recv()

    every, top, low_half = pl.ds(0, SHARD), pl.ds(0, SHARD // 2), pl.ds(SHARD // 2, SHARD // 2)
    halves = (top, low_half)

    def x_first(d, h):
        a_send(c, halves[h], 0, d, 4 * d - 4 + h)

    def y_first(d, h):
        a_send(c, halves[h], d, 0, 4 * d - 2 + h)

    for d in (2, 1, 3):
        x_first(d, 0)
        y_first(d, 1)
    z_send(2, r, top, 2, 0)
    z_send(-2, r, low_half, -2, 1)
    z_send(2, r, low_half, 2, 2)
    z_send(-2, r, top, -2, 3)
    z_send(1, r, every, 1, 4)
    z_send(-1, r, every, -1, 5)
    for d in (2, 1, 3):
        x_first(d, 1)
        y_first(d, 0)
    sib_send(0, every, 0)

    table = place_in[...]
    high = (table // 64).astype(F32).astype(BF16)
    low = (table % 64).astype(F32).astype(BF16)
    lane_id = lax.broadcasted_iota(I32, (LANES, BLOCK), 0)
    row_id = lax.broadcasted_iota(I32, (64, BLOCK), 0)
    for m in range(POS):
        entity = pos_in[m : m + 1, :]
        hot = jnp.where(lane_id == entity % LANES, 1.0, 0.0).astype(BF16)
        value = jnp.dot(high, hot, preferred_element_type=F32) * 64.0 + jnp.dot(
            low, hot, preferred_element_type=F32
        )
        found = jnp.sum(jnp.where(row_id == entity // LANES, value, 0.0), axis=0, keepdims=True)
        pt[POS + m : POS + m + 1, :] = found
        where = found.astype(I32)
        here = (where // SHARD) % COLS == c
        tgt[m : m + 1, :] = jnp.where(here, (where // BLOCK) * SHARD + where % SHARD, -1)

    def turn(d):
        a_wait(0, d, top, 4 * d - 4)
        for e in (2, 1, 3):
            a_send(from_plane(0, d), top, e, 0, 12 + 3 * (d - 1) + e - 1)
        a_wait(d, 0, low_half, 4 * d - 1)
        for e in (2, 1, 3):
            a_send(from_plane(d, 0), low_half, 0, e, 21 + 3 * (d - 1) + e - 1)

    turn(1)
    turn(3)
    z_wait(2, top, 0)
    z_send(4, from_z(2), top, 2, 6)
    z_send(3, from_z(2), top, 1, 7)
    z_wait(-2, low_half, 1)
    z_send(-4, from_z(-2), low_half, -2, 8)
    z_send(-3, from_z(-2), low_half, -1, 9)
    z_wait(2, low_half, 2)
    z_send(3, from_z(2), low_half, 1, 10)
    z_wait(-2, top, 3)
    z_send(-3, from_z(-2), top, -1, 11)
    turn(2)
    for d, slot in ((2, 2), (-2, 6)):
        sib_send(d, every, slot)
    for d, slot in ((1, 4), (-1, 5)):
        z_wait(d, every, slot)
        sib_send(d, every, 1 if d == 1 else 7)
    z_wait(4, top, 6)
    sib_send(4, top, 4)
    z_wait(-4, low_half, 8)
    sib_send(-4, low_half, 8)
    z_wait(3, top, 7)
    z_wait(3, low_half, 10)
    sib_send(3, every, 3)
    z_wait(-3, low_half, 9)
    z_wait(-3, top, 11)
    sib_send(-3, every, 5)
    for d in (1, 3, 2):
        a_wait(0, d, low_half, 4 * d - 3)
        a_wait(d, 0, top, 4 * d - 2)
    for d in (1, 3, 2):
        for e in (1, 3, 2):
            a_wait(e, d, top, 12 + 3 * (d - 1) + e - 1)
            a_wait(d, e, low_half, 21 + 3 * (d - 1) + e - 1)
    anchors = a_buf[...].reshape(BLOCK, WIDTH)
    iota_k = lax.broadcasted_iota(I32, (STEP, LANES), 0)
    iota_a = lax.broadcasted_iota(I32, (STEP, LANES), 1)
    steps = BLOCK // STEP

    def fold(value):
        return jnp.sum(value.reshape(STEP // 8, 8, LANES), axis=0)

    def cut(q):
        return slice(q * LANES, (q + 1) * LANES)

    def score(first, last):
        chips = [(z + i) % ZS for i in range(first, last)]
        cand = jnp.concatenate([c_buf[pl.ds(2 * chip, 2)].reshape(STEP, WIDTH) for chip in chips], axis=0)
        product = HALF * lax.dot_general(
            cand, anchors, (((1,), (1,)), ((), ())), preferred_element_type=F32
        )
        for i, chip in enumerate(chips):
            s_ref[pl.ds(pl.multiple_of(chip * STEP, STEP), STEP), :] = product[i * STEP : (i + 1) * STEP]

    def pick(first, last, sums):
        new = []
        for q in range(4):
            rows = [tgt[m : m + 1, cut(q)] for m in range(POS)]

            def step(i, acc, q=q, rows=rows):
                k0 = pl.multiple_of(((z + i) % ZS) * STEP, STEP)
                tile = s_ref[pl.ds(k0, STEP), cut(q)]
                return tuple(
                    acc[m] + fold(jnp.where(iota_k == rows[m] - k0, tile, 0.0)) for m in range(POS)
                )

            new.append(lax.fori_loop(first, last, step, sums[q]))
        return new

    for d, slot in ((0, 0), (1, 1), (-1, 7), (2, 2), (-2, 6)):
        sib_wait(d, every, slot)
    score(6, 11)
    own_rows = pl.ds(pl.multiple_of(r * SHARD, SHARD), SHARD)
    own_lanes = pl.ds(pl.multiple_of(y * LANES, LANES), LANES)
    me_row = lax.broadcasted_iota(I32, (SHARD, LANES), 0)
    me_lane = lax.broadcasted_iota(I32, (SHARD, LANES), 1)
    s_ref[own_rows, own_lanes] = jnp.where(me_lane - x * SHARD == me_row, -1e30, s_ref[own_rows, own_lanes])
    sums = pick(6, 11, [(jnp.zeros((8, LANES), F32),) * POS] * 4)
    for d, slot in ((3, 3), (-3, 5)):
        sib_wait(d, every, slot)
    sib_wait(4, top, 4)
    sib_wait(-4, low_half, 8)
    score(3, 6)
    sums = pick(3, 6, sums)
    for q in range(4):
        for m in range(POS):
            x1s[m * POS + q : m * POS + q + 1, :] = jnp.sum(sums[q][m], axis=0, keepdims=True)

    def exchange(src, dst, ss, rs, peer, order):
        for o in order:
            remote(src, dst, ss.at[o], rs.at[o], peer(o)).start()

    def arrive(src, dst, ss, rs, peer, index):
        def wait(o, carry):
            remote(src, dst.at[index ^ o], ss.at[o], rs.at[o], peer(o)).wait_recv()
            return carry

        lax.fori_loop(1, 16, wait, 0)

    def leave(src, dst, ss, rs, peer):
        def wait(o, carry):
            remote(src, dst, ss.at[o], rs.at[o], peer(o)).wait_send()
            return carry

        lax.fori_loop(1, 16, wait, 0)

    def peer_c(o):
        return (r, c ^ o)

    def peer_r(o):
        return (r ^ o, c)

    exchange(x1s, x1r.at[c], x1_ss, x1_rs, peer_c, PLANE)
    x1r[c] = x1s[...]
    arrive(x1s, x1r, x1_ss, x1_rs, peer_c, c)
    scores = jnp.sum(x1r[...], axis=0)
    for m in range(POS):
        for q in range(4):
            pt[m : m + 1, cut(q)] = scores[m * POS + q : m * POS + q + 1, :]

    group = pl.ds(pl.multiple_of(y * LANES, LANES), LANES)
    def line_meet(tiles, columns, whole, other, sem):
        for h in range(2):
            rows = slice(256 * h, 256 * h + 256)
            product = sum(jnp.dot(g[rows, :], columns, preferred_element_type=F32) for g in tiles)
            whole[4 * h : 4 * h + 4] = product.reshape(4, 2, SHARD, product.shape[1])
        remote(whole.at[:, 1 - core], other, sem.at[0], sem.at[1], (r ^ 1, c)).start()

    def line_go(whole, other, part_ref, landed_ref, sem, ss, rs):
        meet = remote(whole.at[:, 1 - core], other, sem.at[0], sem.at[1], (r ^ 1, c))
        meet.wait_recv()
        part_ref[...] = (whole[:, core] + other[...]).astype(BF16)
        for d in DEPTHS:
            to = (z + d) % ZS
            remote(part_ref.at[to], landed_ref.at[z], ss.at[d], rs.at[d], in_line(d)).start()
        meet.wait_send()
        return whole[z, core] + other[z]

    def line_sum(landed_ref, ss, rs, first, width):
        for d in reversed(DEPTHS):
            frm = (z + ZS - d) % ZS
            remote(landed_ref.at[frm], landed_ref.at[frm], ss.at[d], rs.at[d], in_line(d)).wait_recv()
            out[:, first : first + width] += landed_ref[frm].astype(F32)

    def line_sent(part_ref, landed_ref, ss, rs):
        for d in DEPTHS:
            to = (z + d) % ZS
            remote(part_ref.at[to], landed_ref.at[z], ss.at[d], rs.at[d], in_line(d)).wait_send()

    for q in range(4):
        rows = [pt[m : m + 1, cut(q)] for m in range(POS)]

        def count(i, acc, q=q, rows=rows):
            k0 = pl.multiple_of(i * STEP, STEP)
            score = s_ref[pl.ds(k0, STEP), cut(q)]
            new = []
            for m in range(POS):
                t = jnp.tanh(score - rows[m])
                u = 1.0 + t
                v = 1.0 - t * t
                vi[m, pl.ds(k0, STEP), cut(q)] = v
                new.append(acc[2 * m] + fold(u))
                new.append(acc[2 * m + 1] + fold(v))
            return tuple(new)

        acc = lax.fori_loop(0, steps, count, (jnp.zeros((8, LANES), F32),) * (2 * POS))
        for m in range(POS):
            at = m * POS + q
            x2s[at : at + 1, :] = jnp.sum(acc[2 * m], axis=0, keepdims=True)
            x2s[16 + at : 17 + at, :] = jnp.sum(acc[2 * m + 1], axis=0, keepdims=True)
    exchange(x2s, x2r.at[c], x2_ss, x2_rs, peer_c, PLANE)
    x2r[c] = x2s[...]
    exchange(pt.at[:, group], jp.at[r], p_ss, p_rs, peer_r, LINE)
    jp[r] = pt[:, group]

    def columns(src, first):
        jt[...] = jnp.transpose(src[...].reshape(ROWS * 8, LANES))
        mine_cols = jt[pl.ds(pl.multiple_of(x * SHARD, SHARD), SHARD), :]
        for b in range(ROWS):
            for n in range(8):
                jc[first + n, b * SHARD : (b + 1) * SHARD, :] = jnp.broadcast_to(
                    mine_cols[:, b * 8 + n : b * 8 + n + 1], (SHARD, LANES)
                )

    arrive(x2s, x2r, x2_ss, x2_rs, peer_c, c)
    total = jnp.sum(x2r[...], axis=0)
    factor = 1.0 / (POS * SHARD * ROWS * COLS)

    def of(value, m):
        return value[m * POS : (m + 1) * POS]

    p = [of(scores, m) for m in range(POS)]
    rank = [0.5 + 0.5 * of(total[0:16], m) for m in range(POS)]
    slope = [0.25 * of(total[16:32], m) for m in range(POS)]
    prank = [jnp.full((POS, LANES), 1.0, F32) for _ in range(POS)]
    grad = [-factor / rank[m] for m in range(POS)]
    pulled = [jnp.zeros((POS, LANES), F32) for _ in range(POS)]
    for m in range(POS):
        for n in range(m + 1, POS):
            t = jnp.tanh(p[n] - p[m])
            prank[m] = prank[m] + 0.5 * (1.0 + t)
            prank[n] = prank[n] + 0.5 * (1.0 - t)
            pair = (0.25 / TAU) * (1.0 - t) * (1.0 + t) * (grad[n] - grad[m])
            pulled[m] = pulled[m] + pair
            pulled[n] = pulled[n] - pair
    for m in range(POS):
        weight = prank[m] / (rank[m] * rank[m]) * factor / TAU
        quarter, extra = 0.25 * weight, pulled[m] - weight * slope[m]
        for q in range(4):
            we[m : m + 1, cut(q)] = quarter[q : q + 1, :]
            we[POS + m : POS + m + 1, cut(q)] = extra[q : q + 1, :]

    exchange(we.at[:, group], jw.at[r], w_ss, w_rs, peer_r, LINE)
    jw[r] = we[:, group]

    for q in range(4):
        rows = [tgt[m : m + 1, cut(q)] for m in range(POS)]
        weights = [we[m : m + 1, cut(q)] for m in range(POS)]
        extras = [we[POS + m : POS + m + 1, cut(q)] for m in range(POS)]

        def tile_i(i, carry, q=q, rows=rows, weights=weights, extras=extras):
            k0 = pl.multiple_of(i * STEP, STEP)
            dense = weights[0] * vi[0, pl.ds(k0, STEP), cut(q)]
            for m in range(1, POS):
                dense = dense + weights[m] * vi[m, pl.ds(k0, STEP), cut(q)]
            extra = jnp.where(iota_k == rows[0] - k0, extras[0], 0.0)
            for m in range(1, POS):
                extra = jnp.where(iota_k == rows[m] - k0, extras[m], extra)
            dense = dense + extra
            gi[pl.ds(k0, STEP), cut(q)] = dense.astype(BF16)
            return carry

        lax.fori_loop(0, steps, tile_i, 0)

    over_rows = (((0,), (0,)), ((), ()))
    line_meet((gi,), a_buf[:, :, BOTH_AT:].reshape(BLOCK, EARLY), e_whole, e_other, e_sem)
    early_plane = c_buf[:, :, BOTH_AT:].reshape(BLOCK, EARLY)
    for h in range(2):
        rows = slice(256 * h, 256 * h + 256)
        product = lax.dot_general(gi[:, rows], early_plane, over_rows, preferred_element_type=F32)
        ep_part[8 * h : 8 * h + 8] = product.astype(BF16).reshape(8, SHARD, EARLY)

        @pl.when(c // 8 == h)
        def _(product=product):
            e_mine[...] = product.reshape(8, SHARD, EARLY)

    for o in PLANE:
        remote(ep_part.at[c ^ o], ep_landed.at[c], f_ss.at[o], f_rs.at[o], (r, c ^ o)).start()
    out[:, BOTH_AT:] = e_mine[c % 8]

    arrive(pt.at[:, group], jp, p_ss, p_rs, peer_r, r)
    columns(jp, 0)
    out[:, BOTH_AT:] += line_go(e_whole, e_other, ez_part, ez_landed, e_sem, e_ss, e_rs)

    def slopes(i, carry):
        k0 = pl.multiple_of(i * STEP, STEP)
        for m in range(POS):
            col = jc[m, pl.ds(k0, STEP), :]
            for q in range(4):
                t = jnp.tanh(s_ref[pl.ds(k0, STEP), cut(q)] - col)
                vj[m, pl.ds(k0, STEP), cut(q)] = 1.0 - t * t
            where = jc[POS + m, pl.ds(k0, STEP), :].astype(I32)
            jc[POS + m, pl.ds(k0, STEP), :] = jnp.where(
                where // BLOCK == r, where % BLOCK, -1
            ).astype(F32)
        return carry

    lax.fori_loop(0, steps, slopes, 0)

    arrive(we.at[:, group], jw, w_ss, w_rs, peer_r, r)
    columns(jw, 2 * POS)

    def tile_j(i, carry):
        for part_id in range(2):
            k0 = pl.ds(pl.multiple_of(i * 32 + part_id * 16, 16), 16)
            weights = [jc[2 * POS + m, k0, :] for m in range(POS)]
            extras = [jc[3 * POS + m, k0, :] for m in range(POS)]
            at = [jc[POS + m, k0, :] for m in range(POS)]
            for q in range(4):
                dense = weights[0] * vj[0, k0, cut(q)]
                for m in range(1, POS):
                    dense = dense + weights[m] * vj[m, k0, cut(q)]
                lane = (iota_a[0:16, :] + q * LANES).astype(F32)
                extra = jnp.where(at[0] == lane, extras[0], 0.0)
                for m in range(1, POS):
                    extra = jnp.where(at[m] == lane, extras[m], extra)
                dense = dense + extra
                gj[k0, cut(q)] = dense.astype(BF16)
        return carry

    lax.fori_loop(0, BLOCK // 32, tile_j, 0)

    line_meet((gi, gj), a_buf[:, :, LINE_AT:BOTH_AT].reshape(BLOCK, NARROW), z_whole, z_other, z_sem)

    left = c_buf[:, :, :BROAD].reshape(BLOCK, BROAD)
    wide = 2 * LANES
    for turn_id in range(2):
        h = (c // 8) ^ (1 - turn_id)
        half = pl.ds(pl.multiple_of(h * wide, wide), wide)
        product = lax.dot_general(gi[:, half], left, over_rows, preferred_element_type=F32)
        product = product + lax.dot_general(gj[:, half], left, over_rows, preferred_element_type=F32)
        part[pl.ds(h * 8, 8)] = product.astype(BF16).reshape(8, SHARD, BROAD)
        if turn_id == 1:
            mine[...] = product.reshape(8, SHARD, BROAD)

        for o in PLANE:
            if (o < 8) == (turn_id == 1):
                remote(part.at[c ^ o], landed.at[c], g_ss.at[o], g_rs.at[o], (r, c ^ o)).start()

    out[:, :BROAD] = mine[c % 8]
    out[:, LINE_AT:BOTH_AT] = line_go(z_whole, z_other, z_part, z_landed, z_sem, h_ss, h_rs)

    def plane_sum(part_ref, landed_ref, ss, rs, first, width):
        def add(o, carry):
            frm = c ^ o
            remote(part_ref.at[frm], landed_ref.at[frm], ss.at[o], rs.at[o], (r, frm)).wait_recv()
            out[:, first : first + width] += landed_ref[frm].astype(F32)
            return carry

        lax.fori_loop(1, 16, add, 0)

    def plane_sent(part_ref, landed_ref, ss, rs):
        def wait(o, carry):
            frm = c ^ o
            remote(part_ref.at[frm], landed_ref.at[frm], ss.at[o], rs.at[o], (r, frm)).wait_send()
            return carry

        lax.fori_loop(1, 16, wait, 0)

    line_sum(ez_landed, e_ss, e_rs, BOTH_AT, EARLY)
    plane_sum(ep_part, ep_landed, f_ss, f_rs, BOTH_AT, EARLY)
    line_sent(ez_part, ez_landed, e_ss, e_rs)
    plane_sent(ep_part, ep_landed, f_ss, f_rs)
    leave(x1s, x1r.at[c], x1_ss, x1_rs, peer_c)
    leave(x2s, x2r.at[c], x2_ss, x2_rs, peer_c)
    leave(pt.at[:, group], jp.at[r], p_ss, p_rs, peer_r)
    leave(we.at[:, group], jw.at[r], w_ss, w_rs, peer_r)
    for copy in sent:
        copy.wait_send()
    line_sum(z_landed, h_ss, h_rs, LINE_AT, NARROW)
    plane_sum(part, landed, g_ss, g_rs, 0, BROAD)
    line_sent(z_part, z_landed, h_ss, h_rs)
    plane_sent(part, landed, g_ss, g_rs)


def body(embed, positives, placement):
    dma = pltpu.SemaphoreType.DMA
    return pl.pallas_call(
        kernel,
        out_shape=pltpu.VMEM((SHARD, WIDTH), F32),
        in_specs=[pl.BlockSpec(memory_space=pl.ANY)] * 3,
        out_specs=pl.BlockSpec(memory_space=pltpu.VMEM),
        scratch_shapes=[
            pltpu.VMEM((COLS, SHARD, WIDTH), BF16),
            pltpu.VMEM((ROWS, SHARD, WIDTH), BF16),
            pltpu.VMEM((BLOCK, BLOCK), F32),
            pltpu.VMEM((POS, BLOCK, BLOCK), F32),
            pltpu.VMEM((POS, BLOCK, BLOCK), F32),
            pltpu.VMEM((BLOCK, BLOCK), BF16),
            pltpu.VMEM((BLOCK, BLOCK), BF16),
            pltpu.VMEM((COLS, SHARD, BROAD), BF16),
            pltpu.VMEM((COLS, SHARD, BROAD), BF16),
            pltpu.VMEM((8, SHARD, BROAD), F32),
            pltpu.VMEM((ZS, SHARD, NARROW), BF16),
            pltpu.VMEM((ZS, SHARD, NARROW), BF16),
            pltpu.VMEM((ZS, 2, SHARD, NARROW), F32),
            pltpu.VMEM((ZS, SHARD, NARROW), F32),
            pltpu.VMEM((ZS, SHARD, EARLY), BF16),
            pltpu.VMEM((ZS, SHARD, EARLY), BF16),
            pltpu.VMEM((ZS, 2, SHARD, EARLY), F32),
            pltpu.VMEM((ZS, SHARD, EARLY), F32),
            pltpu.VMEM((COLS, SHARD, EARLY), BF16),
            pltpu.VMEM((COLS, SHARD, EARLY), BF16),
            pltpu.VMEM((8, SHARD, EARLY), F32),
            pltpu.VMEM((POS, BLOCK), I32),
            pltpu.VMEM((64, LANES), I32),
            pltpu.VMEM((8, BLOCK), I32),
            pltpu.VMEM((8, BLOCK), F32),
            pltpu.VMEM((8, BLOCK), F32),
            pltpu.VMEM((16, LANES), F32),
            pltpu.VMEM((COLS, 16, LANES), F32),
            pltpu.VMEM((32, LANES), F32),
            pltpu.VMEM((COLS, 32, LANES), F32),
            pltpu.VMEM((ROWS, 8, LANES), F32),
            pltpu.VMEM((ROWS, 8, LANES), F32),
            pltpu.VMEM((LANES, LANES), F32),
            pltpu.VMEM((4 * POS, BLOCK, LANES), F32),
            dma((4,)),
            dma((2,)),
            dma((2,)),
            dma((32,)),
            dma((32,)),
        ]
        + [dma((16,))] * 20,
        compiler_params=pltpu.CompilerParams(
            collective_id=0, has_side_effects=True, vmem_limit_bytes=60 * 1024 * 1024
        ),
        cost_estimate=pl.CostEstimate(flops=1 << 31, bytes_accessed=1 << 22, transcendentals=1 << 21),
        name="smooth_ap",
    )(embed, positives.T, placement.reshape(64, LANES))


def solution(mesh):
    return jax.shard_map(
        body,
        mesh=mesh,
        in_specs=(P(("row", "col"), None), P("row", None), P()),
        out_specs=P(("row", "col"), None),
        check_vma=False,
    )
```

```python
import functools

import jax
import jax.numpy as jnp
from jax import lax
from jax.experimental import pallas as pl
from jax.experimental.pallas import tpu as pltpu
from jax.sharding import PartitionSpec as P

MESH = pl.DeviceIdType.MESH
TAU = 0.02
HALF = 0.5 / TAU
F32, BF16, I32 = jnp.float32, jnp.bfloat16, jnp.int32

ROWS, COLS, ZS = 16, 16, 8
SHARD, WIDTH, POS = 32, 1024, 4
BLOCK = SHARD * COLS
LANES = 128
STEP = 64

BROAD, NARROW, EARLY = 256, 256, 512
LINE_AT, BOTH_AT = BROAD, BROAD + NARROW

DEPTHS = (4, 3, 5, 2, 6, 1, 7)
PLANE = (10, 11, 14, 9, 6, 8, 2, 15, 13, 7, 5, 12, 4, 3, 1)
LINE = (8, 9, 10, 11, 6, 7, 14, 15, 12, 13, 4, 5, 2, 3, 1)


def remote(src, dst, send, recv, device):
    return pltpu.make_async_remote_copy(
        src_ref=src, dst_ref=dst, send_sem=send, recv_sem=recv,
        device_id=device, device_id_type=MESH,
    )


def kernel(
    embed, positives, placement, out,
    a_buf, c_buf, s_ref, vi, vj, gi, gj, part, landed, mine, z_part, z_landed, z_whole, z_other,
    ez_part, ez_landed, e_whole, e_other, ep_part, ep_landed, e_mine,
    pos_in, place_in, tgt, pt, we, x1s, x1r, x2s, x2r, jp, jw, jt, jc,
    in_sem, z_sem, e_sem, plane_s, plane_r, z_s, z_r, sib_s, sib_r,
    x1_ss, x1_rs, x2_ss, x2_rs, p_ss, p_rs, w_ss, w_rs, g_ss, g_rs, h_ss, h_rs,
    e_ss, e_rs, f_ss, f_rs,
):
    r, c = lax.axis_index("row"), lax.axis_index("col")
    z, core = r // 2, r % 2
    y, x = c // 4, c % 4

    def in_plane(o):
        return (r, ((y + o[0]) % 4) * 4 + (x + o[1]) % 4)

    def in_line(d, k=0):
        return (((z + d) % ZS) * 2 + (core + k) % 2, c)

    loads = [
        pltpu.make_async_copy(embed, a_buf.at[c], in_sem.at[0]),
        pltpu.make_async_copy(embed, c_buf.at[r], in_sem.at[1]),
        pltpu.make_async_copy(positives, pos_in, in_sem.at[2]),
        pltpu.make_async_copy(placement, place_in, in_sem.at[3]),
    ]
    barrier = pltpu.get_barrier_semaphore()

    near = [in_line(2), in_line(6), in_plane((0, 2)), in_plane((2, 0)), in_line(1), in_line(7)]
    near += [in_plane((0, 1)), in_plane((1, 0)), in_plane((0, 3)), in_plane((3, 0)), in_line(0, 1)]
    for peer in near:
        pl.semaphore_signal(barrier, inc=1, device_id=peer, device_id_type=MESH)
    for load in loads:
        load.start()
    for load in loads:
        load.wait()
    pl.semaphore_wait(barrier, len(near))

    sent = []

    def go(src, dst, ss, rs, device):
        copy = remote(src, dst, ss, rs, device)
        copy.start()
        sent.append(copy)

    def z_send(d, block, rows, step, slot):
        view = c_buf.at[block, rows]
        go(view, view, z_s.at[slot], z_r.at[slot], in_line(step % ZS))

    def z_wait(d, rows, slot):
        view = c_buf.at[from_z(d), rows]
        remote(view, view, z_s.at[slot], z_r.at[slot], in_line(d % ZS)).wait_recv()

    def from_z(d, k=0):
        return ((z + ZS - d) % ZS) * 2 + (core + k) % 2

    def from_plane(dy, dx):
        return ((y + 4 - dy) % 4) * 4 + (x + 4 - dx) % 4

    def a_send(block, rows, dy, dx, slot):
        view = a_buf.at[block, rows]
        go(view, view, plane_s.at[slot], plane_r.at[slot], in_plane((dy, dx)))

    def a_wait(dy, dx, rows, slot):
        view = a_buf.at[from_plane(dy, dx), rows]
        remote(view, view, plane_s.at[slot], plane_r.at[slot], in_plane((dy, dx))).wait_recv()

    def sib_send(d, rows, slot):
        view = c_buf.at[from_z(d), rows]
        go(view, view, sib_s.at[slot], sib_r.at[slot], in_line(0, 1))

    def sib_wait(d, rows, slot):
        view = c_buf.at[from_z(d, 1), rows]
        remote(view, view, sib_s.at[slot], sib_r.at[slot], in_line(0, 1)).wait_recv()

    every, top, low_half = pl.ds(0, SHARD), pl.ds(0, SHARD // 2), pl.ds(SHARD // 2, SHARD // 2)
    halves = (top, low_half)

    def x_first(d, h):
        a_send(c, halves[h], 0, d, 4 * d - 4 + h)

    def y_first(d, h):
        a_send(c, halves[h], d, 0, 4 * d - 2 + h)

    for d in (2, 1, 3):
        x_first(d, 0)
        y_first(d, 1)
    z_send(2, r, top, 2, 0)
    z_send(-2, r, low_half, -2, 1)
    z_send(2, r, low_half, 2, 2)
    z_send(-2, r, top, -2, 3)
    z_send(1, r, every, 1, 4)
    z_send(-1, r, every, -1, 5)
    for d in (2, 1, 3):
        x_first(d, 1)
        y_first(d, 0)
    sib_send(0, every, 0)

    table = place_in[...]
    high = (table // 64).astype(F32).astype(BF16)
    low = (table % 64).astype(F32).astype(BF16)
    lane_id = lax.broadcasted_iota(I32, (LANES, BLOCK), 0)
    row_id = lax.broadcasted_iota(I32, (64, BLOCK), 0)
    for m in range(POS):
        entity = pos_in[m : m + 1, :]
        hot = jnp.where(lane_id == entity % LANES, 1.0, 0.0).astype(BF16)
        value = jnp.dot(high, hot, preferred_element_type=F32) * 64.0 + jnp.dot(
            low, hot, preferred_element_type=F32
        )
        found = jnp.sum(jnp.where(row_id == entity // LANES, value, 0.0), axis=0, keepdims=True)
        pt[POS + m : POS + m + 1, :] = found
        where = found.astype(I32)
        here = (where // SHARD) % COLS == c
        tgt[m : m + 1, :] = jnp.where(here, (where // BLOCK) * SHARD + where % SHARD, -1)

    def turn(d):
        a_wait(0, d, top, 4 * d - 4)
        for e in (2, 1, 3):
            a_send(from_plane(0, d), top, e, 0, 12 + 3 * (d - 1) + e - 1)
        a_wait(d, 0, low_half, 4 * d - 1)
        for e in (2, 1, 3):
            a_send(from_plane(d, 0), low_half, 0, e, 21 + 3 * (d - 1) + e - 1)

    turn(1)
    turn(3)
    z_wait(2, top, 0)
    z_send(4, from_z(2), top, 2, 6)
    z_send(3, from_z(2), top, 1, 7)
    z_wait(-2, low_half, 1)
    z_send(-4, from_z(-2), low_half, -2, 8)
    z_send(-3, from_z(-2), low_half, -1, 9)
    z_wait(2, low_half, 2)
    z_send(3, from_z(2), low_half, 1, 10)
    z_wait(-2, top, 3)
    z_send(-3, from_z(-2), top, -1, 11)
    turn(2)
    for d, slot in ((2, 2), (-2, 6)):
        sib_send(d, every, slot)
    for d, slot in ((1, 4), (-1, 5)):
        z_wait(d, every, slot)
        sib_send(d, every, 1 if d == 1 else 7)
    z_wait(4, top, 6)
    sib_send(4, top, 4)
    z_wait(-4, low_half, 8)
    sib_send(-4, low_half, 8)
    z_wait(3, top, 7)
    z_wait(3, low_half, 10)
    sib_send(3, every, 3)
    z_wait(-3, low_half, 9)
    z_wait(-3, top, 11)
    sib_send(-3, every, 5)
    for d in (1, 3, 2):
        a_wait(0, d, low_half, 4 * d - 3)
        a_wait(d, 0, top, 4 * d - 2)
    for d in (1, 3, 2):
        for e in (1, 3, 2):
            a_wait(e, d, top, 12 + 3 * (d - 1) + e - 1)
            a_wait(d, e, low_half, 21 + 3 * (d - 1) + e - 1)
    anchors = a_buf[...].reshape(BLOCK, WIDTH)
    iota_k = lax.broadcasted_iota(I32, (STEP, LANES), 0)
    iota_a = lax.broadcasted_iota(I32, (STEP, LANES), 1)
    steps = BLOCK // STEP

    def fold(value):
        return jnp.sum(value.reshape(STEP // 8, 8, LANES), axis=0)

    def cut(q):
        return slice(q * LANES, (q + 1) * LANES)

    def score(first, last):
        chips = [(z + i) % ZS for i in range(first, last)]
        cand = jnp.concatenate([c_buf[pl.ds(2 * chip, 2)].reshape(STEP, WIDTH) for chip in chips], axis=0)
        product = HALF * lax.dot_general(
            cand, anchors, (((1,), (1,)), ((), ())), preferred_element_type=F32
        )
        for i, chip in enumerate(chips):
            s_ref[pl.ds(pl.multiple_of(chip * STEP, STEP), STEP), :] = product[i * STEP : (i + 1) * STEP]

    def pick(first, last, sums):
        new = []
        for q in range(4):
            rows = [tgt[m : m + 1, cut(q)] for m in range(POS)]

            def step(i, acc, q=q, rows=rows):
                k0 = pl.multiple_of(((z + i) % ZS) * STEP, STEP)
                tile = s_ref[pl.ds(k0, STEP), cut(q)]
                return tuple(
                    acc[m] + fold(jnp.where(iota_k == rows[m] - k0, tile, 0.0)) for m in range(POS)
                )

            new.append(lax.fori_loop(first, last, step, sums[q]))
        return new

    for d, slot in ((0, 0), (1, 1), (-1, 7), (2, 2), (-2, 6)):
        sib_wait(d, every, slot)
    score(6, 11)
    own_rows = pl.ds(pl.multiple_of(r * SHARD, SHARD), SHARD)
    own_lanes = pl.ds(pl.multiple_of(y * LANES, LANES), LANES)
    me_row = lax.broadcasted_iota(I32, (SHARD, LANES), 0)
    me_lane = lax.broadcasted_iota(I32, (SHARD, LANES), 1)
    s_ref[own_rows, own_lanes] = jnp.where(me_lane - x * SHARD == me_row, -1e30, s_ref[own_rows, own_lanes])
    sums = pick(6, 11, [(jnp.zeros((8, LANES), F32),) * POS] * 4)
    for d, slot in ((3, 3), (-3, 5)):
        sib_wait(d, every, slot)
    sib_wait(4, top, 4)
    sib_wait(-4, low_half, 8)
    score(3, 6)
    sums = pick(3, 6, sums)
    for q in range(4):
        for m in range(POS):
            x1s[m * POS + q : m * POS + q + 1, :] = jnp.sum(sums[q][m], axis=0, keepdims=True)

    def exchange(src, dst, ss, rs, peer, order):
        for o in order:
            remote(src, dst, ss.at[o], rs.at[o], peer(o)).start()

    def arrive(src, dst, ss, rs, peer, index):
        def wait(o, carry):
            remote(src, dst.at[index ^ o], ss.at[o], rs.at[o], peer(o)).wait_recv()
            return carry

        lax.fori_loop(1, 16, wait, 0)

    def leave(src, dst, ss, rs, peer):
        def wait(o, carry):
            remote(src, dst, ss.at[o], rs.at[o], peer(o)).wait_send()
            return carry

        lax.fori_loop(1, 16, wait, 0)

    def peer_c(o):
        return (r, c ^ o)

    def peer_r(o):
        return (r ^ o, c)

    exchange(x1s, x1r.at[c], x1_ss, x1_rs, peer_c, PLANE)
    x1r[c] = x1s[...]
    arrive(x1s, x1r, x1_ss, x1_rs, peer_c, c)
    scores = jnp.sum(x1r[...], axis=0)
    for m in range(POS):
        for q in range(4):
            pt[m : m + 1, cut(q)] = scores[m * POS + q : m * POS + q + 1, :]

    group = pl.ds(pl.multiple_of(y * LANES, LANES), LANES)
    def line_meet(tiles, columns, whole, other, sem):
        for h in range(2):
            rows = slice(256 * h, 256 * h + 256)
            product = sum(jnp.dot(g[rows, :], columns, preferred_element_type=F32) for g in tiles)
            whole[4 * h : 4 * h + 4] = product.reshape(4, 2, SHARD, product.shape[1])
        remote(whole.at[:, 1 - core], other, sem.at[0], sem.at[1], (r ^ 1, c)).start()

    def line_go(whole, other, part_ref, landed_ref, sem, ss, rs):
        meet = remote(whole.at[:, 1 - core], other, sem.at[0], sem.at[1], (r ^ 1, c))
        meet.wait_recv()
        part_ref[...] = (whole[:, core] + other[...]).astype(BF16)
        for d in DEPTHS:
            to = (z + d) % ZS
            remote(part_ref.at[to], landed_ref.at[z], ss.at[d], rs.at[d], in_line(d)).start()
        meet.wait_send()
        return whole[z, core] + other[z]

    def line_sum(landed_ref, ss, rs, first, width):
        for d in DEPTHS:
            frm = (z + ZS - d) % ZS
            remote(landed_ref.at[frm], landed_ref.at[frm], ss.at[d], rs.at[d], in_line(d)).wait_recv()
            out[:, first : first + width] += landed_ref[frm].astype(F32)

    def line_sent(part_ref, landed_ref, ss, rs):
        for d in DEPTHS:
            to = (z + d) % ZS
            remote(part_ref.at[to], landed_ref.at[z], ss.at[d], rs.at[d], in_line(d)).wait_send()

    for q in range(4):
        rows = [pt[m : m + 1, cut(q)] for m in range(POS)]

        def count(i, acc, q=q, rows=rows):
            k0 = pl.multiple_of(i * STEP, STEP)
            score = s_ref[pl.ds(k0, STEP), cut(q)]
            new = []
            for m in range(POS):
                t = jnp.tanh(score - rows[m])
                u = 1.0 + t
                v = 1.0 - t * t
                vi[m, pl.ds(k0, STEP), cut(q)] = v
                new.append(acc[2 * m] + fold(u))
                new.append(acc[2 * m + 1] + fold(v))
            return tuple(new)

        acc = lax.fori_loop(0, steps, count, (jnp.zeros((8, LANES), F32),) * (2 * POS))
        for m in range(POS):
            at = m * POS + q
            x2s[at : at + 1, :] = jnp.sum(acc[2 * m], axis=0, keepdims=True)
            x2s[16 + at : 17 + at, :] = jnp.sum(acc[2 * m + 1], axis=0, keepdims=True)
    exchange(x2s, x2r.at[c], x2_ss, x2_rs, peer_c, PLANE)
    x2r[c] = x2s[...]
    exchange(pt.at[:, group], jp.at[r], p_ss, p_rs, peer_r, LINE)
    jp[r] = pt[:, group]

    def columns(src, first):
        jt[...] = jnp.transpose(src[...].reshape(ROWS * 8, LANES))
        mine_cols = jt[pl.ds(pl.multiple_of(x * SHARD, SHARD), SHARD), :]
        for b in range(ROWS):
            for n in range(8):
                jc[first + n, b * SHARD : (b + 1) * SHARD, :] = jnp.broadcast_to(
                    mine_cols[:, b * 8 + n : b * 8 + n + 1], (SHARD, LANES)
                )

    arrive(x2s, x2r, x2_ss, x2_rs, peer_c, c)
    total = jnp.sum(x2r[...], axis=0)
    factor = 1.0 / (POS * SHARD * ROWS * COLS)

    def of(value, m):
        return value[m * POS : (m + 1) * POS]

    p = [of(scores, m) for m in range(POS)]
    rank = [0.5 + 0.5 * of(total[0:16], m) for m in range(POS)]
    slope = [0.25 * of(total[16:32], m) for m in range(POS)]
    prank = [jnp.full((POS, LANES), 1.0, F32) for _ in range(POS)]
    grad = [-factor / rank[m] for m in range(POS)]
    pulled = [jnp.zeros((POS, LANES), F32) for _ in range(POS)]
    for m in range(POS):
        for n in range(m + 1, POS):
            t = jnp.tanh(p[n] - p[m])
            prank[m] = prank[m] + 0.5 * (1.0 + t)
            prank[n] = prank[n] + 0.5 * (1.0 - t)
            pair = (0.25 / TAU) * (1.0 - t) * (1.0 + t) * (grad[n] - grad[m])
            pulled[m] = pulled[m] + pair
            pulled[n] = pulled[n] - pair
    for m in range(POS):
        weight = prank[m] / (rank[m] * rank[m]) * factor / TAU
        quarter, extra = 0.25 * weight, pulled[m] - weight * slope[m]
        for q in range(4):
            we[m : m + 1, cut(q)] = quarter[q : q + 1, :]
            we[POS + m : POS + m + 1, cut(q)] = extra[q : q + 1, :]

    exchange(we.at[:, group], jw.at[r], w_ss, w_rs, peer_r, LINE)
    jw[r] = we[:, group]

    for q in range(4):
        rows = [tgt[m : m + 1, cut(q)] for m in range(POS)]
        weights = [we[m : m + 1, cut(q)] for m in range(POS)]
        extras = [we[POS + m : POS + m + 1, cut(q)] for m in range(POS)]

        def tile_i(i, carry, q=q, rows=rows, weights=weights, extras=extras):
            k0 = pl.multiple_of(i * STEP, STEP)
            dense = weights[0] * vi[0, pl.ds(k0, STEP), cut(q)]
            for m in range(1, POS):
                dense = dense + weights[m] * vi[m, pl.ds(k0, STEP), cut(q)]
            extra = jnp.where(iota_k == rows[0] - k0, extras[0], 0.0)
            for m in range(1, POS):
                extra = jnp.where(iota_k == rows[m] - k0, extras[m], extra)
            dense = dense + extra
            gi[pl.ds(k0, STEP), cut(q)] = dense.astype(BF16)
            return carry

        lax.fori_loop(0, steps, tile_i, 0)

    over_rows = (((0,), (0,)), ((), ()))
    line_meet((gi,), a_buf[:, :, BOTH_AT:].reshape(BLOCK, EARLY), e_whole, e_other, e_sem)
    early_plane = c_buf[:, :, BOTH_AT:].reshape(BLOCK, EARLY)
    for h in range(2):
        rows = slice(256 * h, 256 * h + 256)
        product = lax.dot_general(gi[:, rows], early_plane, over_rows, preferred_element_type=F32)
        ep_part[8 * h : 8 * h + 8] = product.astype(BF16).reshape(8, SHARD, EARLY)

        @pl.when(c // 8 == h)
        def _(product=product):
            e_mine[...] = product.reshape(8, SHARD, EARLY)

    for o in PLANE:
        remote(ep_part.at[c ^ o], ep_landed.at[c], f_ss.at[o], f_rs.at[o], (r, c ^ o)).start()
    out[:, BOTH_AT:] = e_mine[c % 8]

    arrive(pt.at[:, group], jp, p_ss, p_rs, peer_r, r)
    columns(jp, 0)
    out[:, BOTH_AT:] += line_go(e_whole, e_other, ez_part, ez_landed, e_sem, e_ss, e_rs)

    def slopes(i, carry):
        k0 = pl.multiple_of(i * STEP, STEP)
        for m in range(POS):
            col = jc[m, pl.ds(k0, STEP), :]
            for q in range(4):
                t = jnp.tanh(s_ref[pl.ds(k0, STEP), cut(q)] - col)
                vj[m, pl.ds(k0, STEP), cut(q)] = 1.0 - t * t
            where = jc[POS + m, pl.ds(k0, STEP), :].astype(I32)
            jc[POS + m, pl.ds(k0, STEP), :] = jnp.where(
                where // BLOCK == r, where % BLOCK, -1
            ).astype(F32)
        return carry

    lax.fori_loop(0, steps, slopes, 0)

    arrive(we.at[:, group], jw, w_ss, w_rs, peer_r, r)
    columns(jw, 2 * POS)

    def tile_j(i, carry):
        for part_id in range(2):
            k0 = pl.ds(pl.multiple_of(i * 32 + part_id * 16, 16), 16)
            weights = [jc[2 * POS + m, k0, :] for m in range(POS)]
            extras = [jc[3 * POS + m, k0, :] for m in range(POS)]
            at = [jc[POS + m, k0, :] for m in range(POS)]
            for q in range(4):
                dense = weights[0] * vj[0, k0, cut(q)]
                for m in range(1, POS):
                    dense = dense + weights[m] * vj[m, k0, cut(q)]
                lane = (iota_a[0:16, :] + q * LANES).astype(F32)
                extra = jnp.where(at[0] == lane, extras[0], 0.0)
                for m in range(1, POS):
                    extra = jnp.where(at[m] == lane, extras[m], extra)
                dense = dense + extra
                gj[k0, cut(q)] = dense.astype(BF16)
        return carry

    lax.fori_loop(0, BLOCK // 32, tile_j, 0)

    line_meet((gi, gj), a_buf[:, :, LINE_AT:BOTH_AT].reshape(BLOCK, NARROW), z_whole, z_other, z_sem)

    left = c_buf[:, :, :BROAD].reshape(BLOCK, BROAD)
    wide = 2 * LANES
    for turn_id in range(2):
        h = (c // 8) ^ (1 - turn_id)
        half = pl.ds(pl.multiple_of(h * wide, wide), wide)
        product = lax.dot_general(gi[:, half], left, over_rows, preferred_element_type=F32)
        product = product + lax.dot_general(gj[:, half], left, over_rows, preferred_element_type=F32)
        part[pl.ds(h * 8, 8)] = product.astype(BF16).reshape(8, SHARD, BROAD)
        if turn_id == 1:
            mine[...] = product.reshape(8, SHARD, BROAD)

        for o in PLANE:
            if (o < 8) == (turn_id == 1):
                remote(part.at[c ^ o], landed.at[c], g_ss.at[o], g_rs.at[o], (r, c ^ o)).start()

    out[:, :BROAD] = mine[c % 8]
    out[:, LINE_AT:BOTH_AT] = line_go(z_whole, z_other, z_part, z_landed, z_sem, h_ss, h_rs)

    def plane_sum(part_ref, landed_ref, ss, rs, first, width):
        for o in PLANE:
            frm = c ^ o
            remote(part_ref.at[frm], landed_ref.at[frm], ss.at[o], rs.at[o], (r, frm)).wait_recv()
            out[:, first : first + width] += landed_ref[frm].astype(F32)

    def plane_sent(part_ref, landed_ref, ss, rs):
        def wait(o, carry):
            frm = c ^ o
            remote(part_ref.at[frm], landed_ref.at[frm], ss.at[o], rs.at[o], (r, frm)).wait_send()
            return carry

        lax.fori_loop(1, 16, wait, 0)

    line_sum(ez_landed, e_ss, e_rs, BOTH_AT, EARLY)
    plane_sum(ep_part, ep_landed, f_ss, f_rs, BOTH_AT, EARLY)
    line_sent(ez_part, ez_landed, e_ss, e_rs)
    plane_sent(ep_part, ep_landed, f_ss, f_rs)
    leave(x1s, x1r.at[c], x1_ss, x1_rs, peer_c)
    leave(x2s, x2r.at[c], x2_ss, x2_rs, peer_c)
    leave(pt.at[:, group], jp.at[r], p_ss, p_rs, peer_r)
    leave(we.at[:, group], jw.at[r], w_ss, w_rs, peer_r)
    for copy in sent:
        copy.wait_send()
    line_sum(z_landed, h_ss, h_rs, LINE_AT, NARROW)
    plane_sum(part, landed, g_ss, g_rs, 0, BROAD)
    line_sent(z_part, z_landed, h_ss, h_rs)
    plane_sent(part, landed, g_ss, g_rs)


def body(embed, positives, placement):
    dma = pltpu.SemaphoreType.DMA
    return pl.pallas_call(
        kernel,
        out_shape=pltpu.VMEM((SHARD, WIDTH), F32),
        in_specs=[pl.BlockSpec(memory_space=pl.ANY)] * 3,
        out_specs=pl.BlockSpec(memory_space=pltpu.VMEM),
        scratch_shapes=[
            pltpu.VMEM((COLS, SHARD, WIDTH), BF16),
            pltpu.VMEM((ROWS, SHARD, WIDTH), BF16),
            pltpu.VMEM((BLOCK, BLOCK), F32),
            pltpu.VMEM((POS, BLOCK, BLOCK), F32),
            pltpu.VMEM((POS, BLOCK, BLOCK), F32),
            pltpu.VMEM((BLOCK, BLOCK), BF16),
            pltpu.VMEM((BLOCK, BLOCK), BF16),
            pltpu.VMEM((COLS, SHARD, BROAD), BF16),
            pltpu.VMEM((COLS, SHARD, BROAD), BF16),
            pltpu.VMEM((8, SHARD, BROAD), F32),
            pltpu.VMEM((ZS, SHARD, NARROW), BF16),
            pltpu.VMEM((ZS, SHARD, NARROW), BF16),
            pltpu.VMEM((ZS, 2, SHARD, NARROW), F32),
            pltpu.VMEM((ZS, SHARD, NARROW), F32),
            pltpu.VMEM((ZS, SHARD, EARLY), BF16),
            pltpu.VMEM((ZS, SHARD, EARLY), BF16),
            pltpu.VMEM((ZS, 2, SHARD, EARLY), F32),
            pltpu.VMEM((ZS, SHARD, EARLY), F32),
            pltpu.VMEM((COLS, SHARD, EARLY), BF16),
            pltpu.VMEM((COLS, SHARD, EARLY), BF16),
            pltpu.VMEM((8, SHARD, EARLY), F32),
            pltpu.VMEM((POS, BLOCK), I32),
            pltpu.VMEM((64, LANES), I32),
            pltpu.VMEM((8, BLOCK), I32),
            pltpu.VMEM((8, BLOCK), F32),
            pltpu.VMEM((8, BLOCK), F32),
            pltpu.VMEM((16, LANES), F32),
            pltpu.VMEM((COLS, 16, LANES), F32),
            pltpu.VMEM((32, LANES), F32),
            pltpu.VMEM((COLS, 32, LANES), F32),
            pltpu.VMEM((ROWS, 8, LANES), F32),
            pltpu.VMEM((ROWS, 8, LANES), F32),
            pltpu.VMEM((LANES, LANES), F32),
            pltpu.VMEM((4 * POS, BLOCK, LANES), F32),
            dma((4,)),
            dma((2,)),
            dma((2,)),
            dma((32,)),
            dma((32,)),
        ]
        + [dma((16,))] * 20,
        compiler_params=pltpu.CompilerParams(
            collective_id=0, has_side_effects=True, vmem_limit_bytes=60 * 1024 * 1024
        ),
        cost_estimate=pl.CostEstimate(flops=1 << 31, bytes_accessed=1 << 22, transcendentals=1 << 21),
        name="smooth_ap",
    )(embed, positives.T, placement.reshape(64, LANES))


def solution(mesh):
    return jax.shard_map(
        body,
        mesh=mesh,
        in_specs=(P(("row", "col"), None), P("row", None), P()),
        out_specs=P(("row", "col"), None),
        check_vma=False,
    )
```
